32 devices in a mesh: dp: 8 (over y, x, core), tensor: 4 (over z).
Axes of the slice: x: 2, y: 2, z: 4, core: 2. Of those that a mesh axis runs over, the one named last changes fastest.
Arguments:
- hidden_in: bfloat16 [16384, 768], P(('dp', 'tensor')), may hold values from -6 to 6
- lengths: int32 [16], P('dp'), may hold values from 64 to 1024, as said below
- ln1_gain: bfloat16 [768], replicated, may hold values from 0.099609375 to 1.8984375
- ln1_bias: bfloat16 [768], replicated, may hold values from -3 to 3
- w_qkv: bfloat16 [768, 3, 768], P(None, None, 'tensor'), may hold values from -0.21875 to 0.21875
- b_query: bfloat16 [768], P('tensor'), may hold values from -3 to 3
- b_value: bfloat16 [768], P('tensor'), may hold values from -3 to 3
- w_out: bfloat16 [768, 768], P('tensor'), may hold values from -2.5 to 2.5
- b_out: bfloat16 [768], replicated, may hold values from -3 to 3
- ln2_gain: bfloat16 [768], replicated, may hold values from 0.099609375 to 1.8984375
- ln2_bias: bfloat16 [768], replicated, may hold values from -3 to 3
- w_fc: bfloat16 [768, 3072], P(None, 'tensor'), may hold values from -0.21875 to 0.21875
- b_fc: bfloat16 [3072], P('tensor'), may hold values from -3 to 3
- w_proj: bfloat16 [3072, 768], P('tensor'), may hold values from -0.4375 to 0.4375
- b_proj: bfloat16 [768], replicated, may hold values from -3 to 3
- out_grad: bfloat16 [16384, 768], P(('dp', 'tensor')), may hold values from -6 to 6
Outputs:
- block_out: bfloat16 [16384, 768], P(('dp', 'tensor'))
- grad_input: bfloat16 [16384, 768], P(('dp', 'tensor'))
- grad_ln1_gain: float32 [768], replicated
- grad_ln1_bias: float32 [768], replicated
- grad_w_qkv: float32 [768, 3, 768], P(None, None, 'tensor')
- grad_b_query: float32 [768], P('tensor')
- grad_b_value: float32 [768], P('tensor')
- grad_w_out: float32 [768, 768], P('tensor')
- grad_b_out: float32 [768], replicated
- grad_ln2_gain: float32 [768], replicated
- grad_ln2_bias: float32 [768], replicated
- grad_w_fc: float32 [768, 3072], P(None, 'tensor')
- grad_b_fc: float32 [3072], P('tensor')
- grad_w_proj: float32 [3072, 768], P('tensor')
- grad_b_proj: float32 [768], replicated
The draws below stay inside these ranges and needn't reach their ends.
Inputs may be any that keep to these rules, and one draw needn't show every extreme that they name: `lengths`: valid tokens of each sequence; one of the 16 sequences has exactly 1024.
All inputs are finite; a program needn't handle non-finite values.
Results may differ from the reference program's by a relative error of at most 0.018.
Values may be sent and summed in bfloat16 or wider, within the bound.
A program may use at most 128 MiB of HBM per device.

```python
import jax
import jax.numpy as jnp
from jax import lax

D = 768
HEADS = 12
HEAD_DIM = 64
FF = 3072
LEN = 1024
SEQ_DEV = 2
MIN_LEN = 64
SEQS = 16
TOKENS = 16384


def draw_lengths(key, part):
    key = jax.random.fold_in(key, 7)
    key_list = jax.random.split(key, 4)
    upper = LEN - MIN_LEN + 1
    first = jax.random.randint(key_list[0], (SEQS,), 0, upper)
    second = jax.random.randint(key_list[1], (SEQS,), 0, upper)
    third = jax.random.randint(key_list[2], (SEQS,), 0, upper)
    shortfall = jnp.minimum(jnp.minimum(first, second), third)
    chosen = jax.random.randint(key_list[3], (), 0, SEQS)
    drawn = LEN - shortfall
    return jnp.where(jnp.arange(SEQS) == chosen, LEN, drawn).astype(jnp.int32)


def block_levels(rng, extent, pieces, least, high):
    factor_of = 1.0
    for axis_at, blocks in pieces:
        heights = jax.random.uniform(jax.random.fold_in(jax.random.fold_in(rng, 6), axis_at), (blocks,), jnp.float32, least / len(pieces), high / len(pieces))
        factor_of = factor_of * jnp.repeat(jnp.exp(heights), extent[axis_at] // blocks).reshape((-1,) + (1,) * (len(extent) - 1 - axis_at))
    return factor_of


def gaussian(rng, dims, deviation, bound, cuts=(), held_as=jnp.bfloat16):
    values = deviation * jax.random.normal(rng, dims, jnp.float32)
    if cuts:
        values = values * block_levels(rng, dims, cuts, -0.22, 0.18)
    return jnp.clip(values, -bound, bound).astype(held_as)


def setup_inputs(seed: int = 0) -> dict:
    splits = jax.random.split(jax.random.key(seed), 17)
    hidden_in = gaussian(splits[0], (TOKENS, D), 1.0, 6.0, ((0, 32),))
    lengths = draw_lengths(jax.random.fold_in(splits[16], 71), 0)
    ln1_gain = jnp.clip(1.0 + 0.18 * jax.random.normal(splits[2], (D,), jnp.float32), 0.099609375, 1.8984375).astype(jnp.bfloat16)
    ln1_bias = gaussian(splits[3], (D,), 0.5, 3.0)
    w_qkv = gaussian(splits[4], (D, 3, D), D ** -0.5, 0.21875, ((2, 4),))
    b_query = gaussian(splits[5], (D,), 0.5, 3.0, ((0, 4),))
    b_value = gaussian(splits[6], (D,), 0.5, 3.0, ((0, 4),))
    w_out = gaussian(splits[7], (D, D), (max(D // 128, 1)) ** -0.5, 2.5, ((0, 4),))
    b_out = gaussian(splits[8], (D,), 0.5, 3.0)
    ln2_gain = jnp.clip(1.0 + 0.18 * jax.random.normal(splits[9], (D,), jnp.float32), 0.099609375, 1.8984375).astype(jnp.bfloat16)
    ln2_bias = gaussian(splits[10], (D,), 0.5, 3.0)
    w_fc = gaussian(splits[11], (D, FF), D ** -0.5, 0.21875, ((1, 4),))
    b_fc = gaussian(splits[12], (FF,), 0.5, 3.0, ((0, 4),))
    w_proj = gaussian(splits[13], (FF, D), (max(FF // 16, 1)) ** -0.5, 0.4375, ((0, 4),))
    b_proj = gaussian(splits[14], (D,), 0.5, 3.0)
    out_grad = gaussian(splits[15], (TOKENS, D), 1.0, 6.0, ((0, 32),))
    return {"hidden_in": hidden_in, "lengths": lengths, "ln1_gain": ln1_gain, "ln1_bias": ln1_bias, "w_qkv": w_qkv, "b_query": b_query, "b_value": b_value, "w_out": w_out, "b_out": b_out, "ln2_gain": ln2_gain, "ln2_bias": ln2_bias, "w_fc": w_fc, "b_fc": b_fc, "w_proj": w_proj, "b_proj": b_proj, "out_grad": out_grad}


@jax.custom_vjp
def low(v):
    return lax.optimization_barrier(v.astype(jnp.bfloat16)).astype(jnp.float32)

@jax.custom_vjp
def low_back(v):
    return v

def low_keep(v):
    return (low(v), None)

def low_pass(kept, grad):
    return (grad,)

def back_keep(v):
    return (v, None)

def back_low(kept, grad):
    return (low(grad),)
low.defvjp(low_keep, low_pass)
low_back.defvjp(back_keep, back_low)
eps_norm = 1e-05
masked_score = -1e+30

def both_round(value):
    return low(low_back(value))

def layer_norm(value, gain, shift):
    row_mean = lax.optimization_barrier(jnp.mean(value, axis=-1, keepdims=True))
    centred = value - row_mean
    variance = lax.optimization_barrier(jnp.mean(centred * centred, axis=-1, keepdims=True))
    return centred * lax.rsqrt(variance + eps_norm) * gain + shift

def attend_one(inputs_one):
    queries, key_rows, value_rows, length = inputs_one
    seq_span = queries.shape[0]
    raw_scores = jnp.einsum('qhe,khe->hqk', queries, key_rows, precision=lax.Precision.HIGHEST)
    scores = low_back(raw_scores) * HEAD_DIM ** (-0.5)
    row_ids = jnp.arange(seq_span)[:, None]
    col_ids = jnp.arange(seq_span)[None, :]
    allowed = (col_ids <= row_ids) & (col_ids < length)
    scores = jnp.where(allowed[None], scores, masked_score)
    row_top = lax.optimization_barrier(jnp.max(scores, axis=-1, keepdims=True))
    weights = jnp.exp(scores - row_top)
    weights = weights / lax.optimization_barrier(jnp.sum(weights, axis=-1, keepdims=True))
    return jnp.einsum('hqk,khe->qhe', low(weights), value_rows, precision=lax.Precision.HIGHEST)

def forward(hidden, group_lengths, params):
    ln1_gain, ln1_bias, w_qkv, b_query, b_value, w_out, b_out, ln2_gain, ln2_bias, w_fc, b_fc, w_proj, b_proj = params
    row_total = hidden.shape[0]
    seq_count = group_lengths.shape[0]
    seq_span = row_total // seq_count
    normed_one = low(layer_norm(hidden, ln1_gain, ln1_bias))
    mixed_qkv = jnp.einsum('td,dcn->tcn', normed_one, w_qkv, precision=lax.Precision.HIGHEST)
    queries = both_round(mixed_qkv[:, 0] + b_query)
    key_rows = both_round(mixed_qkv[:, 1])
    value_rows = both_round(mixed_qkv[:, 2] + b_value)
    shape_four = (seq_count, seq_span, HEADS, HEAD_DIM)
    context = lax.map(jax.checkpoint(attend_one), (queries.reshape(shape_four), key_rows.reshape(shape_four), value_rows.reshape(shape_four), group_lengths))
    context = both_round(context.reshape(row_total, D))
    attn_branch = low_back(jnp.dot(context, w_out, precision=lax.Precision.HIGHEST))
    middle = hidden + attn_branch + b_out
    normed_two = low(layer_norm(middle, ln2_gain, ln2_bias))
    pre_act = low_back(jnp.dot(normed_two, w_fc, precision=lax.Precision.HIGHEST) + b_fc)
    activation = low(jax.nn.gelu(pre_act, approximate=True))
    mlp_branch = low_back(jnp.dot(activation, w_proj, precision=lax.Precision.HIGHEST))
    result = middle + mlp_branch + b_proj
    positions = jnp.arange(seq_span)[None, :]
    valid_rows = (positions < group_lengths[:, None]).reshape(row_total, 1)
    return result * valid_rows.astype(jnp.float32)

def reference(hidden_in, lengths, ln1_gain, ln1_bias, w_qkv, b_query, b_value, w_out, b_out, ln2_gain, ln2_bias, w_fc, b_fc, w_proj, b_proj, out_grad):
    params = tuple((item.astype(jnp.float32) for item in (ln1_gain, ln1_bias, w_qkv, b_query, b_value, w_out, b_out, ln2_gain, ln2_bias, w_fc, b_fc, w_proj, b_proj)))
    step_rows = SEQ_DEV * LEN
    hidden_steps = hidden_in.astype(jnp.float32).reshape(-1, step_rows, D)
    grad_steps = out_grad.astype(jnp.float32).reshape(-1, step_rows, D)
    length_steps = lengths.reshape(-1, SEQ_DEV)

    def one_step(running, inputs_one):
        hidden, cotangent, group_lengths = inputs_one
        result, pullback = jax.vjp(lambda hh, pp: forward(hh, group_lengths, pp), hidden, params)
        grad_hidden, grad_params = pullback(cotangent)
        running = jax.tree.map(lambda first, second: first + second, running, grad_params)
        return (running, (result.astype(jnp.bfloat16), grad_hidden.astype(jnp.bfloat16)))
    start_sums = jax.tree.map(jnp.zeros_like, params)
    totals, (outputs, grads) = lax.scan(one_step, start_sums, (hidden_steps, grad_steps, length_steps))
    return (outputs.reshape(-1, D), grads.reshape(-1, D), totals[0], totals[1], totals[2], totals[3], totals[4], totals[5], totals[6], totals[7], totals[8], totals[9], totals[10], totals[11], totals[12])
```

```python
import functools

import jax
import jax.numpy as jnp
from jax import lax
from jax.experimental import pallas as pl
from jax.experimental.pallas import tpu as pltpu
from jax.sharding import PartitionSpec as P

BF = jnp.bfloat16
F32 = jnp.float32
EPS = 1e-5
NEG = -1e30
LOG2E = 1.4426950408889634
MESH = pl.DeviceIdType.MESH
RING = 4
GROUP = 2 * RING


def dot(a, b, ca=1, cb=0):
    return lax.dot_general(a, b, (((ca,), (cb,)), ((), ())), preferred_element_type=F32)


def nt(a, b):
    return dot(a, b, 1, 1)


def tn(a, b):
    return dot(a, b, 0, 0)


def al(v, m):
    return pl.multiple_of(v, m)


class Ids:
    def __init__(self):
        self.n = 0

    def __call__(self, k):
        base = self.n
        self.n += k
        return base


SID = Ids()
S_LEN, S_BIAS, S_HID, S_OG, S_AS1 = SID(1), SID(3), SID(1), SID(1), SID(3)
S_ARA, S_ARB = SID(4), SID(4)
S_MS1, S_MRA, S_MRB, S_MP = SID(6), SID(12), SID(12), SID(6)
S_N1, S_PO, S_GA, S_DX, S_BO, S_GI = SID(1), SID(1), SID(1), SID(1), SID(1), SID(1)
S_GP, S_G1, S_G2, S_GZ = SID(8), SID(16), SID(16), SID(8)
S_FA, S_FB, S_FC = SID(6), SID(4), SID(6)
S_A1, S_A2, S_AZ = SID(6), SID(6), SID(4)
S_HA, S_HB, S_HC = SID(3), SID(2), SID(3)
S_SM = SID(5)
RID = Ids()
R_LEN, R_BIAS, R_HID, R_OG, R_AS1 = RID(1), RID(3), RID(1), RID(1), RID(2)
R_ARA, R_ARB = RID(4), RID(4)
R_MS1, R_MRA, R_MRB, R_MP = RID(6), RID(12), RID(12), RID(6)
R_N1, R_PO, R_GA, R_DX, R_BO, R_GI = RID(1), RID(1), RID(1), RID(1), RID(1), RID(1)
R_GP, R_G1, R_G2, R_GZ = RID(8), RID(16), RID(16), RID(6)
R_FA, R_FB, R_FC = RID(6), RID(4), RID(6)
R_A1, R_A2, R_AZ = RID(6), RID(6), RID(12)
R_HA, R_HB, R_HC = RID(3), RID(2), RID(3)
R_SM = RID(5)


def kernel(
    lens, bias, vecs, hid_in, og_in, wq, wo, wf, wp,
    bo_out, gi_out, gm_out, ga_out, small_out,
    lrecv, bfa, hid, og, n1, watt, wmlp, q, k, v, qt, kt, vt, do, dot_, ot, ctx,
    mid, n2, oacc, dn2, act, dpre, ga, ps, pr, ps2, pr2, bo, gi,
    lse, dqa, cmask, kh, vh, qh,
    prb, r1b, r2b, zb, fs, gatt, a1b, a2b, azb, fa, sb, srb,
    ss, rs, ls,
):
    D = hid_in.shape[1]
    R = hid_in.shape[0]
    T = 2 * R
    HC = D // 2
    BQ = 256
    NB = T // BQ
    dp = lax.axis_index("dp")
    z = lax.axis_index("tensor")
    base = (dp // GROUP) * GROUP
    chip = (dp - base) // 2
    c = dp % 2
    oc = 1 - c
    cy = chip // 2
    cx = chip % 2
    r = 3 * cy + cx - 2 * cx * cy

    def ring_dp(rr, core):
        y = rr // 2
        x = rr % 2 + y - 2 * (rr % 2) * y
        return base + (2 * y + x) * 2 + core

    r_up = (r + 1) % RING
    r_dn = (r + 3) % RING
    r_op = (r + 2) % RING
    dev_up = (ring_dp(r_up, c), z)
    dev_dn = (ring_dp(r_dn, c), z)
    dev_pair = (dp + 1 - 2 * c, z)
    dev_z = [None] + [(dp, (z + dz) % 4) for dz in (1, 2, 3)]
    z_x = z + 1 - 2 * (z % 2)
    dev_swap = (dp + 1 - 2 * c, z_x)
    keep = c == z % 2
    swap = c != z % 2
    own_c = z // 2 == c
    not_own = z // 2 != c
    zz_own = z % 2
    pending = {}

    def when(cond, fn):
        if cond is None:
            fn()
        else:
            pl.when(cond)(fn)

    def desc(src, dst, sid, rid, dev):
        return pltpu.make_async_remote_copy(
            src_ref=src, dst_ref=dst, send_sem=ss.at[sid], recv_sem=rs.at[rid],
            device_id=dev, device_id_type=MESH,
        )

    def send(src, dst, sid, rid, dev, late=None, cond=None):
        desc(src, dst, sid, rid, dev).start()
        if late is not None:
            pending[sid] = (late, cond)

    def wsend(ref, sid):
        desc(ref, ref, sid, 0, dev_pair).wait_send()

    def wrecv(ref, rid):
        desc(ref, ref, 0, rid, dev_pair).wait_recv()

    barrier = pltpu.get_barrier_semaphore()
    for dev in (dev_up, dev_dn, dev_pair, dev_z[1], dev_z[2], dev_z[3], dev_swap):
        pl.semaphore_signal(barrier, inc=1, device_id=dev, device_id_type=MESH)
    pl.semaphore_wait(barrier, 7)

    loc_n = [0]

    def local(src, dst, cond=None):
        i = loc_n[0]
        loc_n[0] += 1
        cp = lambda: pltpu.make_async_copy(src(), dst(), ls.at[i])
        when(cond, lambda: cp().start())
        return lambda: when(cond, lambda: cp().wait())

    when(swap, lambda: send(hid_in, hid, S_HID, R_HID, dev_swap, lambda: hid_in, swap))
    w_hid = local(lambda: hid_in, lambda: hid, keep)
    send(lens, lrecv, S_LEN, R_LEN, dev_pair, lambda: lens)
    for dz in (1, 2, 3):
        send(bias, bfa.at[z], S_BIAS + dz - 1, R_BIAS + dz - 1, dev_z[dz], lambda: bias)
    ZS = D // 4

    def att_rows(zz):
        return pl.ds(al(zz * ZS, 16), ZS)

    def att_s1():
        for dz in (1, 2, 3):
            dst = watt.at[r, att_rows(zz_own)]

            def from_q():
                send(wq.at[jnp.minimum(r, 2)], dst, S_AS1 + dz - 1, R_AS1 + zz_own, dev_z[dz])

            def from_o():
                send(wo, dst, S_AS1 + dz - 1, R_AS1 + zz_own, dev_z[dz])

            pl.when(r < 3)(from_q)
            pl.when(r == 3)(from_o)
            pending[S_AS1 + dz - 1] = (lambda: wo, own_c)

    pl.when(own_c)(att_s1)
    w_wq = local(lambda: wq, lambda: watt.at[pl.ds(0, 3), att_rows(zz_own)], own_c)
    w_wo = local(lambda: wo, lambda: watt.at[3, att_rows(zz_own)], own_c)
    when(swap, lambda: send(og_in, og, S_OG, R_OG, dev_swap, lambda: og_in, swap))
    w_og = local(lambda: og_in, lambda: og, keep)
    w_mlp0 = [local(lambda: wf, lambda: wmlp.at[0, z]), local(lambda: wp, lambda: wmlp.at[1, z])]
    bfa[z] = bias[...]

    def zsh(dz):
        return (z - dz + 4) % 4

    def mg_s1(m, dz):
        w = (wf, wp)[m]
        u = m * 3 + dz - 1
        send(w.at[r, c], wmlp.at[m, z, r, c], S_MS1 + u, R_MS1 + u, dev_z[dz], lambda: w.at[r, c])

    def mg_a(m, dz):
        u = m * 3 + dz - 1
        piece = wmlp.at[m, zsh(dz), r, c]
        wrecv(piece, R_MS1 + u)
        send(piece, piece, S_MRA + 2 * u, R_MRA + 2 * u, dev_up)
        send(piece, piece, S_MRA + 2 * u + 1, R_MRA + 2 * u + 1, dev_dn)

    def mg_b(m, dz):
        u = m * 3 + dz - 1
        zp = zsh(dz)
        wrecv(wmlp.at[m, zp, r_dn, c], R_MRA + 2 * u)
        lo = wmlp.at[m, zp, r_dn, c, pl.ds(0, 48)]
        send(lo, lo, S_MRB + 2 * u, R_MRB + 2 * u, dev_up)
        wrecv(wmlp.at[m, zp, r_up, c], R_MRA + 2 * u + 1)
        hi = wmlp.at[m, zp, r_up, c, pl.ds(48, 48)]
        send(hi, hi, S_MRB + 2 * u + 1, R_MRB + 2 * u + 1, dev_dn)

    def mg_p(m, dz):
        u = m * 3 + dz - 1
        zp = zsh(dz)
        wrecv(wmlp.at[m, zp, r_op, c, pl.ds(0, 48)], R_MRB + 2 * u)
        wrecv(wmlp.at[m, zp, r_op, c, pl.ds(48, 48)], R_MRB + 2 * u + 1)
        mine = wmlp.at[m, zp, :, c]
        send(mine, mine, S_MP + u, R_MP + u, dev_pair)

    def mg_done(m, dz):
        u = m * 3 + dz - 1
        zp = zsh(dz)
        wrecv(wmlp.at[m, zp, :, oc], R_MP + u)
        for s in (0, 1):
            wsend(wmlp.at[m, zp, r, c], S_MRA + 2 * u + s)
            wsend(wmlp.at[m, zp, r, c, pl.ds(0, 48)], S_MRB + 2 * u + s)
        wsend(wmlp.at[m, zp, :, c], S_MP + u)

    munits = [(0, 1), (1, 1), (0, 2), (1, 2), (0, 3), (1, 3)]

    def mg_round(j):
        if 0 <= j < 6:
            mg_a(*munits[j])
        if 0 <= j - 1 < 6:
            mg_b(*munits[j - 1])
        if 0 <= j - 2 < 6:
            mg_p(*munits[j - 2])

    w_hid()
    when(swap, lambda: wrecv(hid, R_HID))
    row0 = c * R
    half = ZS // 2

    def stats(x):
        mu = jnp.mean(x, axis=1, keepdims=True)
        cen = x - mu
        var = jnp.mean(cen * cen, axis=1, keepdims=True)
        rstd = lax.rsqrt(var + EPS)
        return cen * rstd, rstd

    LB = 64

    def ln1_body(i, _):
        rows = pl.ds(al(i * LB, LB), LB)
        n, _r = stats(hid[rows, :].astype(F32))
        out = n * vecs[0:1, :] + vecs[1:2, :]
        n1[pl.ds(al(row0 + i * LB, LB), LB), :] = out.astype(BF)
        return 0

    lax.fori_loop(0, R // LB, ln1_body, 0)
    mine_rows = pl.ds(al(row0, R), R)
    pair_rows = pl.ds(al(oc * R, R), R)
    send(n1.at[mine_rows], n1.at[mine_rows], S_N1, R_N1, dev_pair, lambda: n1.at[mine_rows])

    kk = lax.broadcasted_iota(jnp.int32, (BQ, BQ), 0)
    qq = lax.broadcasted_iota(jnp.int32, (BQ, BQ), 1)
    cmask[...] = jnp.where(kk <= qq, 0.0, NEG)

    needs = (z != 2 * c, z != 2 * c + 1)

    def need(zz):
        return needs[zz]

    def ar_a(zz):
        piece = watt.at[r, att_rows(zz)]
        wrecv(piece, R_AS1 + zz)
        send(piece, piece, S_ARA + 2 * zz, R_ARA + 2 * zz, dev_up, lambda: wo, need(zz))
        send(piece, piece, S_ARA + 2 * zz + 1, R_ARA + 2 * zz + 1, dev_dn, lambda: wo, need(zz))

    def ar_b(zz):
        wrecv(watt.at[r_dn, att_rows(zz)], R_ARA + 2 * zz)
        lo = watt.at[r_dn, pl.ds(al(zz * ZS, 16), half)]
        send(lo, lo, S_ARB + 2 * zz, R_ARB + 2 * zz, dev_up, lambda: watt.at[0, pl.ds(0, half)], need(zz))
        wrecv(watt.at[r_up, att_rows(zz)], R_ARA + 2 * zz + 1)
        hi = watt.at[r_up, pl.ds(al(zz * ZS + half, 16), half)]
        send(hi, hi, S_ARB + 2 * zz + 1, R_ARB + 2 * zz + 1, dev_dn, lambda: watt.at[0, pl.ds(0, half)], need(zz))

    def ar_c(zz):
        wrecv(watt.at[r_op, pl.ds(al(zz * ZS, 16), half)], R_ARB + 2 * zz)
        wrecv(watt.at[r_op, pl.ds(al(zz * ZS + half, 16), half)], R_ARB + 2 * zz + 1)

    for step in (ar_a, ar_b):
        for zz in (0, 1):
            when(need(zz), functools.partial(step, zz))
    for dz in (1, 2, 3):
        mg_s1(0, dz)
        mg_s1(1, dz)
    for zz in (0, 1):
        when(need(zz), functools.partial(ar_c, zz))
    w_wq()
    w_wo()
    for dz in (1, 2, 3):
        wrecv(bfa.at[zsh(dz)], R_BIAS + dz - 1)
    wrecv(lrecv, R_LEN)
    keepf = 1.0 - (c + z % 2 - 2 * c * (z % 2)).astype(F32)
    length = lens[0:1, 0:1] * keepf + lrecv[0:1, 0:1] * (1.0 - keepf)
    wrecv(n1.at[pair_rows], R_N1)

    bqv = bfa[2 * c, 1:2, :] + bfa[2 * c + 1, 1:2, :]

    def qkv_body(i, _):
        rows = pl.ds(al(i * BQ, BQ), BQ)
        x = n1[rows, :]
        q[rows, :] = (nt(x, watt[0]) + bqv[:, :HC]).astype(BF)
        k[rows, :] = nt(x, watt[1]).astype(BF)
        v[rows, :] = (nt(x, watt[2]) + bqv[:, HC:]).astype(BF)
        return 0

    lax.fori_loop(0, NB, qkv_body, 0)

    def tr_body(i, _):
        rows = pl.ds(al(i * BQ, BQ), BQ)
        for hp in range(3):
            lanes = slice(hp * 128, hp * 128 + 128)
            qt[lanes, rows] = q[rows, lanes].T
            kt[lanes, rows] = k[rows, lanes].T
            vt[lanes, rows] = v[rows, lanes].T
        return 0

    lax.fori_loop(0, NB, tr_body, 0)

    lane = lax.broadcasted_iota(jnp.int32, (1, 128), 1)
    sub = lax.broadcasted_iota(jnp.int32, (128, 1), 0)
    pos = lax.broadcasted_iota(jnp.int32, (T, 1), 0).astype(F32)
    keybias = jnp.where(pos < length, 0.0, NEG)
    CS = 0.125 * LOG2E

    def head_prep(hp, hh):
        lanes = pl.ds(al(hp * 128, 128), 128)
        inhead = (lane // 64) == hh
        aux = lane == (1 - hh) * 64
        kp = k[:, lanes].astype(F32)
        kh[...] = jnp.where(inhead, kp, jnp.where(aux, keybias, 0.0)).astype(BF)
        qp = qt[lanes, :].astype(F32)
        qh[...] = jnp.where(sub == (1 - hh) * 64, 1.0, qp).astype(BF)
        return lanes, inhead

    def fwd_head(h, _):
        hp = h // 2
        hh = h % 2
        head_prep(hp, hh)
        hrows = pl.ds(al(h * 64, 64), 64)
        for qb in range(NB):
            nk = (qb + 1) * BQ
            cols = slice(qb * BQ, nk)
            s = dot(kh[:nk, :], qh[:, cols])
            diag = s[nk - BQ :] + cmask[...]
            s = diag if qb == 0 else jnp.concatenate([s[: nk - BQ], diag], axis=0)
            m = jnp.max(s, axis=0, keepdims=True) * CS
            p = jnp.exp2(s * CS - m)
            l = jnp.sum(p, axis=0, keepdims=True)
            o = dot(vt[hrows, :nk], p.astype(BF)) * (1.0 / l)
            ot[hrows, cols] = o.astype(BF)
            lse[h, 0:1, cols] = m + jnp.log(l) * LOG2E
        for j in range(6):
            pl.when(h == j)(functools.partial(mg_round, j))
        return 0

    lax.fori_loop(0, 6, fwd_head, 0)

    def ctx_body(i, _):
        rows = pl.ds(al(i * BQ, BQ), BQ)
        for hp in range(3):
            lanes = slice(hp * 128, hp * 128 + 128)
            ctx[rows, lanes] = ot[lanes, rows].T
        return 0

    lax.fori_loop(0, NB, ctx_body, 0)
    mg_round(6)

    ps[...] = dot(ctx[pair_rows, :], watt[3]).astype(BF)
    send(ps, pr, S_PO, R_PO, dev_pair, lambda: ps)
    mid[...] = hid[...].astype(F32) + vecs[2:3, :] + dot(ctx[mine_rows, :], watt[3])
    w_og()
    when(swap, lambda: wrecv(og, R_OG))
    wrecv(pr, R_PO)

    sb[...] = jnp.zeros_like(sb)

    def ln2_body(i, _):
        rows = pl.ds(al(i * LB, LB), LB)
        x = mid[rows, :] + pr[rows, :].astype(F32)
        mid[rows, :] = x
        n, _r = stats(x)
        n2[rows, :] = (n * vecs[3:4, :] + vecs[4:5, :]).astype(BF)
        p0 = lax.broadcasted_iota(jnp.int32, (LB, 1), 0).astype(F32) + (row0 + i * LB).astype(F32)
        g = og[rows, :].astype(F32) * jnp.where(p0 < length, 1.0, 0.0)
        og[rows, :] = g.astype(BF)
        sb[5:6, :] += jnp.sum(g, axis=0, keepdims=True)
        oacc[rows, :] = jnp.zeros((LB, D), F32)
        dn2[rows, :] = jnp.zeros((LB, D), F32)
        return 0

    lax.fori_loop(0, R // LB, ln2_body, 0)
    for w in w_mlp0:
        w()

    def zdst(i):
        return (z - i + 4) % 4

    def blk(m, i):
        return wmlp.at[m, zdst(i)]

    def add_into(dst, *others):
        t = dst[...].astype(F32)
        for o in others:
            t = t + o[...].astype(F32)
        dst[...] = t.astype(BF)

    def g_s0(m, i):
        u = m * 4 + i
        send(blk(m, i).at[:, oc], prb.at[u], S_GP + u, R_GP + u, dev_pair, lambda: blk(m, i).at[:, oc])

    def g_s1(m, i):
        u = m * 4 + i
        g = blk(m, i)
        wrecv(prb.at[u], R_GP + u)
        add_into(g.at[:, c], prb.at[u])
        send(g.at[r_op, c, pl.ds(0, 48)], r1b.at[u, 0], S_G1 + 2 * u, R_G1 + 2 * u, dev_up,
             lambda: r1b.at[u, 0])
        send(g.at[r_op, c, pl.ds(48, 48)], r1b.at[u, 1], S_G1 + 2 * u + 1, R_G1 + 2 * u + 1, dev_dn,
             lambda: r1b.at[u, 1])

    def g_s2(m, i):
        u = m * 4 + i
        g = blk(m, i)
        wrecv(r1b.at[u, 0], R_G1 + 2 * u)
        add_into(g.at[r_up, c, pl.ds(0, 48)], r1b.at[u, 0])
        send(g.at[r_up, c], r2b.at[u, 0], S_G2 + 2 * u, R_G2 + 2 * u, dev_up, lambda: r2b.at[u, 0])
        wrecv(r1b.at[u, 1], R_G1 + 2 * u + 1)
        add_into(g.at[r_dn, c, pl.ds(48, 48)], r1b.at[u, 1])
        send(g.at[r_dn, c], r2b.at[u, 1], S_G2 + 2 * u + 1, R_G2 + 2 * u + 1, dev_dn, lambda: r2b.at[u, 1])

    def g_s3(m, i):
        u = m * 4 + i
        g = blk(m, i)
        wrecv(r2b.at[u, 0], R_G2 + 2 * u)
        wrecv(r2b.at[u, 1], R_G2 + 2 * u + 1)
        add_into(g.at[r, c], r2b.at[u, 0], r2b.at[u, 1])
        if i > 0:
            send(g.at[r, c], zb.at[m, i - 1], S_GZ + u, R_GZ + m * 3 + i - 1, (dp, zdst(i)),
                 lambda: zb.at[m, i - 1])

    def g_fin(m):
        for i in (1, 2, 3):
            wrecv(zb.at[m, i - 1], R_GZ + m * 3 + i - 1)
        t = wmlp[m, z, r, c].astype(F32)
        for i in range(3):
            t = t + zb[m, i].astype(F32)
        fs[m] = t.astype(BF)
        dst = gm_out.at[m, r, c]
        send(fs.at[m], dst, S_FA + 3 * m, R_FA + 3 * m, dev_up, lambda: fs.at[m])
        send(fs.at[m], dst, S_FA + 3 * m + 1, R_FA + 3 * m + 1, dev_dn, lambda: fs.at[m])
        send(fs.at[m], dst, S_FA + 3 * m + 2, R_FA + 3 * m + 2, dev_pair, lambda: fs.at[m])

    def g_ag(m):
        lo = gm_out.at[m, r_dn, c, pl.ds(0, 48)]
        hi = gm_out.at[m, r_up, c, pl.ds(48, 48)]
        wrecv(gm_out.at[m, r_dn, c], R_FA + 3 * m)
        send(lo, lo, S_FB + 2 * m, R_FB + 2 * m, dev_up, lambda: r1b.at[0, 0])
        full = gm_out.at[m, r_dn, c]
        send(full, full, S_FC + 3 * m, R_FC + 3 * m, dev_pair, lambda: fs.at[m])
        wrecv(gm_out.at[m, r_up, c], R_FA + 3 * m + 1)
        send(hi, hi, S_FB + 2 * m + 1, R_FB + 2 * m + 1, dev_dn, lambda: r1b.at[0, 0])
        full2 = gm_out.at[m, r_up, c]
        send(full2, full2, S_FC + 3 * m + 1, R_FC + 3 * m + 1, dev_pair, lambda: fs.at[m])

    def g_ag2(m):
        wrecv(gm_out.at[m, r_op, c, pl.ds(0, 48)], R_FB + 2 * m)
        wrecv(gm_out.at[m, r_op, c, pl.ds(48, 48)], R_FB + 2 * m + 1)
        full = gm_out.at[m, r_op, c]
        send(full, full, S_FC + 3 * m + 2, R_FC + 3 * m + 2, dev_pair, lambda: fs.at[m])

    def g_end(m):
        wrecv(gm_out.at[m, r, oc], R_FA + 3 * m + 2)
        wrecv(gm_out.at[m, r_dn, oc], R_FC + 3 * m)
        wrecv(gm_out.at[m, r_up, oc], R_FC + 3 * m + 1)
        wrecv(gm_out.at[m, r_op, oc], R_FC + 3 * m + 2)

    GA_ = 0.7978845608028654

    def mlp_body(i, _):
        zp = (z - i + 4) % 4

        def got(dz):
            mg_done(0, dz)
            mg_done(1, dz)

        for dz in (1, 2, 3):
            pl.when(i == dz)(functools.partial(got, dz))
        for fb in range(D // 256):
            cols = slice(fb * 256, fb * 256 + 256)
            fcb = wmlp[0, zp, :, :, :, cols].reshape(D, 256)
            pre = dot(n2[...], fcb) + bfa[zp, 0:1, cols]
            sq = pre * pre
            t = jnp.tanh(GA_ * (pre + 0.044715 * (pre * sq)))
            hf = 0.5 * (1.0 + t)
            act[:, cols] = (pre * hf).astype(BF)
            gp = hf + (0.5 * GA_) * pre * (1.0 - t * t) * (1.0 + 0.134145 * sq)
            prj = wmlp[1, zp].reshape(D, D)[cols, :]
            dp_ = (nt(og[...], prj) * gp).astype(BF)
            dpre[:, cols] = dp_
            sb[pl.ds(6 + zp, 1), cols] = jnp.sum(dp_.astype(F32), axis=0, keepdims=True)
        prj = wmlp[1, zp].reshape(D, D)
        fc = wmlp[0, zp].reshape(D, D)
        for rb in range(R // 256):
            rows = slice(rb * 256, rb * 256 + 256)
            oacc[rows, :] += dot(act[rows, :], prj)
            dn2[rows, :] += nt(dpre[rows, :], fc)
        for j in range(2):
            cols = slice(j * HC, j * HC + HC)
            wmlp[1, zp, 2 * j : 2 * j + 2] = tn(act[:, cols], og[...]).astype(BF).reshape(2, 2, D // 8, D)
        for j in range(2):
            cols = slice(j * HC, j * HC + HC)
            wmlp[0, zp, 2 * j : 2 * j + 2] = tn(n2[:, cols], dpre[...]).astype(BF).reshape(2, 2, D // 8, D)

        def after(kk_):
            if kk_ >= 1:
                for m in (1, 0):
                    g_s1(m, kk_ - 1)
            g_s0(1, kk_)
            g_s0(0, kk_)

        for kk_ in range(4):
            pl.when(i == kk_)(functools.partial(after, kk_))
        return 0

    mg_round(7)
    lax.fori_loop(0, 4, mlp_body, 0)

    def bwd2_body(i, _):
        rows = pl.ds(al(i * LB, LB), LB)
        x = mid[rows, :]
        p0 = lax.broadcasted_iota(jnp.int32, (LB, 1), 0).astype(F32) + (row0 + i * LB).astype(F32)
        ok = jnp.where(p0 < length, 1.0, 0.0)
        bo[rows, :] = ((x + oacc[rows, :] + vecs[5:6, :]) * ok).astype(BF)
        n, rstd = stats(x)
        dn = dn2[rows, :]
        e = dn * vecs[3:4, :]
        em = jnp.mean(e, axis=1, keepdims=True)
        en = jnp.mean(e * n, axis=1, keepdims=True)
        gm = og[rows, :].astype(F32) + (e - em - n * en) * rstd
        mid[rows, :] = gm
        ga[pl.ds(al(row0 + i * LB, LB), LB), :] = gm.astype(BF)
        sb[2:3, :] += jnp.sum(dn * n, axis=0, keepdims=True)
        sb[3:4, :] += jnp.sum(dn, axis=0, keepdims=True)
        sb[4:5, :] += jnp.sum(gm, axis=0, keepdims=True)
        return 0

    lax.fori_loop(0, R // LB, bwd2_body, 0)
    send(ga.at[mine_rows], ga.at[mine_rows], S_GA, R_GA, dev_pair, lambda: ga.at[mine_rows])
    when(swap, lambda: send(bo, bo_out, S_BO, R_BO, dev_swap, lambda: bo, swap))
    w_bo = local(lambda: bo, lambda: bo_out, keep)
    wrecv(ga.at[pair_rows], R_GA)

    def dctx_body(i, _):
        rows = pl.ds(al(i * BQ, BQ), BQ)
        d = nt(ga[rows, :], watt[3])
        do[rows, :] = d.astype(BF)
        for hp in range(3):
            lanes = slice(hp * 128, hp * 128 + 128)
            dot_[lanes, rows] = do[rows, lanes].T
        return 0

    lax.fori_loop(0, NB, dctx_body, 0)

    def a_s1(hp):
        g = gatt.at[hp]
        send(g.at[r_op, pl.ds(0, 64)], a1b.at[hp, 0], S_A1 + 2 * hp, R_A1 + 2 * hp, dev_up, lambda: a1b.at[hp, 0])
        send(g.at[r_op, pl.ds(64, 64)], a1b.at[hp, 1], S_A1 + 2 * hp + 1, R_A1 + 2 * hp + 1, dev_dn,
             lambda: a1b.at[hp, 1])

    def a_s2(hp):
        g = gatt.at[hp]
        wrecv(a1b.at[hp, 0], R_A1 + 2 * hp)
        add_into(g.at[r_up, pl.ds(0, 64)], a1b.at[hp, 0])
        send(g.at[r_up], a2b.at[hp, 0], S_A2 + 2 * hp, R_A2 + 2 * hp, dev_up, lambda: a2b.at[hp, 0])
        wrecv(a1b.at[hp, 1], R_A1 + 2 * hp + 1)
        add_into(g.at[r_dn, pl.ds(64, 64)], a1b.at[hp, 1])
        send(g.at[r_dn], a2b.at[hp, 1], S_A2 + 2 * hp + 1, R_A2 + 2 * hp + 1, dev_dn, lambda: a2b.at[hp, 1])

    parts = [(0, 0, 128, 0, 0), (1, 0, 64, 0, 128), (1, 64, 64, 1, 0), (2, 0, 128, 1, 64)]

    def a_s3(hp):
        g = gatt.at[hp]
        wrecv(a2b.at[hp, 0], R_A2 + 2 * hp)
        wrecv(a2b.at[hp, 1], R_A2 + 2 * hp + 1)
        add_into(g.at[r], a2b.at[hp, 0], a2b.at[hp, 1])
        for pi, (ph, lo, n, zz, to) in enumerate(parts):
            if ph != hp:
                continue

            def go(pi=pi, lo=lo, n=n, zz=zz, to=to):
                zd = 2 * c + zz
                slot = (zd - z + 3) % 4
                send(g.at[r, pl.ds(lo, n)], azb.at[slot, pl.ds(to, n)], S_AZ + pi,
                     R_AZ + 3 * pi + slot, (dp, zd), lambda: gatt.at[hp, 0, pl.ds(lo, n)], need(zz))

            pl.when(need(zz))(go)

    def a_fin(zz):
        for pi, (ph, lo, n, zo, to) in enumerate(parts):
            if zo != zz:
                continue
            for slot in range(3):
                wrecv(azb.at[slot, pl.ds(to, n)], R_AZ + 3 * pi + slot)
            t = gatt[ph, r, lo : lo + n].astype(F32)
            for slot in range(3):
                t = t + azb[slot, to : to + n].astype(F32)
            fa[to : to + n] = t.astype(BF)

    def a_ag():
        for i, dev in enumerate((dev_up, dev_dn, dev_pair)):
            send(fa, ga_out.at[r], S_HA + i, R_HA + i, dev, lambda: fa, own_c)

    def a_ag2():
        lo = ga_out.at[r_dn, pl.ds(0, half)]
        hi = ga_out.at[r_up, pl.ds(half, half)]
        wrecv(ga_out.at[r_dn], R_HA)
        send(lo, lo, S_HB, R_HB, dev_up, lambda: fa.at[pl.ds(0, half)], own_c)
        send(ga_out.at[r_dn], ga_out.at[r_dn], S_HC, R_HC, dev_pair, lambda: fa, own_c)
        wrecv(ga_out.at[r_up], R_HA + 1)
        send(hi, hi, S_HB + 1, R_HB + 1, dev_dn, lambda: fa.at[pl.ds(0, half)], own_c)
        send(ga_out.at[r_up], ga_out.at[r_up], S_HC + 1, R_HC + 1, dev_pair, lambda: fa, own_c)

    def a_ag3():
        wrecv(ga_out.at[r_op, pl.ds(0, half)], R_HB)
        wrecv(ga_out.at[r_op, pl.ds(half, half)], R_HB + 1)
        send(ga_out.at[r_op], ga_out.at[r_op], S_HC + 2, R_HC + 2, dev_pair, lambda: fa, own_c)

    def a_end():
        wrecv(ga_out.at[r], R_HA + 2)
        wrecv(ga_out.at[r_dn], R_HC)
        wrecv(ga_out.at[r_up], R_HC + 1)
        wrecv(ga_out.at[r_op], R_HC + 2)

    def bwd_head(hp, hh):
        h = hp * 2 + hh
        lanes, inhead = head_prep(hp, hh)
        hrows = pl.ds(al(h * 64, 64), 64)
        vh[...] = jnp.where(inhead, v[:, lanes].astype(F32), 0.0).astype(BF)
        dl = jnp.sum(dot_[hrows, :].astype(F32) * ot[hrows, :].astype(F32), axis=0, keepdims=True)
        ls_h = lse[h]
        for kb in range(NB):
            krows = slice(kb * BQ, kb * BQ + BQ)
            qs = slice(kb * BQ, T)
            s = dot(kh[krows, :], qh[:, qs])
            diag = s[:, :BQ] + cmask[...]
            s = diag if kb == NB - 1 else jnp.concatenate([diag, s[:, BQ:]], axis=1)
            p = jnp.exp2(s * CS - ls_h[0:1, qs])
            dpr = dot(vh[krows, :], dot_[lanes, qs])
            ds = (p * (dpr - dl[:, qs])).astype(BF)
            dv = dot(p.astype(BF), do[qs, lanes])
            dk = dot(ds, q[qs, lanes]) * 0.125
            v[krows, lanes] = jnp.where(inhead, dv, v[krows, lanes].astype(F32)).astype(BF)
            k[krows, lanes] = jnp.where(inhead, dk, k[krows, lanes].astype(F32)).astype(BF)
            piece = dot(kt[hrows, krows], ds)
            if kb == 0:
                dqa[...] = piece
            else:
                dqa[:, qs] += piece
        qt[hrows, :] = (dqa[...] * 0.125).astype(BF)

    def bwd_pair(hp, _):
        def head(hh, _):
            bwd_head(hp, hh)
            return 0

        lax.fori_loop(0, 2, head, 0)
        lanes = pl.ds(al(hp * 128, 128), 128)

        def tr2(i, _):
            rows = pl.ds(al(i * BQ, BQ), BQ)
            q[rows, lanes] = qt[lanes, rows].T
            kt[lanes, rows] = k[rows, lanes].T
            vt[lanes, rows] = v[rows, lanes].T
            return 0

        lax.fori_loop(0, NB, tr2, 0)
        for t, ref in enumerate((qt, kt, vt)):
            gatt[hp, t] = dot(ref[lanes, :], n1[...]).astype(BF)
        gatt[hp, 3] = dot(ot[lanes, :], ga[...]).astype(BF)
        for j in range(3):
            pl.when(hp == j)(functools.partial(after_pair, j))
        return 0

    def after_pair(j):
        if j == 0:
            for i in range(3):
                for m in (1, 0):
                    g_s2(m, i)
            for m in (1, 0):
                g_s1(m, 3)
            a_s1(0)
        if j == 1:
            for i in range(3):
                for m in (1, 0):
                    g_s3(m, i)
            for m in (1, 0):
                g_s2(m, 3)
            a_s2(0)
            a_s1(1)
        if j == 2:
            for m in (1, 0):
                g_s3(m, 3)
            a_s2(1)
            a_s1(2)
            a_s3(0)
            for m in (1, 0):
                g_fin(m)

    lax.fori_loop(0, 3, bwd_pair, 0)

    def dx(rows):
        return dot(q[rows, :], watt[0]) + dot(k[rows, :], watt[1]) + dot(v[rows, :], watt[2])

    ps2[...] = dx(pair_rows).astype(BF)
    send(ps2, pr2, S_DX, R_DX, dev_pair, lambda: ps2)
    a_s2(2)
    a_s3(1)
    for m in (1, 0):
        g_ag(m)
    dn2[...] = dx(mine_rows)
    a_s3(2)
    sb[pl.ds(10 + c, 1), :] = jnp.concatenate(
        [jnp.sum(q[...].astype(F32), axis=0, keepdims=True), jnp.sum(v[...].astype(F32), axis=0, keepdims=True)],
        axis=1,
    )
    wrecv(pr2, R_DX)

    def bwd1_body(i, _):
        rows = pl.ds(al(i * LB, LB), LB)
        n, rstd = stats(hid[rows, :].astype(F32))
        dn = dn2[rows, :] + pr2[rows, :].astype(F32)
        e = dn * vecs[0:1, :]
        em = jnp.mean(e, axis=1, keepdims=True)
        en = jnp.mean(e * n, axis=1, keepdims=True)
        gi[rows, :] = (mid[rows, :] + (e - em - n * en) * rstd).astype(BF)
        sb[0:1, :] += jnp.sum(dn * n, axis=0, keepdims=True)
        sb[1:2, :] += jnp.sum(dn, axis=0, keepdims=True)
        return 0

    lax.fori_loop(0, R // LB, bwd1_body, 0)
    when(swap, lambda: send(gi, gi_out, S_GI, R_GI, dev_swap, lambda: gi, swap))
    w_gi = local(lambda: gi, lambda: gi_out, keep)

    p_ra = (ring_dp(r + 1 - 2 * (r % 2), c), z)
    p_rb = (ring_dp((r + 3 + 2 * (r % 2)) % RING, c), z)
    stages = [dev_pair, p_ra, p_rb, (dp, z_x), dev_z[2]]

    def small_step(j):
        send(sb.at[pl.ds(16 * j, 16)], srb.at[j], S_SM + j, R_SM + j, stages[j], lambda: srb.at[j])

    def small_add(j):
        wrecv(srb.at[j], R_SM + j)
        t = sb[16 * j : 16 * j + 16] + srb[j]
        if j < 4:
            sb[16 * j + 16 : 16 * j + 32] = t
        else:
            small_out[...] = t

    small_step(0)
    for m in (1, 0):
        g_ag2(m)
    small_add(0)
    small_step(1)
    for zz in (0, 1):
        when(z == 2 * c + zz, functools.partial(a_fin, zz))
    when(own_c, a_ag)
    small_add(1)
    small_step(2)
    when(own_c, a_ag2)
    small_add(2)
    small_step(3)
    when(own_c, a_ag3)
    small_add(3)
    small_step(4)
    small_add(4)

    w_fs = [local(lambda: fs.at[0], lambda: gm_out.at[0, r, c]), local(lambda: fs.at[1], lambda: gm_out.at[1, r, c])]
    w_fa = local(lambda: fa, lambda: ga_out.at[r], own_c)
    w_bo()
    w_gi()
    for w in w_fs:
        w()
    w_fa()
    for m in (0, 1):
        g_end(m)
    when(not_own, a_end)
    when(swap, lambda: wrecv(bo_out, R_BO))
    when(swap, lambda: wrecv(gi_out, R_GI))
    for sid, (ref, cond) in pending.items():
        when(cond, lambda sid=sid, ref=ref: wsend(ref(), sid))


def body(
    hidden_in, lengths, ln1_gain, ln1_bias, w_qkv, b_query, b_value, w_out, b_out,
    ln2_gain, ln2_bias, w_fc, b_fc, w_proj, b_proj, out_grad,
):
    R, D = hidden_in.shape
    T, HC, ZS, EB = 2 * R, D // 2, D // 4, D // 8
    z = lax.axis_index("tensor")
    lens = jnp.broadcast_to(jnp.where(z // 2 == 0, lengths[0], lengths[1]).astype(F32), (8, 128))
    zero = jnp.zeros((ZS,), BF)
    odd = z % 2 == 1
    qv_row = jnp.concatenate(
        [
            jnp.where(odd, zero, b_query), jnp.where(odd, b_query, zero),
            jnp.where(odd, zero, b_value), jnp.where(odd, b_value, zero),
        ]
    )
    blank = jnp.zeros((D,), BF)
    bias = jnp.stack([b_fc, qv_row] + [blank] * 6).astype(F32)
    vecs = jnp.stack([ln1_gain, ln1_bias, b_out, ln2_gain, ln2_bias, b_proj, blank, blank]).astype(F32)
    wq = jnp.transpose(w_qkv, (1, 2, 0))
    wf = w_fc.reshape(4, 2, EB, D)
    wp = w_proj.reshape(4, 2, EB, D)
    vm = lambda *s: pltpu.VMEM(s, BF)
    vf = lambda *s: pltpu.VMEM(s, F32)
    scratch = [
        vf(8, 128), vf(4, 8, D), vm(R, D), vm(R, D), vm(T, D), vm(4, HC, D), vm(2, 4, 4, 2, EB, D),
        vm(T, HC), vm(T, HC), vm(T, HC), vm(HC, T), vm(HC, T), vm(HC, T),
        vm(T, HC), vm(HC, T), vm(HC, T), vm(T, HC),
        vf(R, D), vm(R, D), vf(R, D), vf(R, D), vm(R, D), vm(R, D), vm(T, D),
        vm(R, D), vm(R, D), vm(R, D), vm(R, D), vm(R, D), vm(R, D),
        vf(6, 1, T), vf(64, T), vf(256, 256), vm(T, 128), vm(T, 128), vm(128, T),
        vm(8, 4, EB, D), vm(8, 2, EB // 2, D), vm(8, 2, EB, D), vm(2, 3, EB, D), vm(2, EB, D),
        vm(3, 4, 128, D), vm(3, 2, 64, D), vm(3, 2, 128, D), vm(3, ZS, D), vm(ZS, D),
        vf(80, D), vf(5, 16, D),
        pltpu.SemaphoreType.DMA((SID.n,)), pltpu.SemaphoreType.DMA((RID.n,)), pltpu.SemaphoreType.DMA((12,)),
    ]
    anyspec = pl.BlockSpec(memory_space=pl.ANY)
    vspec = pl.BlockSpec(memory_space=pltpu.VMEM)
    block_out, grad_input, gm, gatt, small = pl.pallas_call(
        kernel,
        out_shape=(
            jax.ShapeDtypeStruct((R, D), BF),
            jax.ShapeDtypeStruct((R, D), BF),
            jax.ShapeDtypeStruct((2, 4, 2, EB, D), BF),
            jax.ShapeDtypeStruct((4, ZS, D), BF),
            jax.ShapeDtypeStruct((16, D), F32),
        ),
        in_specs=[vspec] * 3 + [anyspec] * 6,
        out_specs=(anyspec, anyspec, anyspec, anyspec, vspec),
        scratch_shapes=scratch,
        compiler_params=pltpu.CompilerParams(
            collective_id=0, has_side_effects=True, vmem_limit_bytes=64 * 1024 * 1024 - 65536
        ),
        name="layer",
    )(lens, bias, vecs, hidden_in, out_grad, wq, w_out, wf, wp)
    data_count = lax.axis_size("dp")
    gm = gm.astype(F32)
    gatt = gatt.astype(F32)
    if data_count > GROUP:
        groups = [list(range(s, data_count, GROUP)) for s in range(GROUP)]
        gm, gatt, small = (lax.psum(t, "dp", axis_index_groups=groups) for t in (gm, gatt, small))
    g_fc = gm[0].reshape(D, D)
    g_proj = gm[1].reshape(D, D)
    g_qkv = jnp.transpose(gatt[:3], (2, 0, 1))
    b_fc_g = lax.dynamic_index_in_dim(small, 6 + z, 0, keepdims=False)
    b_row = lax.dynamic_index_in_dim(small, 10 + z // 2, 0, keepdims=False)
    gbq = jnp.where(odd, b_row[ZS : 2 * ZS], b_row[:ZS])
    gbv = jnp.where(odd, b_row[3 * ZS :], b_row[2 * ZS : 3 * ZS])
    return (
        block_out, grad_input, small[0], small[1], g_qkv, gbq, gbv, gatt[3], small[4],
        small[2], small[3], g_fc, b_fc_g, g_proj, small[5],
    )


def solution(mesh):
    rows = P(("dp", "tensor"), None)
    in_specs = (
        rows, P("dp"), P(), P(), P(None, None, "tensor"), P("tensor"), P("tensor"), P("tensor", None),
        P(), P(), P(), P(None, "tensor"), P("tensor"), P("tensor", None), P(), rows,
    )
    out_specs = (
        rows, rows, P(), P(), P(None, None, "tensor"), P("tensor"), P("tensor"), P("tensor", None),
        P(), P(), P(), P(None, "tensor"), P("tensor"), P("tensor", None), P(),
    )
    return jax.shard_map(body, mesh=mesh, in_specs=in_specs, out_specs=out_specs, check_vma=False)
```

```python
import functools

import jax
import jax.numpy as jnp
from jax import lax
from jax.experimental import pallas as pl
from jax.experimental.pallas import tpu as pltpu
from jax.sharding import PartitionSpec as P

BF = jnp.bfloat16
F32 = jnp.float32
EPS = 1e-5
NEG = -1e30
LOG2E = 1.4426950408889634
MESH = pl.DeviceIdType.MESH
RING = 4
GROUP = 2 * RING


T_LOOP = (("", "10"), ("11 20", "12"), ("13 21", "14"), ("15 22", "16"))
T_BWD2 = "17 23 30"
T_DCTX = "31"
T_ATT = (("24", "32", "25", "33"), ("26", "34", "27", "35"), ("28", "36", "29", "37"))
T_PAIR = ("18", "19", "110")
T_DX = "38"
T_DX2 = "210 39"
T_LAST = "310"
G_EARLY = ""
G_QKV = "a0"
G_TR = ""
G_ATT = (("a1", "", "b0", ""), ("b1 a2", "", "p0 a3", "p1"), ("b2", "", "b3 p2", "a4"))
G_CTX = ""
G_MLP = "p3 a5"
G_LOOP = (("b4", "b5"), ("p4", "p5"), ("", ""), ("", ""))


def dot(a, b, ca=1, cb=0):
    return lax.dot_general(a, b, (((ca,), (cb,)), ((), ())), preferred_element_type=F32)


def nt(a, b):
    return dot(a, b, 1, 1)


def tn(a, b):
    return dot(a, b, 0, 0)


def al(v, m):
    return pl.multiple_of(v, m)


class Ids:
    def __init__(self):
        self.n = 0

    def __call__(self, k):
        base = self.n
        self.n += k
        return base


SID = Ids()
S_LEN, S_BIAS, S_HID, S_OG, S_AS1 = SID(1), SID(3), SID(1), SID(1), SID(3)
S_ARA, S_ARB = SID(4), SID(4)
S_MS1, S_MRA, S_MRB, S_MP = SID(6), SID(12), SID(12), SID(6)
S_N1, S_PO, S_GA, S_DX, S_BO, S_GI = SID(1), SID(1), SID(1), SID(1), SID(1), SID(8)
S_GP, S_G1, S_G2, S_GZ = SID(8), SID(16), SID(16), SID(8)
S_FA, S_FB, S_FC = SID(6), SID(4), SID(6)
S_A1, S_A2, S_AZ = SID(6), SID(6), SID(4)
S_HA, S_HB, S_HC = SID(3), SID(2), SID(3)
S_SM = SID(7)
RID = Ids()
R_LEN, R_BIAS, R_HID, R_OG, R_AS1 = RID(1), RID(3), RID(1), RID(1), RID(2)
R_ARA, R_ARB = RID(4), RID(4)
R_MS1, R_MRA, R_MRB, R_MP = RID(6), RID(12), RID(12), RID(6)
R_N1, R_PO, R_GA, R_DX, R_BO, R_GI = RID(1), RID(1), RID(1), RID(1), RID(1), RID(8)
R_GP, R_G1, R_G2, R_GZ = RID(8), RID(16), RID(16), RID(6)
R_FA, R_FB, R_FC = RID(6), RID(4), RID(6)
R_A1, R_A2, R_AZ = RID(6), RID(6), RID(12)
R_HA, R_HB, R_HC = RID(3), RID(2), RID(3)
R_SM = RID(9)


def kernel(
    lengths, vecs, hid_in, og_in, wq, wo, wf, wp,
    bo_out, gi_out, gm_out, ga_out, small_out,
    lens, lrecv, bfa, hid, og, n1, watt, wmlp, q, k, v, qt, kt, vt, do, dot_, ot, ctx,
    mid, n2, oacc, dn2, act, dpre, ga, ps, pr, ps2, pr2, bo, gi,
    lse, dqa, cmask, kh, vh, qh,
    prb, r1b, r2b, zb, fs, gatt, a1b, a2b, azb, fa, sb, srb,
    ss, rs, ls,
):
    D = hid_in.shape[1]
    R = hid_in.shape[0]
    T = 2 * R
    HC = D // 2
    BQ = 256
    NB = T // BQ
    dp = lax.axis_index("dp")
    z = lax.axis_index("tensor")
    base = (dp // GROUP) * GROUP
    chip = (dp - base) // 2
    c = dp % 2
    oc = 1 - c
    cy = chip // 2
    cx = chip % 2
    r = 3 * cy + cx - 2 * cx * cy

    def ring_dp(rr, core):
        y = rr // 2
        x = rr % 2 + y - 2 * (rr % 2) * y
        return base + (2 * y + x) * 2 + core

    r_up = (r + 1) % RING
    r_dn = (r + 3) % RING
    r_op = (r + 2) % RING
    dev_up = (ring_dp(r_up, c), z)
    dev_dn = (ring_dp(r_dn, c), z)
    dev_op = (ring_dp(r_op, c), z)
    dev_pair = (dp + 1 - 2 * c, z)
    dev_z = [None] + [(dp, (z + dz) % 4) for dz in (1, 2, 3)]
    z_x = z + 1 - 2 * (z % 2)
    dev_swap = (dp + 1 - 2 * c, z_x)
    keep = c == z % 2
    swap = c != z % 2
    own_c = z // 2 == c
    not_own = z // 2 != c
    zz_own = z % 2
    pending = {}

    def when(cond, fn):
        if cond is None:
            fn()
        else:
            pl.when(cond)(fn)

    def desc(src, dst, sid, rid, dev):
        return pltpu.make_async_remote_copy(
            src_ref=src, dst_ref=dst, send_sem=ss.at[sid], recv_sem=rs.at[rid],
            device_id=dev, device_id_type=MESH,
        )

    def send(src, dst, sid, rid, dev, late=None, cond=None):
        desc(src, dst, sid, rid, dev).start()
        if late is not None:
            pending[sid] = (late, cond)

    def wsend(ref, sid):
        desc(ref, ref, sid, 0, dev_pair).wait_send()

    def wrecv(ref, rid):
        desc(ref, ref, 0, rid, dev_pair).wait_recv()

    barrier = pltpu.get_barrier_semaphore()
    cross = [(dp + 1 - 2 * c, (z + dz) % 4) for dz in (1, 2, 3)]
    for dev in (dev_up, dev_dn, dev_op, dev_pair, dev_z[1], dev_z[2], dev_z[3], *cross):
        pl.semaphore_signal(barrier, inc=1, device_id=dev, device_id_type=MESH)

    loc_n = [0]

    def local(src, dst, cond=None):
        i = loc_n[0]
        loc_n[0] += 1
        cp = lambda: pltpu.make_async_copy(src(), dst(), ls.at[i])
        when(cond, lambda: cp().start())
        return lambda: when(cond, lambda: cp().wait())

    w_hid = local(lambda: hid_in, lambda: hid, keep)
    bias = vecs.at[pl.ds(8, 8)]
    ZS = D // 4

    def att_rows(zz):
        return pl.ds(al(zz * ZS, 16), ZS)

    def att_s1():
        for dz in (1, 2, 3):
            dst = watt.at[r, att_rows(zz_own)]

            dev = (dp - c + z // 2, (z + dz) % 4)

            def from_q():
                send(wq.at[jnp.minimum(r, 2)], dst, S_AS1 + dz - 1, R_AS1 + zz_own, dev)

            def from_o():
                send(wo, dst, S_AS1 + dz - 1, R_AS1 + zz_own, dev)

            pl.when(r < 3)(from_q)
            pl.when(r == 3)(from_o)
            pending[S_AS1 + dz - 1] = (lambda: wo, swap)

    w_wq = local(lambda: wq, lambda: watt.at[pl.ds(0, 3), att_rows(zz_own)], own_c)
    w_wo = local(lambda: wo, lambda: watt.at[3, att_rows(zz_own)], own_c)
    w_og = local(lambda: og_in, lambda: og, keep)
    w_mlp0 = [local(lambda: wf, lambda: wmlp.at[0, z]), local(lambda: wp, lambda: wmlp.at[1, z])]
    def zsh(dz):
        return (z - dz + 4) % 4

    def mg_s1(m, dz):
        w = (wf, wp)[m]
        u = m * 3 + dz - 1
        send(w.at[r, c], wmlp.at[m, z, r, c], S_MS1 + u, R_MS1 + u, dev_z[dz], lambda: w.at[r, c])

    def mg_a(m, dz):
        u = m * 3 + dz - 1
        piece = wmlp.at[m, zsh(dz), r, c]
        wrecv(piece, R_MS1 + u)
        send(piece, piece, S_MRA + 2 * u, R_MRA + 2 * u, dev_up)
        send(piece, piece, S_MRA + 2 * u + 1, R_MRA + 2 * u + 1, dev_dn)

    def mg_b(m, dz):
        u = m * 3 + dz - 1
        zp = zsh(dz)
        wrecv(wmlp.at[m, zp, r_dn, c], R_MRA + 2 * u)
        lo = wmlp.at[m, zp, r_dn, c, pl.ds(0, 48)]
        send(lo, lo, S_MRB + 2 * u, R_MRB + 2 * u, dev_up)
        wrecv(wmlp.at[m, zp, r_up, c], R_MRA + 2 * u + 1)
        hi = wmlp.at[m, zp, r_up, c, pl.ds(48, 48)]
        send(hi, hi, S_MRB + 2 * u + 1, R_MRB + 2 * u + 1, dev_dn)

    def mg_p(m, dz):
        u = m * 3 + dz - 1
        zp = zsh(dz)
        wrecv(wmlp.at[m, zp, r_op, c, pl.ds(0, 48)], R_MRB + 2 * u)
        wrecv(wmlp.at[m, zp, r_op, c, pl.ds(48, 48)], R_MRB + 2 * u + 1)
        mine = wmlp.at[m, zp, :, c]
        send(mine, mine, S_MP + u, R_MP + u, dev_pair)

    def mg_done(m, dz):
        u = m * 3 + dz - 1
        zp = zsh(dz)
        wrecv(wmlp.at[m, zp, :, oc], R_MP + u)
        for s in (0, 1):
            wsend(wmlp.at[m, zp, r, c], S_MRA + 2 * u + s)
            wsend(wmlp.at[m, zp, r, c, pl.ds(0, 48)], S_MRB + 2 * u + s)
        wsend(wmlp.at[m, zp, :, c], S_MP + u)

    munits = [(0, 1), (1, 1), (0, 3), (1, 3), (0, 2), (1, 2)]

    def mg(steps):
        for st in steps.split():
            {"a": mg_a, "b": mg_b, "p": mg_p}[st[0]](*munits[int(st[1])])

    row0 = c * R
    half = ZS // 2

    def stats(x):
        mu = jnp.mean(x, axis=1, keepdims=True)
        cen = x - mu
        var = jnp.mean(cen * cen, axis=1, keepdims=True)
        rstd = lax.rsqrt(var + EPS)
        return cen * rstd, rstd

    LB = 128

    def ln1_body(i, _):
        rows = pl.ds(al(i * LB, LB), LB)
        n, _r = stats(hid[rows, :].astype(F32))
        out = n * vecs[0:1, :] + vecs[1:2, :]
        n1[pl.ds(al(row0 + i * LB, LB), LB), :] = out.astype(BF)
        return 0

    mine_rows = pl.ds(al(row0, R), R)
    pair_rows = pl.ds(al(oc * R, R), R)

    def norm_one():
        lax.fori_loop(0, R // LB, ln1_body, 0)

    def norm_one_send():
        send(n1.at[mine_rows], n1.at[mine_rows], S_N1, R_N1, dev_pair, lambda: n1.at[mine_rows])

    def norm_one_far():
        wrecv(hid, R_HID)
        norm_one()
        norm_one_send()

    bfa[z] = bias[...]
    w_hid()
    pl.when(keep)(norm_one)

    kk = lax.broadcasted_iota(jnp.int32, (BQ, BQ), 0)
    qq = lax.broadcasted_iota(jnp.int32, (BQ, BQ), 1)
    cmask[...] = jnp.where(kk <= qq, 0.0, NEG)
    pl.semaphore_wait(barrier, 10)
    pl.when(swap)(att_s1)
    when(swap, lambda: send(hid_in, hid, S_HID, R_HID, dev_swap, lambda: hid_in, swap))
    for dz in (1, 2, 3):
        send(bias, bfa.at[z], S_BIAS + dz - 1, R_BIAS + dz - 1, dev_z[dz], lambda: bias)
    lens[...] = jnp.full((8, 128), lengths[z // 2].astype(F32))
    send(lens, lrecv, S_LEN, R_LEN, dev_pair, lambda: lens)
    pl.when(keep)(norm_one_send)

    needs = (z != 2 * c, z != 2 * c + 1)

    def need(zz):
        return needs[zz]

    def ar_a(zz):
        piece = watt.at[r, att_rows(zz)]
        wrecv(piece, R_AS1 + zz)
        send(piece, piece, S_ARA + 2 * zz, R_ARA + 2 * zz, dev_up, lambda: wo, need(zz))
        send(piece, piece, S_ARA + 2 * zz + 1, R_ARA + 2 * zz + 1, dev_dn, lambda: wo, need(zz))

    def ar_b(zz):
        wrecv(watt.at[r_dn, att_rows(zz)], R_ARA + 2 * zz)
        lo = watt.at[r_dn, pl.ds(al(zz * ZS, 16), half)]
        send(lo, lo, S_ARB + 2 * zz, R_ARB + 2 * zz, dev_up, lambda: watt.at[0, pl.ds(0, half)], need(zz))
        wrecv(watt.at[r_up, att_rows(zz)], R_ARA + 2 * zz + 1)
        hi = watt.at[r_up, pl.ds(al(zz * ZS + half, 16), half)]
        send(hi, hi, S_ARB + 2 * zz + 1, R_ARB + 2 * zz + 1, dev_dn, lambda: watt.at[0, pl.ds(0, half)], need(zz))

    def ar_c(zz):
        wrecv(watt.at[r_op, pl.ds(al(zz * ZS, 16), half)], R_ARB + 2 * zz)
        wrecv(watt.at[r_op, pl.ds(al(zz * ZS + half, 16), half)], R_ARB + 2 * zz + 1)

    for zz in (0, 1):
        when(need(zz), functools.partial(ar_a, zz))
    for dz in (1, 3):
        mg_s1(0, dz)
        mg_s1(1, dz)
    for zz in (0, 1):
        when(need(zz), functools.partial(ar_b, zz))
    pl.when(swap)(norm_one_far)
    mg_s1(0, 2)
    mg_s1(1, 2)
    when(swap, lambda: send(og_in, og, S_OG, R_OG, dev_swap, lambda: og_in, swap))
    mg(G_EARLY)
    for zz in (0, 1):
        when(need(zz), functools.partial(ar_c, zz))
    w_wq()
    w_wo()
    for dz in (1, 2, 3):
        wrecv(bfa.at[zsh(dz)], R_BIAS + dz - 1)
    wrecv(lrecv, R_LEN)
    keepf = 1.0 - (c + z % 2 - 2 * c * (z % 2)).astype(F32)
    length = lens[0:1, 0:1] * keepf + lrecv[0:1, 0:1] * (1.0 - keepf)
    wrecv(n1.at[pair_rows], R_N1)

    bqv = bfa[2 * c, 1:2, :] + bfa[2 * c + 1, 1:2, :]

    def qkv_body(i, _):
        rows = pl.ds(al(i * BQ, BQ), BQ)
        x = n1[rows, :]
        q[rows, :] = (nt(x, watt[0]) + bqv[:, :HC]).astype(BF)
        k[rows, :] = nt(x, watt[1]).astype(BF)
        v[rows, :] = (nt(x, watt[2]) + bqv[:, HC:]).astype(BF)
        return 0

    lax.fori_loop(0, NB, qkv_body, 0)
    mg(G_QKV)

    def tr_body(i, _):
        rows = pl.ds(al(i * BQ, BQ), BQ)
        for hp in range(3):
            lanes = slice(hp * 128, hp * 128 + 128)
            qt[lanes, rows] = q[rows, lanes].T
            kt[lanes, rows] = k[rows, lanes].T
            vt[lanes, rows] = v[rows, lanes].T
        return 0

    lax.fori_loop(0, NB, tr_body, 0)
    mg(G_TR)

    lane = lax.broadcasted_iota(jnp.int32, (1, 128), 1)
    sub = lax.broadcasted_iota(jnp.int32, (128, 1), 0)
    pos = lax.broadcasted_iota(jnp.int32, (T, 1), 0).astype(F32)
    keybias = jnp.where(pos < length, 0.0, NEG)
    CS = 0.125 * LOG2E

    def head_prep(hp, hh):
        lanes = pl.ds(al(hp * 128, 128), 128)
        inhead = (lane // 64) == hh
        aux = lane == (1 - hh) * 64
        kp = k[:, lanes].astype(F32)
        kh[hh] = jnp.where(inhead, kp, jnp.where(aux, keybias, 0.0)).astype(BF)
        qp = qt[lanes, :].astype(F32)
        qh[hh] = jnp.where(sub == (1 - hh) * 64, 1.0, qp).astype(BF)
        return lanes, inhead

    def by_pair(hp, run, steps):
        for j in range(3):
            if steps[j]:
                pl.when(hp == j)(functools.partial(run, steps[j]))

    def fwd_pair(hp, _):
        for hh in (0, 1):
            head_prep(hp, hh)
        for qb in range(NB):
            nk = (qb + 1) * BQ
            cols = slice(qb * BQ, nk)
            for hh in (0, 1):
                h = hp * 2 + hh
                hrows = pl.ds(al(h * 64, 64), 64)
                s = dot(kh[hh, :nk, :], qh[hh, :, cols])
                diag = s[nk - BQ :] + cmask[...]
                s = diag if qb == 0 else jnp.concatenate([s[: nk - BQ], diag], axis=0)
                m = jnp.max(s, axis=0, keepdims=True) * CS
                p = jnp.exp2(s * CS - m)
                l = jnp.sum(p, axis=0, keepdims=True)
                o = dot(vt[hrows, :nk], p.astype(BF)) * (1.0 / l)
                ot[hrows, cols] = o.astype(BF)
                lse[h, 0:1, cols] = m + jnp.log(l) * LOG2E
            by_pair(hp, mg, [G_ATT[j][qb] for j in range(3)])
        return 0

    lax.fori_loop(0, 3, fwd_pair, 0)

    def ctx_body(i, _):
        rows = pl.ds(al(i * BQ, BQ), BQ)
        for hp in range(3):
            lanes = slice(hp * 128, hp * 128 + 128)
            ctx[rows, lanes] = ot[lanes, rows].T
        return 0

    lax.fori_loop(0, NB, ctx_body, 0)
    mg(G_CTX)

    ps[...] = dot(ctx[pair_rows, :], watt[3]).astype(BF)
    send(ps, pr, S_PO, R_PO, dev_pair, lambda: ps)
    mid[...] = hid[...].astype(F32) + vecs[2:3, :] + dot(ctx[mine_rows, :], watt[3])
    w_og()
    when(swap, lambda: wrecv(og, R_OG))
    wrecv(pr, R_PO)

    sb[...] = jnp.zeros_like(sb)

    def ln2_body(i, _):
        rows = pl.ds(al(i * LB, LB), LB)
        x = mid[rows, :] + pr[rows, :].astype(F32)
        mid[rows, :] = x
        n, _r = stats(x)
        n2[rows, :] = (n * vecs[3:4, :] + vecs[4:5, :]).astype(BF)
        p0 = lax.broadcasted_iota(jnp.int32, (LB, 1), 0).astype(F32) + (row0 + i * LB).astype(F32)
        g = og[rows, :].astype(F32) * jnp.where(p0 < length, 1.0, 0.0)
        og[rows, :] = g.astype(BF)
        sb[5:6, :] += jnp.sum(g, axis=0, keepdims=True)
        oacc[rows, :] = jnp.zeros((LB, D), F32)
        dn2[rows, :] = jnp.zeros((LB, D), F32)
        return 0

    lax.fori_loop(0, R // LB, ln2_body, 0)
    for w in w_mlp0:
        w()

    def zdst(i):
        return (z - i - (i // 2) * (1 - 2 * (i % 2)) + 4) % 4

    def blk(m, i):
        return wmlp.at[m, zdst(i)]

    def add_into(dst, *others):
        t = dst[...].astype(F32)
        for o in others:
            t = t + o[...].astype(F32)
        dst[...] = t.astype(BF)

    def g_s0(m, i):
        u = m * 4 + i
        send(blk(m, i).at[:, oc], prb.at[u], S_GP + u, R_GP + u, dev_pair, lambda: blk(m, i).at[:, oc])

    def g_s1(m, i):
        u = m * 4 + i
        g = blk(m, i)
        wrecv(prb.at[u], R_GP + u)
        add_into(g.at[:, c], prb.at[u])
        send(g.at[r_op, c, pl.ds(0, 48)], r1b.at[u, 0], S_G1 + 2 * u, R_G1 + 2 * u, dev_up,
             lambda: r1b.at[u, 0])
        send(g.at[r_op, c, pl.ds(48, 48)], r1b.at[u, 1], S_G1 + 2 * u + 1, R_G1 + 2 * u + 1, dev_dn,
             lambda: r1b.at[u, 1])

    def g_s2(m, i):
        u = m * 4 + i
        g = blk(m, i)
        wrecv(r1b.at[u, 0], R_G1 + 2 * u)
        add_into(g.at[r_up, c, pl.ds(0, 48)], r1b.at[u, 0])
        send(g.at[r_up, c], r2b.at[u, 0], S_G2 + 2 * u, R_G2 + 2 * u, dev_up, lambda: r2b.at[u, 0])
        wrecv(r1b.at[u, 1], R_G1 + 2 * u + 1)
        add_into(g.at[r_dn, c, pl.ds(48, 48)], r1b.at[u, 1])
        send(g.at[r_dn, c], r2b.at[u, 1], S_G2 + 2 * u + 1, R_G2 + 2 * u + 1, dev_dn, lambda: r2b.at[u, 1])

    def g_s3(m, i):
        u = m * 4 + i
        g = blk(m, i)
        wrecv(r2b.at[u, 0], R_G2 + 2 * u)
        wrecv(r2b.at[u, 1], R_G2 + 2 * u + 1)
        add_into(g.at[r, c], r2b.at[u, 0], r2b.at[u, 1])
        if i > 0:
            send(g.at[r, c], zb.at[m, i - 1], S_GZ + u, R_GZ + m * 3 + i - 1, (dp, zdst(i)),
                 lambda: zb.at[m, i - 1])

    def g_fin(m):
        for i in (1, 2, 3):
            wrecv(zb.at[m, i - 1], R_GZ + m * 3 + i - 1)
        t = wmlp[m, z, r, c].astype(F32)
        for i in range(3):
            t = t + zb[m, i].astype(F32)
        fs[m] = t.astype(BF)
        dst = gm_out.at[m, r, c]
        send(fs.at[m], dst, S_FA + 3 * m, R_FA + 3 * m, dev_up, lambda: fs.at[m])
        send(fs.at[m], dst, S_FA + 3 * m + 1, R_FA + 3 * m + 1, dev_dn, lambda: fs.at[m])
        send(fs.at[m], dst, S_FA + 3 * m + 2, R_FA + 3 * m + 2, dev_pair, lambda: fs.at[m])

    def g_ag(m):
        lo = gm_out.at[m, r_dn, c, pl.ds(0, 48)]
        hi = gm_out.at[m, r_up, c, pl.ds(48, 48)]
        wrecv(gm_out.at[m, r_dn, c], R_FA + 3 * m)
        send(lo, lo, S_FB + 2 * m, R_FB + 2 * m, dev_up, lambda: r1b.at[0, 0])
        full = gm_out.at[m, r_dn, c]
        send(full, full, S_FC + 3 * m, R_FC + 3 * m, dev_pair, lambda: fs.at[m])
        wrecv(gm_out.at[m, r_up, c], R_FA + 3 * m + 1)
        send(hi, hi, S_FB + 2 * m + 1, R_FB + 2 * m + 1, dev_dn, lambda: r1b.at[0, 0])
        full2 = gm_out.at[m, r_up, c]
        send(full2, full2, S_FC + 3 * m + 1, R_FC + 3 * m + 1, dev_pair, lambda: fs.at[m])

    def g_ag2(m):
        wrecv(gm_out.at[m, r_op, c, pl.ds(0, 48)], R_FB + 2 * m)
        wrecv(gm_out.at[m, r_op, c, pl.ds(48, 48)], R_FB + 2 * m + 1)
        full = gm_out.at[m, r_op, c]
        send(full, full, S_FC + 3 * m + 2, R_FC + 3 * m + 2, dev_pair, lambda: fs.at[m])

    def g_end(m):
        wrecv(gm_out.at[m, r, oc], R_FA + 3 * m + 2)
        wrecv(gm_out.at[m, r_dn, oc], R_FC + 3 * m)
        wrecv(gm_out.at[m, r_up, oc], R_FC + 3 * m + 1)
        wrecv(gm_out.at[m, r_op, oc], R_FC + 3 * m + 2)

    def a_s1(hp):
        g = gatt.at[hp]
        send(g.at[r_op, pl.ds(0, 64)], a1b.at[hp, 0], S_A1 + 2 * hp, R_A1 + 2 * hp, dev_up, lambda: a1b.at[hp, 0])
        send(g.at[r_op, pl.ds(64, 64)], a1b.at[hp, 1], S_A1 + 2 * hp + 1, R_A1 + 2 * hp + 1, dev_dn,
             lambda: a1b.at[hp, 1])

    def a_s2(hp):
        g = gatt.at[hp]
        wrecv(a1b.at[hp, 0], R_A1 + 2 * hp)
        add_into(g.at[r_up, pl.ds(0, 64)], a1b.at[hp, 0])
        send(g.at[r_up], a2b.at[hp, 0], S_A2 + 2 * hp, R_A2 + 2 * hp, dev_up, lambda: a2b.at[hp, 0])
        wrecv(a1b.at[hp, 1], R_A1 + 2 * hp + 1)
        add_into(g.at[r_dn, pl.ds(64, 64)], a1b.at[hp, 1])
        send(g.at[r_dn], a2b.at[hp, 1], S_A2 + 2 * hp + 1, R_A2 + 2 * hp + 1, dev_dn, lambda: a2b.at[hp, 1])

    parts = [(0, 0, 128, 0, 0), (1, 0, 64, 0, 128), (1, 64, 64, 1, 0), (2, 0, 128, 1, 64)]

    def a_s3(hp):
        g = gatt.at[hp]
        wrecv(a2b.at[hp, 0], R_A2 + 2 * hp)
        wrecv(a2b.at[hp, 1], R_A2 + 2 * hp + 1)
        add_into(g.at[r], a2b.at[hp, 0], a2b.at[hp, 1])
        for pi, (ph, lo, n, zz, to) in enumerate(parts):
            if ph != hp:
                continue

            def go(pi=pi, lo=lo, n=n, zz=zz, to=to):
                zd = 2 * c + zz
                slot = (zd - z + 3) % 4
                send(g.at[r, pl.ds(lo, n)], azb.at[slot, pl.ds(to, n)], S_AZ + pi,
                     R_AZ + 3 * pi + slot, (dp, zd), lambda: gatt.at[hp, 0, pl.ds(lo, n)], need(zz))

            pl.when(need(zz))(go)

    def a_fin(zz):
        for pi, (ph, lo, n, zo, to) in enumerate(parts):
            if zo != zz:
                continue
            for slot in range(3):
                wrecv(azb.at[slot, pl.ds(to, n)], R_AZ + 3 * pi + slot)
            t = gatt[ph, r, lo : lo + n].astype(F32)
            for slot in range(3):
                t = t + azb[slot, to : to + n].astype(F32)
            fa[to : to + n] = t.astype(BF)

    def a_ag():
        for i, dev in enumerate((dev_up, dev_dn, dev_pair)):
            send(fa, ga_out.at[r], S_HA + i, R_HA + i, dev, lambda: fa, own_c)

    def a_ag2():
        lo = ga_out.at[r_dn, pl.ds(0, half)]
        hi = ga_out.at[r_up, pl.ds(half, half)]
        wrecv(ga_out.at[r_dn], R_HA)
        send(lo, lo, S_HB, R_HB, dev_up, lambda: fa.at[pl.ds(0, half)], own_c)
        send(ga_out.at[r_dn], ga_out.at[r_dn], S_HC, R_HC, dev_pair, lambda: fa, own_c)
        wrecv(ga_out.at[r_up], R_HA + 1)
        send(hi, hi, S_HB + 1, R_HB + 1, dev_dn, lambda: fa.at[pl.ds(0, half)], own_c)
        send(ga_out.at[r_up], ga_out.at[r_up], S_HC + 1, R_HC + 1, dev_pair, lambda: fa, own_c)

    def a_ag3():
        wrecv(ga_out.at[r_op, pl.ds(0, half)], R_HB)
        wrecv(ga_out.at[r_op, pl.ds(half, half)], R_HB + 1)
        send(ga_out.at[r_op], ga_out.at[r_op], S_HC + 2, R_HC + 2, dev_pair, lambda: fa, own_c)

    def a_end():
        wrecv(ga_out.at[r], R_HA + 2)
        wrecv(ga_out.at[r_dn], R_HC)
        wrecv(ga_out.at[r_up], R_HC + 1)
        wrecv(ga_out.at[r_op], R_HC + 2)

    GA_ = 0.7978845608028654

    def gr(steps):
        for st in steps.split():
            kind, u = int(st[0]), int(st[1:])
            if u < 8:
                (g_s1, g_s2, g_s3)[kind - 1](1 - u % 2, u // 2)
            else:
                (a_s1, a_s2, a_s3)[kind - 1](u - 8)

    def mlp_body(i, _):
        zp = zdst(i)

        def got(dz):
            mg_done(0, dz)
            mg_done(1, dz)

        for it, dz in ((1, 1), (2, 3), (3, 2)):
            pl.when(i == it)(functools.partial(got, dz))
        for fb in range(D // 256):
            cols = slice(fb * 256, fb * 256 + 256)
            fcb = wmlp[0, zp, :, :, :, cols].reshape(D, 256)
            pre = dot(n2[...], fcb) + bfa[zp, 0:1, cols]
            sq = pre * pre
            t = jnp.tanh(GA_ * (pre + 0.044715 * (pre * sq)))
            hf = 0.5 * (1.0 + t)
            act[:, cols] = (pre * hf).astype(BF)
            gp = hf + (0.5 * GA_) * pre * (1.0 - t * t) * (1.0 + 0.134145 * sq)
            prj = wmlp[1, zp].reshape(D, D)[cols, :]
            dp_ = (nt(og[...], prj) * gp).astype(BF)
            dpre[:, cols] = dp_
            sb[pl.ds(6 + zp, 1), cols] = jnp.sum(dp_.astype(F32), axis=0, keepdims=True)
        prj = wmlp[1, zp].reshape(D, D)
        for rb in range(R // 256):
            rows = slice(rb * 256, rb * 256 + 256)
            oacc[rows, :] += dot(act[rows, :], prj)
        for j in range(2):
            cols = slice(j * HC, j * HC + HC)
            wmlp[1, zp, 2 * j : 2 * j + 2] = tn(act[:, cols], og[...]).astype(BF).reshape(2, 2, D // 8, D)
        at(i, 0)
        fc = wmlp[0, zp].reshape(D, D)
        for rb in range(R // 256):
            rows = slice(rb * 256, rb * 256 + 256)
            dn2[rows, :] += nt(dpre[rows, :], fc)
        for j in range(2):
            cols = slice(j * HC, j * HC + HC)
            wmlp[0, zp, 2 * j : 2 * j + 2] = tn(n2[:, cols], dpre[...]).astype(BF).reshape(2, 2, D // 8, D)
        at(i, 1)
        return 0

    def at(i, where):
        for kk_ in range(4):
            def here(kk_=kk_):
                g_s0(1 - where, kk_)
                mg(G_LOOP[kk_][where])
                gr(T_LOOP[kk_][where])

            pl.when(i == kk_)(here)

    mg(G_MLP)
    lax.fori_loop(0, 4, mlp_body, 0)

    def bwd2_body(i, _):
        rows = pl.ds(al(i * LB, LB), LB)
        x = mid[rows, :]
        p0 = lax.broadcasted_iota(jnp.int32, (LB, 1), 0).astype(F32) + (row0 + i * LB).astype(F32)
        ok = jnp.where(p0 < length, 1.0, 0.0)
        bo[rows, :] = ((x + oacc[rows, :] + vecs[5:6, :]) * ok).astype(BF)
        n, rstd = stats(x)
        dn = dn2[rows, :]
        e = dn * vecs[3:4, :]
        em = jnp.mean(e, axis=1, keepdims=True)
        en = jnp.mean(e * n, axis=1, keepdims=True)
        gm = og[rows, :].astype(F32) + (e - em - n * en) * rstd
        mid[rows, :] = gm
        ga[pl.ds(al(row0 + i * LB, LB), LB), :] = gm.astype(BF)
        sb[2:3, :] += jnp.sum(dn * n, axis=0, keepdims=True)
        sb[3:4, :] += jnp.sum(dn, axis=0, keepdims=True)
        sb[4:5, :] += jnp.sum(gm, axis=0, keepdims=True)
        return 0

    lax.fori_loop(0, R // LB, bwd2_body, 0)
    send(ga.at[mine_rows], ga.at[mine_rows], S_GA, R_GA, dev_pair, lambda: ga.at[mine_rows])
    when(swap, lambda: send(bo, bo_out, S_BO, R_BO, dev_swap, lambda: bo, swap))
    w_bo = local(lambda: bo, lambda: bo_out, keep)
    gr(T_BWD2)
    wrecv(ga.at[pair_rows], R_GA)

    def dctx_body(i, _):
        rows = pl.ds(al(i * BQ, BQ), BQ)
        d = nt(ga[rows, :], watt[3])
        do[rows, :] = d.astype(BF)
        for hp in range(3):
            lanes = slice(hp * 128, hp * 128 + 128)
            dot_[lanes, rows] = do[rows, lanes].T
        return 0

    lax.fori_loop(0, NB, dctx_body, 0)
    gr(T_DCTX)

    def bwd_pair(hp, _):
        prep = []
        for hh in (0, 1):
            h = hp * 2 + hh
            lanes, inhead = head_prep(hp, hh)
            hrows = pl.ds(al(h * 64, 64), 64)
            vh[hh] = jnp.where(inhead, v[:, lanes].astype(F32), 0.0).astype(BF)
            dl = jnp.sum(dot_[hrows, :].astype(F32) * ot[hrows, :].astype(F32), axis=0, keepdims=True)
            prep.append((h, hrows, dl, lse[h]))
        for kb in range(NB):
            krows = slice(kb * BQ, kb * BQ + BQ)
            qs = slice(kb * BQ, T)
            dks, dvs = [], []
            for hh in (0, 1):
                h, hrows, dl, ls_h = prep[hh]
                s = dot(kh[hh, krows, :], qh[hh, :, qs])
                diag = s[:, :BQ] + cmask[...]
                s = diag if kb == NB - 1 else jnp.concatenate([diag, s[:, BQ:]], axis=1)
                p = jnp.exp2(s * CS - ls_h[0:1, qs])
                dpr = dot(vh[hh, krows, :], dot_[lanes, qs])
                ds = (p * (dpr - dl[:, qs])).astype(BF)
                dvs.append(dot(p.astype(BF), do[qs, lanes]))
                dks.append(dot(ds, q[qs, lanes]) * 0.125)
                piece = dot(kt[hrows, krows], ds)
                if kb == 0:
                    dqa[hh] = piece
                else:
                    dqa[hh, :, qs] += piece
            first = lane < 64
            v[krows, lanes] = jnp.where(first, dvs[0], dvs[1]).astype(BF)
            k[krows, lanes] = jnp.where(first, dks[0], dks[1]).astype(BF)
            by_pair(hp, gr, [T_ATT[j][kb] for j in range(3)])
        for hh in (0, 1):
            qt[prep[hh][1], :] = (dqa[hh] * 0.125).astype(BF)
        lanes = pl.ds(al(hp * 128, 128), 128)

        def tr2(i, _):
            rows = pl.ds(al(i * BQ, BQ), BQ)
            q[rows, lanes] = qt[lanes, rows].T
            kt[lanes, rows] = k[rows, lanes].T
            vt[lanes, rows] = v[rows, lanes].T
            return 0

        lax.fori_loop(0, NB, tr2, 0)
        for t, ref in enumerate((qt, kt, vt)):
            gatt[hp, t] = dot(ref[lanes, :], n1[...]).astype(BF)
        gatt[hp, 3] = dot(ot[lanes, :], ga[...]).astype(BF)
        for j in range(3):
            pl.when(hp == j)(functools.partial(gr, T_PAIR[j]))
        return 0

    lax.fori_loop(0, 3, bwd_pair, 0)

    def dx(rows):
        return dot(q[rows, :], watt[0]) + dot(k[rows, :], watt[1]) + dot(v[rows, :], watt[2])

    ps2[...] = dx(pair_rows).astype(BF)
    send(ps2, pr2, S_DX, R_DX, dev_pair, lambda: ps2)
    gr(T_DX)
    g_fin(1)
    g_fin(0)
    dn2[...] = dx(mine_rows)
    gr(T_DX2)
    sb[pl.ds(10 + c, 1), :] = jnp.concatenate(
        [jnp.sum(q[...].astype(F32), axis=0, keepdims=True), jnp.sum(v[...].astype(F32), axis=0, keepdims=True)],
        axis=1,
    )
    wrecv(pr2, R_DX)

    def bwd1_body(i, _):
        rows = pl.ds(al(i * LB, LB), LB)
        n, rstd = stats(hid[rows, :].astype(F32))
        dn = dn2[rows, :] + pr2[rows, :].astype(F32)
        e = dn * vecs[0:1, :]
        em = jnp.mean(e, axis=1, keepdims=True)
        en = jnp.mean(e * n, axis=1, keepdims=True)
        gi[rows, :] = (mid[rows, :] + (e - em - n * en) * rstd).astype(BF)
        sb[0:1, :] += jnp.sum(dn * n, axis=0, keepdims=True)
        sb[1:2, :] += jnp.sum(dn, axis=0, keepdims=True)
        for j in range(R // LB):
            def out(j=j):
                part = pl.ds(j * LB, LB)
                send(gi.at[part], gi_out.at[part], S_GI + j, R_GI + j, dev_swap, lambda: gi.at[part], swap)

            pl.when((i == j) & swap)(out)
        return 0

    g_ag(1)
    g_ag(0)
    lax.fori_loop(0, R // LB, bwd1_body, 0)
    gr(T_LAST)
    w_gi = local(lambda: gi, lambda: gi_out, keep)

    def small_pair():
        send(sb.at[pl.ds(0, 16)], srb.at[8], S_SM, R_SM + 8, dev_pair, lambda: srb.at[0])

    def small_ring():
        wrecv(srb.at[8], R_SM + 8)
        t = sb[0:16] + srb[8]
        sb[16:32] = t
        srb[r] = t
        for j, dev in enumerate((dev_up, dev_dn, dev_op)):
            send(sb.at[pl.ds(16, 16)], srb.at[r], S_SM + 1 + j, R_SM + r, dev, lambda: srb.at[0])

    def small_z():
        for o in (r_up, r_dn, r_op):
            wrecv(srb.at[o], R_SM + o)
        t = (srb[0] + srb[1]) + (srb[2] + srb[3])
        sb[32:48] = t
        srb[4 + z] = t
        for dz in (1, 2, 3):
            send(sb.at[pl.ds(32, 16)], srb.at[4 + z], S_SM + 3 + dz, R_SM + 4 + z, dev_z[dz], lambda: srb.at[0])

    def small_end():
        for dz in (1, 2, 3):
            wrecv(srb.at[4 + zsh(dz)], R_SM + 4 + zsh(dz))
        t = (srb[4] + srb[5]) + (srb[6] + srb[7])
        sb[48:64] = t
        small_out[0:6, :] = t[0:6]
        small_out[6:7, :] = sb[pl.ds(54 + z, 1), :]
        row = sb[pl.ds(58 + z // 2, 1), :]
        odd = (z % 2).astype(F32)
        even = 1.0 - odd
        bq = even * row[:, :ZS] + odd * row[:, ZS : 2 * ZS]
        bv = even * row[:, 2 * ZS : 3 * ZS] + odd * row[:, 3 * ZS :]
        gap = jnp.zeros((1, HC - ZS), F32)
        small_out[7:8, :] = jnp.concatenate([bq, gap, bv, gap], axis=1)

    small_pair()
    for m in (1, 0):
        g_ag2(m)
    small_ring()
    for zz in (0, 1):
        when(z == 2 * c + zz, functools.partial(a_fin, zz))
    when(own_c, a_ag)
    small_z()
    when(own_c, a_ag2)
    when(own_c, a_ag3)
    small_end()

    w_fs = [local(lambda: fs.at[0], lambda: gm_out.at[0, r, c]), local(lambda: fs.at[1], lambda: gm_out.at[1, r, c])]
    w_fa = local(lambda: fa, lambda: ga_out.at[r], own_c)
    w_bo()
    w_gi()
    for w in w_fs:
        w()
    w_fa()
    for m in (0, 1):
        g_end(m)
    when(not_own, a_end)
    when(swap, lambda: wrecv(bo_out, R_BO))
    for j in range(R // LB):
        when(swap, lambda: wrecv(gi_out.at[pl.ds(j * LB, LB)], R_GI + j))
    for sid, (ref, cond) in pending.items():
        when(cond, lambda sid=sid, ref=ref: wsend(ref(), sid))


def widen_kernel(bo, gi, gm, ga, bo_o, gi_o, fc_o, proj_o, qkv_o, out_o):
    bo_o[...] = bo[...]
    gi_o[...] = gi[...]
    fc_o[...] = gm[0].astype(F32)
    proj_o[...] = gm[1].astype(F32)
    qkv_o[...] = ga[:3].astype(F32)
    out_o[...] = ga[3].astype(F32)


def widen(bo, gi, gm, ga):
    n = 4
    (R, D), ZS = bo.shape, ga.shape[1]
    rows = lambda m: pl.BlockSpec((m // n, D), lambda i: (i, 0))
    stack = lambda k, m: pl.BlockSpec((k, m // n, D), lambda i: (0, i, 0))
    return pl.pallas_call(
        widen_kernel,
        grid=(n,),
        out_shape=(
            jax.ShapeDtypeStruct((R, D), BF), jax.ShapeDtypeStruct((R, D), BF),
            jax.ShapeDtypeStruct((D, D), F32), jax.ShapeDtypeStruct((D, D), F32),
            jax.ShapeDtypeStruct((3, ZS, D), F32), jax.ShapeDtypeStruct((ZS, D), F32),
        ),
        in_specs=[rows(R), rows(R), stack(2, D), stack(4, ZS)],
        out_specs=(rows(R), rows(R), rows(D), rows(D), stack(3, ZS), rows(ZS)),
        compiler_params=pltpu.CompilerParams(vmem_limit_bytes=64 * 1024 * 1024 - 65536),
        name="widen",
    )(bo, gi, gm, ga)


def body(
    hidden_in, lengths, ln1_gain, ln1_bias, w_qkv, b_query, b_value, w_out, b_out,
    ln2_gain, ln2_bias, w_fc, b_fc, w_proj, b_proj, out_grad,
):
    R, D = hidden_in.shape
    T, HC, ZS, EB = 2 * R, D // 2, D // 4, D // 8
    z = lax.axis_index("tensor")
    odd = z % 2 == 1
    lo, hi = (lambda t: jnp.pad(t, (0, HC - ZS))), (lambda t: jnp.pad(t, (HC - ZS, 0)))
    place = lambda t: jnp.where(odd, hi(t), lo(t))
    qv_row = jnp.pad(place(b_query), (0, HC)) + jnp.pad(place(b_value), (HC, 0))
    row = lax.broadcasted_iota(jnp.int32, (16, D), 0)
    vecs = jnp.zeros((16, D), BF)
    for at_row, vec in (
        (0, ln1_gain), (1, ln1_bias), (2, b_out), (3, ln2_gain), (4, ln2_bias), (5, b_proj), (8, b_fc), (9, qv_row),
    ):
        vecs = jnp.where(row == at_row, vec[None, :], vecs)
    vecs = vecs.astype(F32)
    wq = jnp.transpose(w_qkv, (1, 2, 0))
    wf = w_fc.reshape(4, 2, EB, D)
    wp = w_proj.reshape(4, 2, EB, D)
    vm = lambda *s: pltpu.VMEM(s, BF)
    vf = lambda *s: pltpu.VMEM(s, F32)
    scratch = [
        vf(8, 128), vf(8, 128), vf(4, 8, D), vm(R, D), vm(R, D), vm(T, D), vm(4, HC, D), vm(2, 4, 4, 2, EB, D),
        vm(T, HC), vm(T, HC), vm(T, HC), vm(HC, T), vm(HC, T), vm(HC, T),
        vm(T, HC), vm(HC, T), vm(HC, T), vm(T, HC),
        vf(R, D), vm(R, D), vf(R, D), vf(R, D), vm(R, D), vm(R, D), vm(T, D),
        vm(R, D), vm(R, D), vm(R, D), vm(R, D), vm(R, D), vm(R, D),
        vf(6, 1, T), vf(2, 64, T), vf(256, 256), vm(2, T, 128), vm(2, T, 128), vm(2, 128, T),
        vm(8, 4, EB, D), vm(8, 2, EB // 2, D), vm(8, 2, EB, D), vm(2, 3, EB, D), vm(2, EB, D),
        vm(3, 4, 128, D), vm(3, 2, 64, D), vm(3, 2, 128, D), vm(3, ZS, D), vm(ZS, D),
        vf(64, D), vf(9, 16, D),
        pltpu.SemaphoreType.DMA((SID.n,)), pltpu.SemaphoreType.DMA((RID.n,)), pltpu.SemaphoreType.DMA((12,)),
    ]
    anyspec = pl.BlockSpec(memory_space=pl.ANY)
    vspec = pl.BlockSpec(memory_space=pltpu.VMEM)
    block_out, grad_input, gm, gatt, small = pl.pallas_call(
        kernel,
        out_shape=(
            jax.ShapeDtypeStruct((R, D), BF),
            jax.ShapeDtypeStruct((R, D), BF),
            jax.ShapeDtypeStruct((2, 4, 2, EB, D), BF),
            jax.ShapeDtypeStruct((4, ZS, D), BF),
            jax.ShapeDtypeStruct((8, D), F32),
        ),
        in_specs=[pl.BlockSpec(memory_space=pltpu.SMEM), vspec] + [anyspec] * 6,
        out_specs=(anyspec, anyspec, anyspec, anyspec, vspec),
        scratch_shapes=scratch,
        compiler_params=pltpu.CompilerParams(
            collective_id=0, has_side_effects=True, vmem_limit_bytes=64 * 1024 * 1024 - 65536
        ),
        name="layer",
    )(lengths, vecs, hidden_in, out_grad, wq, w_out, wf, wp)
    data_count = lax.axis_size("dp")
    gm = gm.reshape(2, D, D)
    if data_count > GROUP:
        groups = [list(range(s, data_count, GROUP)) for s in range(GROUP)]
        gm, gatt, small = (
            lax.psum(t.astype(F32), "dp", axis_index_groups=groups) for t in (gm, gatt, small)
        )
    block_out, grad_input, g_fc, g_proj, g_qkv, g_out = widen(block_out, grad_input, gm, gatt)
    g_qkv = jnp.transpose(g_qkv, (2, 0, 1))
    gbq = small[7, :ZS]
    gbv = small[7, HC : HC + ZS]
    return (
        block_out, grad_input, small[0], small[1], g_qkv, gbq, gbv, g_out, small[4],
        small[2], small[3], g_fc, small[6], g_proj, small[5],
    )


def solution(mesh):
    rows = P(("dp", "tensor"), None)
    in_specs = (
        rows, P("dp"), P(), P(), P(None, None, "tensor"), P("tensor"), P("tensor"), P("tensor", None),
        P(), P(), P(), P(None, "tensor"), P("tensor"), P("tensor", None), P(), rows,
    )
    out_specs = (
        rows, rows, P(), P(), P(None, None, "tensor"), P("tensor"), P("tensor"), P("tensor", None),
        P(), P(), P(), P(None, "tensor"), P("tensor"), P("tensor", None), P(),
    )
    return jax.shard_map(body, mesh=mesh, in_specs=in_specs, out_specs=out_specs, check_vma=False)
```

```python
import functools

import jax
import jax.numpy as jnp
from jax import lax
from jax.experimental import pallas as pl
from jax.experimental.pallas import tpu as pltpu
from jax.sharding import PartitionSpec as P

BF = jnp.bfloat16
F32 = jnp.float32
EPS = 1e-5
NEG = -1e30
LOG2E = 1.4426950408889634
MESH = pl.DeviceIdType.MESH
RING = 4
GROUP = 2 * RING


T_LOOP = (("", "10"), ("11 20", "12"), ("13 21", "14"), ("15 22", "16"))
T_BWD2 = "17 23 30"
T_DCTX = "31"
T_ATT = (("24", "32", "25", "33"), ("26", "34", "27", "35"), ("28 36", "29", "37 210", "211"))
T_PAIR = ("18 19", "110 111", "112 113 41 40")
T_DX = "38 39"
T_DX2 = "212 213 310 311"
T_AG = "51 50"
T_LAST = "312 313"
T_AG2 = "61 60"
G_EARLY = ""
G_QKV = "a0"
G_TR = ""
G_ATT = (("a1", "", "b0", ""), ("b1 a2", "", "p0 a3", "p1"), ("b2", "", "b3 p2", "a4"))
G_CTX = ""
G_MLP = "p3 a5"
G_LOOP = (("b4", "b5"), ("p4", "p5"), ("", ""), ("", ""))


def dot(a, b, ca=1, cb=0):
    return lax.dot_general(a, b, (((ca,), (cb,)), ((), ())), preferred_element_type=F32)


def nt(a, b):
    return dot(a, b, 1, 1)


def tn(a, b):
    return dot(a, b, 0, 0)


def al(v, m):
    return pl.multiple_of(v, m)


class Ids:
    def __init__(self):
        self.n = 0

    def __call__(self, k):
        base = self.n
        self.n += k
        return base


SID = Ids()
S_LEN, S_BIAS, S_HID, S_OG, S_AS1 = SID(1), SID(3), SID(1), SID(1), SID(6)
S_ARA, S_ARB = SID(8), SID(8)
S_MS1, S_MRA, S_MRB, S_MP = SID(6), SID(12), SID(12), SID(6)
S_N1, S_PO, S_GA, S_DX, S_BO, S_GI = SID(1), SID(1), SID(1), SID(1), SID(1), SID(8)
S_GP, S_G1, S_G2, S_GZ = SID(8), SID(16), SID(16), SID(8)
S_FA, S_FB, S_FC = SID(6), SID(4), SID(6)
S_A1, S_A2, S_AZ = SID(12), SID(12), SID(6)
S_HA, S_HB, S_HC = SID(9), SID(6), SID(9)
S_SM = SID(7)
RID = Ids()
R_LEN, R_BIAS, R_HID, R_OG, R_AS1 = RID(1), RID(3), RID(1), RID(1), RID(4)
R_ARA, R_ARB = RID(8), RID(8)
R_MS1, R_MRA, R_MRB, R_MP = RID(6), RID(12), RID(12), RID(6)
R_N1, R_PO, R_GA, R_DX, R_BO, R_GI = RID(1), RID(1), RID(1), RID(1), RID(1), RID(8)
R_GP, R_G1, R_G2, R_GZ = RID(8), RID(16), RID(16), RID(6)
R_FA, R_FB, R_FC = RID(6), RID(4), RID(6)
R_A1, R_A2, R_AZ = RID(12), RID(12), RID(18)
R_HA, R_HB, R_HC = RID(9), RID(6), RID(9)
R_SM = RID(9)


def kernel(
    lengths, vecs, hid_in, og_in, wq, wo, wf, wp,
    bo_out, gi_out, gm_out, ga_out, small_out,
    lens, lrecv, bfa, hid, og, n1, watt, wmlp, q, k, v, qt, kt, vt, do, dot_, ot,
    mid, n2, oacc, dn2, act, dpre, ga, ps, pr, ps2, pr2, bo, gi,
    lse, dqa, cmask, kh, vh, qh,
    prb, r1b, r2b, zb, fs, gatt, a1b, a2b, azb, fa, sb, srb,
    ss, rs, ls,
):
    D = hid_in.shape[1]
    R = hid_in.shape[0]
    T = 2 * R
    HC = D // 2
    BQ = 256
    NB = T // BQ
    dp = lax.axis_index("dp")
    z = lax.axis_index("tensor")
    base = (dp // GROUP) * GROUP
    chip = (dp - base) // 2
    c = dp % 2
    oc = 1 - c
    cy = chip // 2
    cx = chip % 2
    r = 3 * cy + cx - 2 * cx * cy

    def ring_dp(rr, core):
        y = rr // 2
        x = rr % 2 + y - 2 * (rr % 2) * y
        return base + (2 * y + x) * 2 + core

    r_up = (r + 1) % RING
    r_dn = (r + 3) % RING
    r_op = (r + 2) % RING
    dev_up = (ring_dp(r_up, c), z)
    dev_dn = (ring_dp(r_dn, c), z)
    dev_op = (ring_dp(r_op, c), z)
    dev_pair = (dp + 1 - 2 * c, z)
    dev_z = [None] + [(dp, (z + dz) % 4) for dz in (1, 2, 3)]
    z_x = z + 1 - 2 * (z % 2)
    dev_swap = (dp + 1 - 2 * c, z_x)
    keep = c == z % 2
    swap = c != z % 2
    own_c = z // 2 == c
    mine = (z == 2 * c, z == 2 * c + 1)
    not_own = z // 2 != c
    zz_own = z % 2
    pending = {}

    def when(cond, fn):
        if cond is None:
            fn()
        else:
            pl.when(cond)(fn)

    def desc(src, dst, sid, rid, dev):
        return pltpu.make_async_remote_copy(
            src_ref=src, dst_ref=dst, send_sem=ss.at[sid], recv_sem=rs.at[rid],
            device_id=dev, device_id_type=MESH,
        )

    def send(src, dst, sid, rid, dev, late=None, cond=None):
        desc(src, dst, sid, rid, dev).start()
        if late is not None:
            pending[sid] = (late, cond)

    def wsend(ref, sid):
        desc(ref, ref, sid, 0, dev_pair).wait_send()

    def wrecv(ref, rid):
        desc(ref, ref, 0, rid, dev_pair).wait_recv()

    barrier = pltpu.get_barrier_semaphore()
    cross = [(dp + 1 - 2 * c, (z + dz) % 4) for dz in (1, 2, 3)]
    for dev in (dev_up, dev_dn, dev_op, dev_pair, dev_z[1], dev_z[2], dev_z[3], *cross):
        pl.semaphore_signal(barrier, inc=1, device_id=dev, device_id_type=MESH)

    loc_n = [0]

    def local(src, dst, cond=None):
        i = loc_n[0]
        loc_n[0] += 1
        cp = lambda: pltpu.make_async_copy(src(), dst(), ls.at[i])
        when(cond, lambda: cp().start())
        return lambda: when(cond, lambda: cp().wait())

    w_hid = local(lambda: hid_in, lambda: hid, keep)
    bias = vecs.at[pl.ds(8, 8)]
    ZS = D // 4

    def att_rows(zz):
        return pl.ds(al(zz * ZS, 16), ZS)

    ZQ = ZS // RING

    def att_piece(e, zz, rr):
        rows = pl.ds(al(zz * ZS + rr * ZQ, 16), ZQ)
        return watt.at[3, rows] if e else watt.at[pl.ds(0, 3), rows]

    def att_half(e, zz, rr, side):
        rows = pl.ds(al(zz * ZS + rr * ZQ, 16), ZQ)
        cols = pl.ds(side * HC, HC)
        return watt.at[3, rows, cols] if e else watt.at[pl.ds(0, 3), rows, cols]

    def att_s1(e):
        for dz in (1, 2, 3):
            rows = pl.ds(al(r * ZQ, 16), ZQ)
            src = wo.at[rows] if e else wq.at[:, rows]
            dev = (dp - c + z // 2, (z + dz) % 4)
            send(src, att_piece(e, zz_own, r), S_AS1 + 3 * e + dz - 1, R_AS1 + 2 * e + zz_own, dev,
                 lambda: att_piece(e, 0, 0), swap)

    w_wq = local(lambda: wq, lambda: watt.at[pl.ds(0, 3), att_rows(zz_own)], own_c)
    w_wo = local(lambda: wo, lambda: watt.at[3, att_rows(zz_own)], own_c)
    w_og = local(lambda: og_in, lambda: og, keep)
    w_mlp0 = [local(lambda: wf, lambda: wmlp.at[0, z]), local(lambda: wp, lambda: wmlp.at[1, z])]
    def zsh(dz):
        return (z - dz + 4) % 4

    def mg_s1(m, dz):
        w = (wf, wp)[m]
        u = m * 3 + dz - 1
        send(w.at[r, c], wmlp.at[m, z, r, c], S_MS1 + u, R_MS1 + u, dev_z[dz], lambda: w.at[r, c])

    def mg_a(m, dz):
        u = m * 3 + dz - 1
        piece = wmlp.at[m, zsh(dz), r, c]
        wrecv(piece, R_MS1 + u)
        send(piece, piece, S_MRA + 2 * u, R_MRA + 2 * u, dev_up)
        send(piece, piece, S_MRA + 2 * u + 1, R_MRA + 2 * u + 1, dev_dn)

    def mg_b(m, dz):
        u = m * 3 + dz - 1
        zp = zsh(dz)
        wrecv(wmlp.at[m, zp, r_dn, c], R_MRA + 2 * u)
        lo = wmlp.at[m, zp, r_dn, c, pl.ds(0, 48)]
        send(lo, lo, S_MRB + 2 * u, R_MRB + 2 * u, dev_up)
        wrecv(wmlp.at[m, zp, r_up, c], R_MRA + 2 * u + 1)
        hi = wmlp.at[m, zp, r_up, c, pl.ds(48, 48)]
        send(hi, hi, S_MRB + 2 * u + 1, R_MRB + 2 * u + 1, dev_dn)

    def mg_p(m, dz):
        u = m * 3 + dz - 1
        zp = zsh(dz)
        wrecv(wmlp.at[m, zp, r_op, c, pl.ds(0, 48)], R_MRB + 2 * u)
        wrecv(wmlp.at[m, zp, r_op, c, pl.ds(48, 48)], R_MRB + 2 * u + 1)
        mine = wmlp.at[m, zp, :, c]
        send(mine, mine, S_MP + u, R_MP + u, dev_pair)

    def mg_done(m, dz):
        u = m * 3 + dz - 1
        zp = zsh(dz)
        wrecv(wmlp.at[m, zp, :, oc], R_MP + u)
        for s in (0, 1):
            wsend(wmlp.at[m, zp, r, c], S_MRA + 2 * u + s)
            wsend(wmlp.at[m, zp, r, c, pl.ds(0, 48)], S_MRB + 2 * u + s)
        wsend(wmlp.at[m, zp, :, c], S_MP + u)

    munits = [(0, 1), (1, 1), (0, 3), (1, 3), (0, 2), (1, 2)]

    def mg(steps):
        for st in steps.split():
            {"a": mg_a, "b": mg_b, "p": mg_p}[st[0]](*munits[int(st[1])])

    row0 = c * R
    half = ZS // 2

    def stats(x):
        mu = jnp.mean(x, axis=1, keepdims=True)
        cen = x - mu
        var = jnp.mean(cen * cen, axis=1, keepdims=True)
        rstd = lax.rsqrt(var + EPS)
        return cen * rstd, rstd

    LB = 128

    def ln1_body(i, _):
        rows = pl.ds(al(i * LB, LB), LB)
        n, _r = stats(hid[rows, :].astype(F32))
        out = n * vecs[0:1, :] + vecs[1:2, :]
        n1[pl.ds(al(row0 + i * LB, LB), LB), :] = out.astype(BF)
        return 0

    mine_rows = pl.ds(al(row0, R), R)
    pair_rows = pl.ds(al(oc * R, R), R)

    def norm_one():
        lax.fori_loop(0, R // LB, ln1_body, 0)

    def norm_one_send():
        send(n1.at[mine_rows], n1.at[mine_rows], S_N1, R_N1, dev_pair, lambda: n1.at[mine_rows])

    def norm_one_far():
        wrecv(hid, R_HID)
        norm_one()
        norm_one_send()

    bfa[z] = bias[...]
    w_hid()
    pl.when(keep)(norm_one)

    kk = lax.broadcasted_iota(jnp.int32, (BQ, BQ), 0)
    qq = lax.broadcasted_iota(jnp.int32, (BQ, BQ), 1)
    cmask[...] = jnp.where(kk <= qq, 0.0, NEG)
    pl.semaphore_wait(barrier, 10)
    pl.when(swap)(lambda: att_s1(0))
    when(swap, lambda: send(hid_in, hid, S_HID, R_HID, dev_swap, lambda: hid_in, swap))
    pl.when(swap)(lambda: att_s1(1))
    for dz in (1, 2, 3):
        send(bias, bfa.at[z], S_BIAS + dz - 1, R_BIAS + dz - 1, dev_z[dz], lambda: bias)
    lens[...] = jnp.full((8, 128), lengths[z // 2].astype(F32))
    send(lens, lrecv, S_LEN, R_LEN, dev_pair, lambda: lens)
    pl.when(keep)(norm_one_send)

    needs = (z != 2 * c, z != 2 * c + 1)

    def need(zz):
        return needs[zz]

    def ar_a(e, zz):
        u = 2 * e + zz
        piece = att_piece(e, zz, r)
        wrecv(piece, R_AS1 + u)
        for j, dev in enumerate((dev_up, dev_dn)):
            send(piece, piece, S_ARA + 2 * u + j, R_ARA + 2 * u + j, dev, lambda: att_piece(e, 0, 0), need(zz))

    def ar_b(e, zz):
        u = 2 * e + zz
        for j, (dev, rr) in enumerate(((dev_up, r_dn), (dev_dn, r_up))):
            wrecv(att_piece(e, zz, rr), R_ARA + 2 * u + j)
            part = att_half(e, zz, rr, j)
            send(part, part, S_ARB + 2 * u + j, R_ARB + 2 * u + j, dev, lambda: att_half(e, 0, 0, 0), need(zz))

    def ar_c(e, zz):
        u = 2 * e + zz
        for j in (0, 1):
            wrecv(att_half(e, zz, r_op, j), R_ARB + 2 * u + j)

    def ar(step, e):
        for zz in (0, 1):
            when(need(zz), functools.partial(step, e, zz))

    ar(ar_a, 0)
    for dz in (1, 3):
        mg_s1(0, dz)
        mg_s1(1, dz)
    ar(ar_b, 0)
    pl.when(swap)(norm_one_far)
    ar(ar_a, 1)
    mg_s1(0, 2)
    mg_s1(1, 2)
    when(swap, lambda: send(og_in, og, S_OG, R_OG, dev_swap, lambda: og_in, swap))
    mg(G_EARLY)
    ar(ar_c, 0)
    w_wq()
    w_wo()
    for dz in (1, 2, 3):
        wrecv(bfa.at[zsh(dz)], R_BIAS + dz - 1)
    wrecv(lrecv, R_LEN)
    keepf = 1.0 - (c + z % 2 - 2 * c * (z % 2)).astype(F32)
    length = lens[0:1, 0:1] * keepf + lrecv[0:1, 0:1] * (1.0 - keepf)
    wrecv(n1.at[pair_rows], R_N1)

    bqv = bfa[2 * c, 1:2, :] + bfa[2 * c + 1, 1:2, :]

    def qkv_body(i, _):
        rows = pl.ds(al(i * BQ, BQ), BQ)
        x = n1[rows, :]
        q[rows, :] = (nt(x, watt[0]) + bqv[:, :HC]).astype(BF)
        k[rows, :] = nt(x, watt[1]).astype(BF)
        v[rows, :] = (nt(x, watt[2]) + bqv[:, HC:]).astype(BF)
        return 0

    lax.fori_loop(0, NB, qkv_body, 0)
    ar(ar_b, 1)
    mg(G_QKV)

    def tr_body(i, _):
        rows = pl.ds(al(i * BQ, BQ), BQ)
        for hp in range(3):
            lanes = slice(hp * 128, hp * 128 + 128)
            qt[lanes, rows] = q[rows, lanes].T
            kt[lanes, rows] = k[rows, lanes].T
            vt[lanes, rows] = v[rows, lanes].T
        return 0

    lax.fori_loop(0, NB, tr_body, 0)
    mg(G_TR)

    lane = lax.broadcasted_iota(jnp.int32, (1, 128), 1)
    sub = lax.broadcasted_iota(jnp.int32, (128, 1), 0)
    pos = lax.broadcasted_iota(jnp.int32, (T, 1), 0).astype(F32)
    keybias = jnp.where(pos < length, 0.0, NEG)
    CS = 0.125 * LOG2E

    def head_prep(hp, hh):
        lanes = pl.ds(al(hp * 128, 128), 128)
        inhead = (lane // 64) == hh
        aux = lane == (1 - hh) * 64
        kp = k[:, lanes].astype(F32)
        kh[hh] = jnp.where(inhead, kp, jnp.where(aux, keybias, 0.0)).astype(BF)
        qp = qt[lanes, :].astype(F32)
        qh[hh] = jnp.where(sub == (1 - hh) * 64, 1.0, qp).astype(BF)
        return lanes, inhead

    def by_pair(hp, run, steps):
        for j in range(3):
            if steps[j]:
                pl.when(hp == j)(functools.partial(run, steps[j]))

    def fwd_pair(hp, _):
        for hh in (0, 1):
            head_prep(hp, hh)
        for qb in range(NB):
            nk = (qb + 1) * BQ
            cols = slice(qb * BQ, nk)
            for hh in (0, 1):
                h = hp * 2 + hh
                hrows = pl.ds(al(h * 64, 64), 64)
                s = dot(kh[hh, :nk, :], qh[hh, :, cols])
                diag = s[nk - BQ :] + cmask[...]
                s = diag if qb == 0 else jnp.concatenate([s[: nk - BQ], diag], axis=0)
                m = jnp.max(s, axis=0, keepdims=True) * CS
                p = jnp.exp2(s * CS - m)
                l = jnp.sum(p, axis=0, keepdims=True)
                o = dot(vt[hrows, :nk], p.astype(BF)) * (1.0 / l)
                ot[hrows, cols] = o.astype(BF)
                lse[h, 0:1, cols] = m + jnp.log(l) * LOG2E
            by_pair(hp, mg, [G_ATT[j][qb] for j in range(3)])
        return 0

    lax.fori_loop(0, 3, fwd_pair, 0)

    ar(ar_c, 1)
    mg(G_CTX)

    ps[...] = tn(ot[:, pl.ds(al(oc * R, R), R)], watt[3]).astype(BF)
    send(ps, pr, S_PO, R_PO, dev_pair, lambda: ps)
    mid[...] = hid[...].astype(F32) + vecs[2:3, :] + tn(ot[:, pl.ds(al(row0, R), R)], watt[3])
    w_og()
    when(swap, lambda: wrecv(og, R_OG))
    wrecv(pr, R_PO)

    sb[...] = jnp.zeros_like(sb)

    def ln2_body(i, _):
        rows = pl.ds(al(i * LB, LB), LB)
        x = mid[rows, :] + pr[rows, :].astype(F32)
        mid[rows, :] = x
        n, _r = stats(x)
        n2[rows, :] = (n * vecs[3:4, :] + vecs[4:5, :]).astype(BF)
        p0 = lax.broadcasted_iota(jnp.int32, (LB, 1), 0).astype(F32) + (row0 + i * LB).astype(F32)
        g = og[rows, :].astype(F32) * jnp.where(p0 < length, 1.0, 0.0)
        og[rows, :] = g.astype(BF)
        sb[5:6, :] += jnp.sum(g, axis=0, keepdims=True)
        oacc[rows, :] = jnp.zeros((LB, D), F32)
        dn2[rows, :] = jnp.zeros((LB, D), F32)
        return 0

    lax.fori_loop(0, R // LB, ln2_body, 0)
    for w in w_mlp0:
        w()

    def zdst(i):
        return (z - i - (i // 2) * (1 - 2 * (i % 2)) + 4) % 4

    def blk(m, i):
        return wmlp.at[m, zdst(i)]

    def add_into(dst, *others):
        t = dst[...].astype(F32)
        for o in others:
            t = t + o[...].astype(F32)
        dst[...] = t.astype(BF)

    def g_s0(m, i):
        u = m * 4 + i
        send(blk(m, i).at[:, oc], prb.at[u], S_GP + u, R_GP + u, dev_pair, lambda: blk(m, i).at[:, oc])

    def g_s1(m, i):
        u = m * 4 + i
        g = blk(m, i)
        wrecv(prb.at[u], R_GP + u)
        add_into(g.at[:, c], prb.at[u])
        send(g.at[r_op, c, pl.ds(0, 48)], r1b.at[u, 0], S_G1 + 2 * u, R_G1 + 2 * u, dev_up,
             lambda: r1b.at[u, 0])
        send(g.at[r_op, c, pl.ds(48, 48)], r1b.at[u, 1], S_G1 + 2 * u + 1, R_G1 + 2 * u + 1, dev_dn,
             lambda: r1b.at[u, 1])

    def g_s2(m, i):
        u = m * 4 + i
        g = blk(m, i)
        wrecv(r1b.at[u, 0], R_G1 + 2 * u)
        add_into(g.at[r_up, c, pl.ds(0, 48)], r1b.at[u, 0])
        send(g.at[r_up, c], r2b.at[u, 0], S_G2 + 2 * u, R_G2 + 2 * u, dev_up, lambda: r2b.at[u, 0])
        wrecv(r1b.at[u, 1], R_G1 + 2 * u + 1)
        add_into(g.at[r_dn, c, pl.ds(48, 48)], r1b.at[u, 1])
        send(g.at[r_dn, c], r2b.at[u, 1], S_G2 + 2 * u + 1, R_G2 + 2 * u + 1, dev_dn, lambda: r2b.at[u, 1])

    def g_s3(m, i):
        u = m * 4 + i
        g = blk(m, i)
        wrecv(r2b.at[u, 0], R_G2 + 2 * u)
        wrecv(r2b.at[u, 1], R_G2 + 2 * u + 1)
        add_into(g.at[r, c], r2b.at[u, 0], r2b.at[u, 1])
        if i > 0:
            send(g.at[r, c], zb.at[m, i - 1], S_GZ + u, R_GZ + m * 3 + i - 1, (dp, zdst(i)),
                 lambda: zb.at[m, i - 1])

    def g_fin(m):
        for i in (1, 2, 3):
            wrecv(zb.at[m, i - 1], R_GZ + m * 3 + i - 1)
        t = wmlp[m, z, r, c].astype(F32)
        for i in range(3):
            t = t + zb[m, i].astype(F32)
        fs[m] = t.astype(BF)
        dst = gm_out.at[m, r, c]
        send(fs.at[m], dst, S_FA + 3 * m, R_FA + 3 * m, dev_up, lambda: fs.at[m])
        send(fs.at[m], dst, S_FA + 3 * m + 1, R_FA + 3 * m + 1, dev_dn, lambda: fs.at[m])
        send(fs.at[m], dst, S_FA + 3 * m + 2, R_FA + 3 * m + 2, dev_pair, lambda: fs.at[m])

    def g_ag(m):
        lo = gm_out.at[m, r_dn, c, pl.ds(0, 48)]
        hi = gm_out.at[m, r_up, c, pl.ds(48, 48)]
        wrecv(gm_out.at[m, r_dn, c], R_FA + 3 * m)
        send(lo, lo, S_FB + 2 * m, R_FB + 2 * m, dev_up, lambda: r1b.at[0, 0])
        full = gm_out.at[m, r_dn, c]
        send(full, full, S_FC + 3 * m, R_FC + 3 * m, dev_pair, lambda: fs.at[m])
        wrecv(gm_out.at[m, r_up, c], R_FA + 3 * m + 1)
        send(hi, hi, S_FB + 2 * m + 1, R_FB + 2 * m + 1, dev_dn, lambda: r1b.at[0, 0])
        full2 = gm_out.at[m, r_up, c]
        send(full2, full2, S_FC + 3 * m + 1, R_FC + 3 * m + 1, dev_pair, lambda: fs.at[m])

    def g_ag2(m):
        wrecv(gm_out.at[m, r_op, c, pl.ds(0, 48)], R_FB + 2 * m)
        wrecv(gm_out.at[m, r_op, c, pl.ds(48, 48)], R_FB + 2 * m + 1)
        full = gm_out.at[m, r_op, c]
        send(full, full, S_FC + 3 * m + 2, R_FC + 3 * m + 2, dev_pair, lambda: fs.at[m])

    def g_end(m):
        wrecv(gm_out.at[m, r, oc], R_FA + 3 * m + 2)
        wrecv(gm_out.at[m, r_dn, oc], R_FC + 3 * m)
        wrecv(gm_out.at[m, r_up, oc], R_FC + 3 * m + 1)
        wrecv(gm_out.at[m, r_op, oc], R_FC + 3 * m + 2)

    def hat(h):
        return gatt.at[h // 2], (h % 2) * 64

    def a_s1(h):
        g, o = hat(h)
        for j, dev in enumerate((dev_up, dev_dn)):
            send(g.at[r_op, pl.ds(o + 32 * j, 32)], a1b.at[h, j], S_A1 + 2 * h + j, R_A1 + 2 * h + j, dev,
                 lambda j=j: a1b.at[h, j])

    def a_s2(h):
        g, o = hat(h)
        for j, (dev, rr) in enumerate(((dev_up, r_up), (dev_dn, r_dn))):
            wrecv(a1b.at[h, j], R_A1 + 2 * h + j)
            add_into(g.at[rr, pl.ds(o + 32 * j, 32)], a1b.at[h, j])
            send(g.at[rr, pl.ds(o, 64)], a2b.at[h, j], S_A2 + 2 * h + j, R_A2 + 2 * h + j, dev,
                 lambda j=j: a2b.at[h, j])

    def a_s3(h):
        g, o = hat(h)
        for j in (0, 1):
            wrecv(a2b.at[h, j], R_A2 + 2 * h + j)
        add_into(g.at[r, pl.ds(o, 64)], a2b.at[h, 0], a2b.at[h, 1])
        zz, to = h // 3, (h % 3) * 64

        def go():
            zd = 2 * c + zz
            slot = (zd - z + 3) % 4
            send(g.at[r, pl.ds(o, 64)], azb.at[slot, pl.ds(to, 64)], S_AZ + h, R_AZ + 3 * h + slot, (dp, zd),
                 lambda: a2b.at[h, 0], need(zz))

        pl.when(need(zz))(go)

    def a_fin(jj):
        def go(zz):
            h = 3 * zz + jj
            g, o = hat(h)
            for slot in range(3):
                wrecv(azb.at[slot, pl.ds(jj * 64, 64)], R_AZ + 3 * h + slot)
            t = g[r, o : o + 64].astype(F32)
            for slot in range(3):
                t = t + azb[slot, jj * 64 : jj * 64 + 64].astype(F32)
            fa[jj * 64 : jj * 64 + 64] = t.astype(BF)

        for zz in (0, 1):
            when(mine[zz], functools.partial(go, zz))

    def a_ag(jj):
        part = fa.at[pl.ds(jj * 64, 64)]
        for i, dev in enumerate((dev_up, dev_dn, dev_pair)):
            send(part, ga_out.at[r, pl.ds(jj * 64, 64)], S_HA + 3 * jj + i, R_HA + 3 * jj + i, dev,
                 lambda: fa.at[pl.ds(0, 64)], own_c)

    def a_ag2(jj):
        for j, (dev, rr) in enumerate(((dev_up, r_dn), (dev_dn, r_up))):
            part = ga_out.at[rr, pl.ds(jj * 64, 64)]
            wrecv(part, R_HA + 3 * jj + j)
            piece = ga_out.at[rr, pl.ds(jj * 64 + 32 * j, 32)]
            send(piece, piece, S_HB + 2 * jj + j, R_HB + 2 * jj + j, dev, lambda: fa.at[pl.ds(0, 32)], own_c)
            send(part, part, S_HC + 3 * jj + j, R_HC + 3 * jj + j, dev_pair, lambda: fa.at[pl.ds(0, 64)], own_c)

    def a_ag3(jj):
        for j in (0, 1):
            wrecv(ga_out.at[r_op, pl.ds(jj * 64 + 32 * j, 32)], R_HB + 2 * jj + j)
        part = ga_out.at[r_op, pl.ds(jj * 64, 64)]
        send(part, part, S_HC + 3 * jj + 2, R_HC + 3 * jj + 2, dev_pair, lambda: fa.at[pl.ds(0, 64)], own_c)

    def a_end():
        for jj in range(3):
            part = pl.ds(jj * 64, 64)
            wrecv(ga_out.at[r, part], R_HA + 3 * jj + 2)
            for j, rr in enumerate((r_dn, r_up, r_op)):
                wrecv(ga_out.at[rr, part], R_HC + 3 * jj + j)

    GA_ = 0.7978845608028654

    def gr(steps):
        for st in steps.split():
            kind, u = int(st[0]), int(st[1:])
            if kind > 3:
                (g_fin, g_ag, g_ag2)[kind - 4](u)
            elif u < 8:
                (g_s1, g_s2, g_s3)[kind - 1](1 - u % 2, u // 2)
            else:
                (a_s1, a_s2, a_s3)[kind - 1](u - 8)

    def mlp_body(i, _):
        zp = zdst(i)

        def got(dz):
            mg_done(0, dz)
            mg_done(1, dz)

        for it, dz in ((1, 1), (2, 3), (3, 2)):
            pl.when(i == it)(functools.partial(got, dz))
        for fb in range(D // 256):
            cols = slice(fb * 256, fb * 256 + 256)
            fcb = wmlp[0, zp, :, :, :, cols].reshape(D, 256)
            pre = dot(n2[...], fcb) + bfa[zp, 0:1, cols]
            sq = pre * pre
            t = jnp.tanh(pre * (GA_ + (0.044715 * GA_) * sq))
            hf = 0.5 * (1.0 + t)
            act[:, cols] = (pre * hf).astype(BF)
            gp = hf * (1.0 + (1.0 - hf) * (pre * (2.0 * GA_ + (0.26829 * GA_) * sq)))
            prj = wmlp[1, zp].reshape(D, D)[cols, :]
            dp_ = (nt(og[...], prj) * gp).astype(BF)
            dpre[:, cols] = dp_
            sb[pl.ds(6 + zp, 1), cols] = jnp.sum(dp_.astype(F32), axis=0, keepdims=True)
        prj = wmlp[1, zp].reshape(D, D)
        for rb in range(R // 256):
            rows = slice(rb * 256, rb * 256 + 256)
            oacc[rows, :] += dot(act[rows, :], prj)
        for j in range(2):
            cols = slice(j * HC, j * HC + HC)
            wmlp[1, zp, 2 * j : 2 * j + 2] = tn(act[:, cols], og[...]).astype(BF).reshape(2, 2, D // 8, D)
        at(i, 0)
        fc = wmlp[0, zp].reshape(D, D)
        for rb in range(R // 256):
            rows = slice(rb * 256, rb * 256 + 256)
            dn2[rows, :] += nt(dpre[rows, :], fc)
        for j in range(2):
            cols = slice(j * HC, j * HC + HC)
            wmlp[0, zp, 2 * j : 2 * j + 2] = tn(n2[:, cols], dpre[...]).astype(BF).reshape(2, 2, D // 8, D)
        at(i, 1)
        return 0

    def at(i, where):
        for kk_ in range(4):
            def here(kk_=kk_):
                g_s0(1 - where, kk_)
                mg(G_LOOP[kk_][where])
                gr(T_LOOP[kk_][where])

            pl.when(i == kk_)(here)

    mg(G_MLP)
    lax.fori_loop(0, 4, mlp_body, 0)

    def bwd2_body(i, _):
        rows = pl.ds(al(i * LB, LB), LB)
        x = mid[rows, :]
        p0 = lax.broadcasted_iota(jnp.int32, (LB, 1), 0).astype(F32) + (row0 + i * LB).astype(F32)
        ok = jnp.where(p0 < length, 1.0, 0.0)
        bo[rows, :] = ((x + oacc[rows, :] + vecs[5:6, :]) * ok).astype(BF)
        n, rstd = stats(x)
        dn = dn2[rows, :]
        e = dn * vecs[3:4, :]
        em = jnp.mean(e, axis=1, keepdims=True)
        en = jnp.mean(e * n, axis=1, keepdims=True)
        gm = og[rows, :].astype(F32) + (e - em - n * en) * rstd
        mid[rows, :] = gm
        ga[pl.ds(al(row0 + i * LB, LB), LB), :] = gm.astype(BF)
        sb[2:3, :] += jnp.sum(dn * n, axis=0, keepdims=True)
        sb[3:4, :] += jnp.sum(dn, axis=0, keepdims=True)
        sb[4:5, :] += jnp.sum(gm, axis=0, keepdims=True)
        return 0

    lax.fori_loop(0, R // LB, bwd2_body, 0)
    send(ga.at[mine_rows], ga.at[mine_rows], S_GA, R_GA, dev_pair, lambda: ga.at[mine_rows])
    when(swap, lambda: send(bo, bo_out, S_BO, R_BO, dev_swap, lambda: bo, swap))
    w_bo = local(lambda: bo, lambda: bo_out, keep)
    gr(T_BWD2)
    wrecv(ga.at[pair_rows], R_GA)

    def dctx_body(i, _):
        rows = pl.ds(al(i * BQ, BQ), BQ)
        d = nt(ga[rows, :], watt[3])
        do[rows, :] = d.astype(BF)
        for hp in range(3):
            lanes = slice(hp * 128, hp * 128 + 128)
            dot_[lanes, rows] = do[rows, lanes].T
        return 0

    lax.fori_loop(0, NB, dctx_body, 0)
    gr(T_DCTX)

    def bwd_pair(hp, _):
        prep = []
        for hh in (0, 1):
            h = hp * 2 + hh
            lanes, inhead = head_prep(hp, hh)
            hrows = pl.ds(al(h * 64, 64), 64)
            vh[hh] = jnp.where(inhead, v[:, lanes].astype(F32), 0.0).astype(BF)
            dl = jnp.sum(dot_[hrows, :].astype(F32) * ot[hrows, :].astype(F32), axis=0, keepdims=True)
            prep.append((h, hrows, dl, lse[h]))
        for kb in range(NB):
            krows = slice(kb * BQ, kb * BQ + BQ)
            qs = slice(kb * BQ, T)
            dks, dvs = [], []
            for hh in (0, 1):
                h, hrows, dl, ls_h = prep[hh]
                s = dot(kh[hh, krows, :], qh[hh, :, qs])
                diag = s[:, :BQ] + cmask[...]
                s = diag if kb == NB - 1 else jnp.concatenate([diag, s[:, BQ:]], axis=1)
                p = jnp.exp2(s * CS - ls_h[0:1, qs])
                dpr = dot(vh[hh, krows, :], dot_[lanes, qs])
                ds = (p * (dpr - dl[:, qs])).astype(BF)
                dvs.append(dot(p.astype(BF), do[qs, lanes]))
                dks.append(dot(ds, q[qs, lanes]) * 0.125)
                piece = dot(kt[hrows, krows], ds)
                if kb == 0:
                    dqa[hh] = piece
                else:
                    dqa[hh, :, qs] += piece
            first = lane < 64
            v[krows, lanes] = jnp.where(first, dvs[0], dvs[1]).astype(BF)
            k[krows, lanes] = jnp.where(first, dks[0], dks[1]).astype(BF)
            by_pair(hp, gr, [T_ATT[j][kb] for j in range(3)])
        for hh in (0, 1):
            qt[prep[hh][1], :] = (dqa[hh] * 0.125).astype(BF)
        lanes = pl.ds(al(hp * 128, 128), 128)

        def tr2(i, _):
            rows = pl.ds(al(i * BQ, BQ), BQ)
            q[rows, lanes] = qt[lanes, rows].T
            kt[lanes, rows] = k[rows, lanes].T
            vt[lanes, rows] = v[rows, lanes].T
            return 0

        lax.fori_loop(0, NB, tr2, 0)
        for t, ref in enumerate((qt, kt, vt)):
            gatt[hp, t] = dot(ref[lanes, :], n1[...]).astype(BF)
        gatt[hp, 3] = dot(ot[lanes, :], ga[...]).astype(BF)
        for j in range(3):
            pl.when(hp == j)(functools.partial(gr, T_PAIR[j]))
        return 0

    lax.fori_loop(0, 3, bwd_pair, 0)

    def dx(rows):
        return dot(q[rows, :], watt[0]) + dot(k[rows, :], watt[1]) + dot(v[rows, :], watt[2])

    ps2[...] = dx(pair_rows).astype(BF)
    send(ps2, pr2, S_DX, R_DX, dev_pair, lambda: ps2)
    gr(T_DX)
    dn2[...] = dx(mine_rows)
    gr(T_DX2)
    sb[pl.ds(10 + c, 1), :] = jnp.concatenate(
        [jnp.sum(q[...].astype(F32), axis=0, keepdims=True), jnp.sum(v[...].astype(F32), axis=0, keepdims=True)],
        axis=1,
    )
    wrecv(pr2, R_DX)

    def bwd1_body(i, _):
        rows = pl.ds(al(i * LB, LB), LB)
        n, rstd = stats(hid[rows, :].astype(F32))
        dn = dn2[rows, :] + pr2[rows, :].astype(F32)
        e = dn * vecs[0:1, :]
        em = jnp.mean(e, axis=1, keepdims=True)
        en = jnp.mean(e * n, axis=1, keepdims=True)
        gi[rows, :] = (mid[rows, :] + (e - em - n * en) * rstd).astype(BF)
        sb[0:1, :] += jnp.sum(dn * n, axis=0, keepdims=True)
        sb[1:2, :] += jnp.sum(dn, axis=0, keepdims=True)
        for j in range(R // LB):
            def out(j=j):
                part = pl.ds(j * LB, LB)
                send(gi.at[part], gi_out.at[part], S_GI + j, R_GI + j, dev_swap, lambda: gi.at[part], swap)

            pl.when((i == j) & swap)(out)
        return 0

    gr(T_AG)
    lax.fori_loop(0, R // LB, bwd1_body, 0)
    gr(T_LAST)
    w_gi = local(lambda: gi, lambda: gi_out, keep)

    def small_pair():
        send(sb.at[pl.ds(0, 16)], srb.at[8], S_SM, R_SM + 8, dev_pair, lambda: srb.at[0])

    def small_ring():
        wrecv(srb.at[8], R_SM + 8)
        t = sb[0:16] + srb[8]
        sb[16:32] = t
        srb[r] = t
        for j, dev in enumerate((dev_up, dev_dn, dev_op)):
            send(sb.at[pl.ds(16, 16)], srb.at[r], S_SM + 1 + j, R_SM + r, dev, lambda: srb.at[0])

    def small_z():
        for o in (r_up, r_dn, r_op):
            wrecv(srb.at[o], R_SM + o)
        t = (srb[0] + srb[1]) + (srb[2] + srb[3])
        sb[32:48] = t
        srb[4 + z] = t
        for dz in (1, 2, 3):
            send(sb.at[pl.ds(32, 16)], srb.at[4 + z], S_SM + 3 + dz, R_SM + 4 + z, dev_z[dz], lambda: srb.at[0])

    def small_end():
        for dz in (1, 2, 3):
            wrecv(srb.at[4 + zsh(dz)], R_SM + 4 + zsh(dz))
        t = (srb[4] + srb[5]) + (srb[6] + srb[7])
        sb[48:64] = t
        small_out[0:6, :] = t[0:6]
        small_out[6:7, :] = sb[pl.ds(54 + z, 1), :]
        row = sb[pl.ds(58 + z // 2, 1), :]
        odd = (z % 2).astype(F32)
        even = 1.0 - odd
        bq = even * row[:, :ZS] + odd * row[:, ZS : 2 * ZS]
        bv = even * row[:, 2 * ZS : 3 * ZS] + odd * row[:, 3 * ZS :]
        gap = jnp.zeros((1, HC - ZS), F32)
        small_out[7:8, :] = jnp.concatenate([bq, gap, bv, gap], axis=1)

    small_pair()
    gr(T_AG2)
    small_ring()
    for jj in range(3):
        a_fin(jj)
        when(own_c, functools.partial(a_ag, jj))
    small_z()
    for jj in range(3):
        when(own_c, functools.partial(a_ag2, jj))
    for jj in range(3):
        when(own_c, functools.partial(a_ag3, jj))
    small_end()

    w_fs = [local(lambda: fs.at[0], lambda: gm_out.at[0, r, c]), local(lambda: fs.at[1], lambda: gm_out.at[1, r, c])]
    w_fa = local(lambda: fa, lambda: ga_out.at[r], own_c)
    w_bo()
    w_gi()
    for w in w_fs:
        w()
    w_fa()
    for m in (0, 1):
        g_end(m)
    when(not_own, a_end)
    when(swap, lambda: wrecv(bo_out, R_BO))
    for j in range(R // LB):
        when(swap, lambda: wrecv(gi_out.at[pl.ds(j * LB, LB)], R_GI + j))
    for sid, (ref, cond) in pending.items():
        when(cond, lambda sid=sid, ref=ref: wsend(ref(), sid))


def widen_kernel(bo, gi, gm, ga, bo_o, gi_o, fc_o, proj_o, qkv_o, out_o):
    bo_o[...] = bo[...]
    gi_o[...] = gi[...]
    fc_o[...] = gm[0].astype(F32)
    proj_o[...] = gm[1].astype(F32)
    qkv_o[...] = ga[:3].astype(F32)
    out_o[...] = ga[3].astype(F32)


def widen(bo, gi, gm, ga):
    n = 4
    (R, D), ZS = bo.shape, ga.shape[1]
    rows = lambda m: pl.BlockSpec((m // n, D), lambda i: (i, 0))
    stack = lambda k, m: pl.BlockSpec((k, m // n, D), lambda i: (0, i, 0))
    return pl.pallas_call(
        widen_kernel,
        grid=(n,),
        out_shape=(
            jax.ShapeDtypeStruct((R, D), BF), jax.ShapeDtypeStruct((R, D), BF),
            jax.ShapeDtypeStruct((D, D), F32), jax.ShapeDtypeStruct((D, D), F32),
            jax.ShapeDtypeStruct((3, ZS, D), F32), jax.ShapeDtypeStruct((ZS, D), F32),
        ),
        in_specs=[rows(R), rows(R), stack(2, D), stack(4, ZS)],
        out_specs=(rows(R), rows(R), rows(D), rows(D), stack(3, ZS), rows(ZS)),
        compiler_params=pltpu.CompilerParams(vmem_limit_bytes=64 * 1024 * 1024 - 65536),
        name="widen",
    )(bo, gi, gm, ga)


def body(
    hidden_in, lengths, ln1_gain, ln1_bias, w_qkv, b_query, b_value, w_out, b_out,
    ln2_gain, ln2_bias, w_fc, b_fc, w_proj, b_proj, out_grad,
):
    R, D = hidden_in.shape
    T, HC, ZS, EB = 2 * R, D // 2, D // 4, D // 8
    z = lax.axis_index("tensor")
    odd = z % 2 == 1
    lo, hi = (lambda t: jnp.pad(t, (0, HC - ZS))), (lambda t: jnp.pad(t, (HC - ZS, 0)))
    place = lambda t: jnp.where(odd, hi(t), lo(t))
    qv_row = jnp.pad(place(b_query), (0, HC)) + jnp.pad(place(b_value), (HC, 0))
    row = lax.broadcasted_iota(jnp.int32, (16, D), 0)
    vecs = jnp.zeros((16, D), BF)
    for at_row, vec in (
        (0, ln1_gain), (1, ln1_bias), (2, b_out), (3, ln2_gain), (4, ln2_bias), (5, b_proj), (8, b_fc), (9, qv_row),
    ):
        vecs = jnp.where(row == at_row, vec[None, :], vecs)
    vecs = vecs.astype(F32)
    wq = jnp.transpose(w_qkv, (1, 2, 0))
    wf = w_fc.reshape(4, 2, EB, D)
    wp = w_proj.reshape(4, 2, EB, D)
    vm = lambda *s: pltpu.VMEM(s, BF)
    vf = lambda *s: pltpu.VMEM(s, F32)
    scratch = [
        vf(8, 128), vf(8, 128), vf(4, 8, D), vm(R, D), vm(R, D), vm(T, D), vm(4, HC, D), vm(2, 4, 4, 2, EB, D),
        vm(T, HC), vm(T, HC), vm(T, HC), vm(HC, T), vm(HC, T), vm(HC, T),
        vm(T, HC), vm(HC, T), vm(HC, T),
        vf(R, D), vm(R, D), vf(R, D), vf(R, D), vm(R, D), vm(R, D), vm(T, D),
        vm(R, D), vm(R, D), vm(R, D), vm(R, D), vm(R, D), vm(R, D),
        vf(6, 1, T), vf(2, 64, T), vf(256, 256), vm(2, T, 128), vm(2, T, 128), vm(2, 128, T),
        vm(8, 4, EB, D), vm(8, 2, EB // 2, D), vm(8, 2, EB, D), vm(2, 3, EB, D), vm(2, EB, D),
        vm(3, 4, 128, D), vm(6, 2, 32, D), vm(6, 2, 64, D), vm(3, ZS, D), vm(ZS, D),
        vf(64, D), vf(9, 16, D),
        pltpu.SemaphoreType.DMA((SID.n,)), pltpu.SemaphoreType.DMA((RID.n,)), pltpu.SemaphoreType.DMA((12,)),
    ]
    anyspec = pl.BlockSpec(memory_space=pl.ANY)
    vspec = pl.BlockSpec(memory_space=pltpu.VMEM)
    block_out, grad_input, gm, gatt, small = pl.pallas_call(
        kernel,
        out_shape=(
            jax.ShapeDtypeStruct((R, D), BF),
            jax.ShapeDtypeStruct((R, D), BF),
            jax.ShapeDtypeStruct((2, 4, 2, EB, D), BF),
            jax.ShapeDtypeStruct((4, ZS, D), BF),
            jax.ShapeDtypeStruct((8, D), F32),
        ),
        in_specs=[pl.BlockSpec(memory_space=pltpu.SMEM), vspec] + [anyspec] * 6,
        out_specs=(anyspec, anyspec, anyspec, anyspec, vspec),
        scratch_shapes=scratch,
        compiler_params=pltpu.CompilerParams(
            collective_id=0, has_side_effects=True, vmem_limit_bytes=64 * 1024 * 1024 - 65536
        ),
        name="layer",
    )(lengths, vecs, hidden_in, out_grad, wq, w_out, wf, wp)
    data_count = lax.axis_size("dp")
    gm = gm.reshape(2, D, D)
    if data_count > GROUP:
        groups = [list(range(s, data_count, GROUP)) for s in range(GROUP)]
        gm, gatt, small = (
            lax.psum(t.astype(F32), "dp", axis_index_groups=groups) for t in (gm, gatt, small)
        )
    block_out, grad_input, g_fc, g_proj, g_qkv, g_out = widen(block_out, grad_input, gm, gatt)
    g_qkv = jnp.transpose(g_qkv, (2, 0, 1))
    gbq = small[7, :ZS]
    gbv = small[7, HC : HC + ZS]
    return (
        block_out, grad_input, small[0], small[1], g_qkv, gbq, gbv, g_out, small[4],
        small[2], small[3], g_fc, small[6], g_proj, small[5],
    )


def solution(mesh):
    rows = P(("dp", "tensor"), None)
    in_specs = (
        rows, P("dp"), P(), P(), P(None, None, "tensor"), P("tensor"), P("tensor"), P("tensor", None),
        P(), P(), P(), P(None, "tensor"), P("tensor"), P("tensor", None), P(), rows,
    )
    out_specs = (
        rows, rows, P(), P(), P(None, None, "tensor"), P("tensor"), P("tensor"), P("tensor", None),
        P(), P(), P(), P(None, "tensor"), P("tensor"), P("tensor", None), P(),
    )
    return jax.shard_map(body, mesh=mesh, in_specs=in_specs, out_specs=out_specs, check_vma=False)
```

```python
import functools

import jax
import jax.numpy as jnp
from jax import lax
from jax.experimental import pallas as pl
from jax.experimental.pallas import tpu as pltpu
from jax.sharding import PartitionSpec as P

BF = jnp.bfloat16
F32 = jnp.float32
EPS = 1e-5
NEG = -1e30
LOG2E = 1.4426950408889634
MESH = pl.DeviceIdType.MESH
RING = 4
GROUP = 2 * RING


T_LOOP = (("", "10"), ("11 20", "12"), ("13 21", "14"), ("15 22", "16"))
T_BWD2 = "17 23 30"
T_DCTX = "31"
T_ATT = (("24", "32", "25", "33"), ("26", "34", "27", "35"), ("28 36", "29", "37 210", "211"))
T_PAIR = ("18 19", "110 111", "112 113 41 40")
T_DX = "38 39"
T_DX2 = "212 213 310 311"
T_AG = "51 50"
T_LAST = "312 313"
T_AG2 = "61 60"
G_EARLY = ""
G_QKV = "a0"
G_TR = ""
G_ATT = (("a1", "", "b0", ""), ("b1 a2", "", "p0 a3", "p1"), ("b2", "", "b3 p2", "a4"))
G_CTX = ""
G_MLP = "p3 a5"
G_LOOP = (("b4", "b5"), ("p4", "p5"), ("", ""), ("", ""))


def dot(a, b, ca=1, cb=0):
    return lax.dot_general(a, b, (((ca,), (cb,)), ((), ())), preferred_element_type=F32)


def nt(a, b):
    return dot(a, b, 1, 1)


def tn(a, b):
    return dot(a, b, 0, 0)


def al(v, m):
    return pl.multiple_of(v, m)


class Ids:
    def __init__(self):
        self.n = 0

    def __call__(self, k):
        base = self.n
        self.n += k
        return base


SID = Ids()
S_LEN, S_BIAS, S_HID, S_OG, S_AS1 = SID(1), SID(3), SID(1), SID(1), SID(6)
S_ARA, S_ARB = SID(8), SID(8)
S_MS1, S_MRA, S_MRB, S_MP = SID(6), SID(12), SID(12), SID(6)
S_N1, S_PO, S_GA, S_DX, S_BO, S_GI = SID(1), SID(1), SID(1), SID(1), SID(1), SID(8)
S_GP, S_G1, S_G2, S_GZ = SID(8), SID(16), SID(16), SID(8)
S_FA, S_FB, S_FC = SID(6), SID(4), SID(6)
S_A1, S_A2, S_AZ = SID(12), SID(12), SID(6)
S_HA, S_HB, S_HC = SID(9), SID(6), SID(9)
S_SM = SID(7)
RID = Ids()
R_LEN, R_BIAS, R_HID, R_OG, R_AS1 = RID(1), RID(3), RID(1), RID(1), RID(4)
R_ARA, R_ARB = RID(8), RID(8)
R_MS1, R_MRA, R_MRB, R_MP = RID(6), RID(12), RID(12), RID(6)
R_N1, R_PO, R_GA, R_DX, R_BO, R_GI = RID(1), RID(1), RID(1), RID(1), RID(1), RID(8)
R_GP, R_G1, R_G2, R_GZ = RID(8), RID(16), RID(16), RID(6)
R_FA, R_FB, R_FC = RID(6), RID(4), RID(6)
R_A1, R_A2, R_AZ = RID(12), RID(12), RID(18)
R_HA, R_HB, R_HC = RID(9), RID(6), RID(9)
R_SM = RID(9)


def kernel(
    lengths, vecs, hid_in, og_in, wq, wo, wf, wp,
    bo_out, gi_out, gm_out, ga_out, small_out,
    lens, lrecv, bfa, hid, og, n1, watt, wmlp, q, k, v, qt, kt, vt, do, dot_, ot,
    mid, n2, oacc, dn2, act, dpre, ga, ps, pr, ps2, pr2, bo, gi,
    lse, dqa, cmask, kh, vh, qh,
    prb, r1b, r2b, zb, fs, gatt, a1b, a2b, azb, fa, sb, srb,
    ss, rs, ls,
):
    D = hid_in.shape[1]
    R = hid_in.shape[0]
    T = 2 * R
    HC = D // 2
    BQ = 256
    NB = T // BQ
    dp = lax.axis_index("dp")
    z = lax.axis_index("tensor")
    base = (dp // GROUP) * GROUP
    chip = (dp - base) // 2
    c = dp % 2
    oc = 1 - c
    cy = chip // 2
    cx = chip % 2
    r = 3 * cy + cx - 2 * cx * cy

    def ring_dp(rr, core):
        y = rr // 2
        x = rr % 2 + y - 2 * (rr % 2) * y
        return base + (2 * y + x) * 2 + core

    r_up = (r + 1) % RING
    r_dn = (r + 3) % RING
    r_op = (r + 2) % RING
    dev_up = (ring_dp(r_up, c), z)
    dev_dn = (ring_dp(r_dn, c), z)
    dev_op = (ring_dp(r_op, c), z)
    dev_pair = (dp + 1 - 2 * c, z)
    dev_z = [None] + [(dp, (z + dz) % 4) for dz in (1, 2, 3)]
    z_x = z + 1 - 2 * (z % 2)
    dev_swap = (dp + 1 - 2 * c, z_x)
    keep = c == z % 2
    swap = c != z % 2
    own_c = z // 2 == c
    mine = (z == 2 * c, z == 2 * c + 1)
    not_own = z // 2 != c
    zz_own = z % 2
    pending = {}

    def when(cond, fn):
        if cond is None:
            fn()
        else:
            pl.when(cond)(fn)

    def desc(src, dst, sid, rid, dev):
        return pltpu.make_async_remote_copy(
            src_ref=src, dst_ref=dst, send_sem=ss.at[sid], recv_sem=rs.at[rid],
            device_id=dev, device_id_type=MESH,
        )

    def send(src, dst, sid, rid, dev, late=None, cond=None):
        desc(src, dst, sid, rid, dev).start()
        if late is not None:
            pending[sid] = (late, cond)

    def wsend(ref, sid):
        desc(ref, ref, sid, 0, dev_pair).wait_send()

    def wrecv(ref, rid):
        desc(ref, ref, 0, rid, dev_pair).wait_recv()

    barrier = pltpu.get_barrier_semaphore()
    cross = [(dp + 1 - 2 * c, (z + dz) % 4) for dz in (1, 2, 3)]
    for dev in (dev_up, dev_dn, dev_op, dev_pair, dev_z[1], dev_z[2], dev_z[3], *cross):
        pl.semaphore_signal(barrier, inc=1, device_id=dev, device_id_type=MESH)

    loc_n = [0]

    def local(src, dst, cond=None):
        i = loc_n[0]
        loc_n[0] += 1
        cp = lambda: pltpu.make_async_copy(src(), dst(), ls.at[i])
        when(cond, lambda: cp().start())
        return lambda: when(cond, lambda: cp().wait())

    w_hid = local(lambda: hid_in, lambda: hid, keep)
    bias = vecs.at[pl.ds(8, 8)]
    ZS = D // 4

    def att_rows(zz):
        return pl.ds(al(zz * ZS, 16), ZS)

    ZQ = ZS // RING

    def att_piece(e, zz, rr):
        rows = pl.ds(al(zz * ZS + rr * ZQ, 16), ZQ)
        return watt.at[3, rows] if e else watt.at[pl.ds(0, 3), rows]

    def att_half(e, zz, rr, side):
        rows = pl.ds(al(zz * ZS + rr * ZQ, 16), ZQ)
        cols = pl.ds(side * HC, HC)
        return watt.at[3, rows, cols] if e else watt.at[pl.ds(0, 3), rows, cols]

    def att_s1(e):
        for dz in (1, 2, 3):
            rows = pl.ds(al(r * ZQ, 16), ZQ)
            src = wo.at[rows] if e else wq.at[:, rows]
            dev = (dp - c + z // 2, (z + dz) % 4)
            send(src, att_piece(e, zz_own, r), S_AS1 + 3 * e + dz - 1, R_AS1 + 2 * e + zz_own, dev,
                 lambda: att_piece(e, 0, 0), swap)

    w_wq = local(lambda: wq, lambda: watt.at[pl.ds(0, 3), att_rows(zz_own)], own_c)
    w_wo = local(lambda: wo, lambda: watt.at[3, att_rows(zz_own)], own_c)
    w_og = local(lambda: og_in, lambda: og, keep)
    w_mlp0 = [local(lambda: wf, lambda: wmlp.at[0, z]), local(lambda: wp, lambda: wmlp.at[1, z])]
    def zsh(dz):
        return (z - dz + 4) % 4

    def mg_s1(m, dz):
        w = (wf, wp)[m]
        u = m * 3 + dz - 1
        send(w.at[r, c], wmlp.at[m, z, r, c], S_MS1 + u, R_MS1 + u, dev_z[dz], lambda: w.at[r, c])

    def mg_a(m, dz):
        u = m * 3 + dz - 1
        piece = wmlp.at[m, zsh(dz), r, c]
        wrecv(piece, R_MS1 + u)
        send(piece, piece, S_MRA + 2 * u, R_MRA + 2 * u, dev_up)
        send(piece, piece, S_MRA + 2 * u + 1, R_MRA + 2 * u + 1, dev_dn)

    def mg_b(m, dz):
        u = m * 3 + dz - 1
        zp = zsh(dz)
        wrecv(wmlp.at[m, zp, r_dn, c], R_MRA + 2 * u)
        lo = wmlp.at[m, zp, r_dn, c, pl.ds(0, 48)]
        send(lo, lo, S_MRB + 2 * u, R_MRB + 2 * u, dev_up)
        wrecv(wmlp.at[m, zp, r_up, c], R_MRA + 2 * u + 1)
        hi = wmlp.at[m, zp, r_up, c, pl.ds(48, 48)]
        send(hi, hi, S_MRB + 2 * u + 1, R_MRB + 2 * u + 1, dev_dn)

    def mg_p(m, dz):
        u = m * 3 + dz - 1
        zp = zsh(dz)
        wrecv(wmlp.at[m, zp, r_op, c, pl.ds(0, 48)], R_MRB + 2 * u)
        wrecv(wmlp.at[m, zp, r_op, c, pl.ds(48, 48)], R_MRB + 2 * u + 1)
        mine = wmlp.at[m, zp, :, c]
        send(mine, mine, S_MP + u, R_MP + u, dev_pair)

    def mg_done(m, dz):
        u = m * 3 + dz - 1
        zp = zsh(dz)
        wrecv(wmlp.at[m, zp, :, oc], R_MP + u)
        for s in (0, 1):
            wsend(wmlp.at[m, zp, r, c], S_MRA + 2 * u + s)
            wsend(wmlp.at[m, zp, r, c, pl.ds(0, 48)], S_MRB + 2 * u + s)
        wsend(wmlp.at[m, zp, :, c], S_MP + u)

    munits = [(0, 1), (1, 1), (0, 3), (1, 3), (0, 2), (1, 2)]

    def mg(steps):
        for st in steps.split():
            {"a": mg_a, "b": mg_b, "p": mg_p}[st[0]](*munits[int(st[1])])

    row0 = c * R
    half = ZS // 2

    def stats(x):
        mu = jnp.mean(x, axis=1, keepdims=True)
        cen = x - mu
        var = jnp.mean(cen * cen, axis=1, keepdims=True)
        rstd = lax.rsqrt(var + EPS)
        return cen * rstd, rstd

    LB = 128

    def ln1_body(i, _):
        rows = pl.ds(al(i * LB, LB), LB)
        n, _r = stats(hid[rows, :].astype(F32))
        out = n * vecs[0:1, :] + vecs[1:2, :]
        n1[pl.ds(al(row0 + i * LB, LB), LB), :] = out.astype(BF)
        return 0

    mine_rows = pl.ds(al(row0, R), R)
    pair_rows = pl.ds(al(oc * R, R), R)

    def norm_one():
        lax.fori_loop(0, R // LB, ln1_body, 0)

    def norm_one_send():
        send(n1.at[mine_rows], n1.at[mine_rows], S_N1, R_N1, dev_pair, lambda: n1.at[mine_rows])

    def norm_one_far():
        wrecv(hid, R_HID)
        norm_one()
        norm_one_send()

    bfa[z] = bias[...]
    w_hid()
    pl.when(keep)(norm_one)

    kk = lax.broadcasted_iota(jnp.int32, (BQ, BQ), 0)
    qq = lax.broadcasted_iota(jnp.int32, (BQ, BQ), 1)
    cmask[...] = jnp.where(kk <= qq, 0.0, NEG)
    pl.semaphore_wait(barrier, 10)
    pl.when(swap)(lambda: att_s1(0))
    when(swap, lambda: send(hid_in, hid, S_HID, R_HID, dev_swap, lambda: hid_in, swap))
    pl.when(swap)(lambda: att_s1(1))
    for dz in (1, 2, 3):
        send(bias, bfa.at[z], S_BIAS + dz - 1, R_BIAS + dz - 1, dev_z[dz], lambda: bias)
    lens[...] = jnp.full((8, 128), lengths[z // 2].astype(F32))
    send(lens, lrecv, S_LEN, R_LEN, dev_pair, lambda: lens)
    pl.when(keep)(norm_one_send)

    needs = (z != 2 * c, z != 2 * c + 1)

    def need(zz):
        return needs[zz]

    def ar_a(e, zz):
        u = 2 * e + zz
        piece = att_piece(e, zz, r)
        wrecv(piece, R_AS1 + u)
        for j, dev in enumerate((dev_up, dev_dn)):
            send(piece, piece, S_ARA + 2 * u + j, R_ARA + 2 * u + j, dev, lambda: att_piece(e, 0, 0), need(zz))

    def ar_b(e, zz):
        u = 2 * e + zz
        for j, (dev, rr) in enumerate(((dev_up, r_dn), (dev_dn, r_up))):
            wrecv(att_piece(e, zz, rr), R_ARA + 2 * u + j)
            part = att_half(e, zz, rr, j)
            send(part, part, S_ARB + 2 * u + j, R_ARB + 2 * u + j, dev, lambda: att_half(e, 0, 0, 0), need(zz))

    def ar_c(e, zz):
        u = 2 * e + zz
        for j in (0, 1):
            wrecv(att_half(e, zz, r_op, j), R_ARB + 2 * u + j)

    def ar(step, e):
        for zz in (0, 1):
            when(need(zz), functools.partial(step, e, zz))

    ar(ar_a, 0)
    for dz in (1, 3):
        mg_s1(0, dz)
        mg_s1(1, dz)
    ar(ar_b, 0)
    pl.when(swap)(norm_one_far)
    ar(ar_a, 1)
    mg_s1(0, 2)
    mg_s1(1, 2)
    when(swap, lambda: send(og_in, og, S_OG, R_OG, dev_swap, lambda: og_in, swap))
    mg(G_EARLY)
    ar(ar_c, 0)
    w_wq()
    w_wo()
    for dz in (1, 2, 3):
        wrecv(bfa.at[zsh(dz)], R_BIAS + dz - 1)
    wrecv(lrecv, R_LEN)
    keepf = 1.0 - (c + z % 2 - 2 * c * (z % 2)).astype(F32)
    length = lens[0:1, 0:1] * keepf + lrecv[0:1, 0:1] * (1.0 - keepf)
    wrecv(n1.at[pair_rows], R_N1)

    bqv = bfa[2 * c, 1:2, :] + bfa[2 * c + 1, 1:2, :]

    def qkv_body(i, _):
        rows = pl.ds(al(i * BQ, BQ), BQ)
        x = n1[rows, :]
        q[rows, :] = (nt(x, watt[0]) + bqv[:, :HC]).astype(BF)
        k[rows, :] = nt(x, watt[1]).astype(BF)
        v[rows, :] = (nt(x, watt[2]) + bqv[:, HC:]).astype(BF)
        return 0

    lax.fori_loop(0, NB, qkv_body, 0)
    ar(ar_b, 1)
    mg(G_QKV)

    def tr_body(i, _):
        rows = pl.ds(al(i * BQ, BQ), BQ)
        for hp in range(3):
            lanes = slice(hp * 128, hp * 128 + 128)
            qt[lanes, rows] = q[rows, lanes].T
            kt[lanes, rows] = k[rows, lanes].T
            vt[lanes, rows] = v[rows, lanes].T
        return 0

    lax.fori_loop(0, NB, tr_body, 0)
    mg(G_TR)

    lane = lax.broadcasted_iota(jnp.int32, (1, 128), 1)
    sub = lax.broadcasted_iota(jnp.int32, (128, 1), 0)
    pos = lax.broadcasted_iota(jnp.int32, (T, 1), 0).astype(F32)
    keybias = jnp.where(pos < length, 0.0, NEG)
    CS = 0.125 * LOG2E

    def head_prep(hp, hh):
        lanes = pl.ds(al(hp * 128, 128), 128)
        inhead = (lane // 64) == hh
        aux = lane == (1 - hh) * 64
        kp = k[:, lanes].astype(F32)
        kh[hh] = jnp.where(inhead, kp, jnp.where(aux, keybias, 0.0)).astype(BF)
        qp = qt[lanes, :].astype(F32)
        qh[hh] = jnp.where(sub == (1 - hh) * 64, 1.0, qp).astype(BF)
        return lanes, inhead

    def by_pair(hp, run, steps):
        for j in range(3):
            if steps[j]:
                pl.when(hp == j)(functools.partial(run, steps[j]))

    def fwd_pair(hp, _):
        for hh in (0, 1):
            head_prep(hp, hh)
        for qb in range(NB):
            nk = (qb + 1) * BQ
            cols = slice(qb * BQ, nk)
            for hh in (0, 1):
                h = hp * 2 + hh
                hrows = pl.ds(al(h * 64, 64), 64)
                s = dot(kh[hh, :nk, :], qh[hh, :, cols])
                diag = s[nk - BQ :] + cmask[...]
                s = diag if qb == 0 else jnp.concatenate([s[: nk - BQ], diag], axis=0)
                m = jnp.max(s, axis=0, keepdims=True) * CS
                p = jnp.exp2(s * CS - m)
                l = jnp.sum(p, axis=0, keepdims=True)
                o = dot(vt[hrows, :nk], p.astype(BF)) * (1.0 / l)
                ot[hrows, cols] = o.astype(BF)
                lse[h, 0:1, cols] = m + jnp.log(l) * LOG2E
            by_pair(hp, mg, [G_ATT[j][qb] for j in range(3)])
        return 0

    lax.fori_loop(0, 3, fwd_pair, 0)

    ar(ar_c, 1)
    mg(G_CTX)

    ps[...] = tn(ot[:, pl.ds(al(oc * R, R), R)], watt[3]).astype(BF)
    send(ps, pr, S_PO, R_PO, dev_pair, lambda: ps)
    mid[...] = hid[...].astype(F32) + vecs[2:3, :] + tn(ot[:, pl.ds(al(row0, R), R)], watt[3])
    w_og()
    when(swap, lambda: wrecv(og, R_OG))
    wrecv(pr, R_PO)

    sb[...] = jnp.zeros_like(sb)

    def ln2_body(i, _):
        rows = pl.ds(al(i * LB, LB), LB)
        x = mid[rows, :] + pr[rows, :].astype(F32)
        mid[rows, :] = x
        n, _r = stats(x)
        n2[rows, :] = (n * vecs[3:4, :] + vecs[4:5, :]).astype(BF)
        p0 = lax.broadcasted_iota(jnp.int32, (LB, 1), 0).astype(F32) + (row0 + i * LB).astype(F32)
        g = og[rows, :].astype(F32) * jnp.where(p0 < length, 1.0, 0.0)
        og[rows, :] = g.astype(BF)
        sb[5:6, :] += jnp.sum(g, axis=0, keepdims=True)
        oacc[rows, :] = jnp.zeros((LB, D), F32)
        dn2[rows, :] = jnp.zeros((LB, D), F32)
        return 0

    lax.fori_loop(0, R // LB, ln2_body, 0)
    for w in w_mlp0:
        w()

    def zdst(i):
        return (z - i - (i // 2) * (1 - 2 * (i % 2)) + 4) % 4

    def blk(m, i):
        return wmlp.at[m, zdst(i)]

    def add_into(dst, *others):
        t = dst[...].astype(F32)
        for o in others:
            t = t + o[...].astype(F32)
        dst[...] = t.astype(BF)

    def g_s0(m, i):
        u = m * 4 + i
        send(blk(m, i).at[:, oc], prb.at[u], S_GP + u, R_GP + u, dev_pair, lambda: blk(m, i).at[:, oc])

    def g_s1(m, i):
        u = m * 4 + i
        g = blk(m, i)
        wrecv(prb.at[u], R_GP + u)
        add_into(g.at[:, c], prb.at[u])
        send(g.at[r_op, c, pl.ds(0, 48)], r1b.at[u, 0], S_G1 + 2 * u, R_G1 + 2 * u, dev_up,
             lambda: r1b.at[u, 0])
        send(g.at[r_op, c, pl.ds(48, 48)], r1b.at[u, 1], S_G1 + 2 * u + 1, R_G1 + 2 * u + 1, dev_dn,
             lambda: r1b.at[u, 1])

    def g_s2(m, i):
        u = m * 4 + i
        g = blk(m, i)
        wrecv(r1b.at[u, 0], R_G1 + 2 * u)
        add_into(g.at[r_up, c, pl.ds(0, 48)], r1b.at[u, 0])
        send(g.at[r_up, c], r2b.at[u, 0], S_G2 + 2 * u, R_G2 + 2 * u, dev_up, lambda: r2b.at[u, 0])
        wrecv(r1b.at[u, 1], R_G1 + 2 * u + 1)
        add_into(g.at[r_dn, c, pl.ds(48, 48)], r1b.at[u, 1])
        send(g.at[r_dn, c], r2b.at[u, 1], S_G2 + 2 * u + 1, R_G2 + 2 * u + 1, dev_dn, lambda: r2b.at[u, 1])

    def g_s3(m, i):
        u = m * 4 + i
        g = blk(m, i)
        wrecv(r2b.at[u, 0], R_G2 + 2 * u)
        wrecv(r2b.at[u, 1], R_G2 + 2 * u + 1)
        add_into(g.at[r, c], r2b.at[u, 0], r2b.at[u, 1])
        if i > 0:
            send(g.at[r, c], zb.at[m, i - 1], S_GZ + u, R_GZ + m * 3 + i - 1, (dp, zdst(i)),
                 lambda: zb.at[m, i - 1])

    def g_fin(m):
        for i in (1, 2, 3):
            wrecv(zb.at[m, i - 1], R_GZ + m * 3 + i - 1)
        t = wmlp[m, z, r, c].astype(F32)
        for i in range(3):
            t = t + zb[m, i].astype(F32)
        fs[m] = t.astype(BF)
        dst = gm_out.at[m, r, c]
        send(fs.at[m], dst, S_FA + 3 * m, R_FA + 3 * m, dev_up, lambda: fs.at[m])
        send(fs.at[m], dst, S_FA + 3 * m + 1, R_FA + 3 * m + 1, dev_dn, lambda: fs.at[m])
        send(fs.at[m], dst, S_FA + 3 * m + 2, R_FA + 3 * m + 2, dev_pair, lambda: fs.at[m])

    def g_ag(m):
        lo = gm_out.at[m, r_dn, c, pl.ds(0, 48)]
        hi = gm_out.at[m, r_up, c, pl.ds(48, 48)]
        wrecv(gm_out.at[m, r_dn, c], R_FA + 3 * m)
        send(lo, lo, S_FB + 2 * m, R_FB + 2 * m, dev_up, lambda: r1b.at[0, 0])
        full = gm_out.at[m, r_dn, c]
        send(full, full, S_FC + 3 * m, R_FC + 3 * m, dev_pair, lambda: fs.at[m])
        wrecv(gm_out.at[m, r_up, c], R_FA + 3 * m + 1)
        send(hi, hi, S_FB + 2 * m + 1, R_FB + 2 * m + 1, dev_dn, lambda: r1b.at[0, 0])
        full2 = gm_out.at[m, r_up, c]
        send(full2, full2, S_FC + 3 * m + 1, R_FC + 3 * m + 1, dev_pair, lambda: fs.at[m])

    def g_ag2(m):
        wrecv(gm_out.at[m, r_op, c, pl.ds(0, 48)], R_FB + 2 * m)
        wrecv(gm_out.at[m, r_op, c, pl.ds(48, 48)], R_FB + 2 * m + 1)
        full = gm_out.at[m, r_op, c]
        send(full, full, S_FC + 3 * m + 2, R_FC + 3 * m + 2, dev_pair, lambda: fs.at[m])

    def g_end(m):
        wrecv(gm_out.at[m, r, oc], R_FA + 3 * m + 2)
        wrecv(gm_out.at[m, r_dn, oc], R_FC + 3 * m)
        wrecv(gm_out.at[m, r_up, oc], R_FC + 3 * m + 1)
        wrecv(gm_out.at[m, r_op, oc], R_FC + 3 * m + 2)

    def hat(h):
        return gatt.at[h // 2], (h % 2) * 64

    def a_s1(h):
        g, o = hat(h)
        for j, dev in enumerate((dev_up, dev_dn)):
            send(g.at[r_op, pl.ds(o + 32 * j, 32)], a1b.at[h, j], S_A1 + 2 * h + j, R_A1 + 2 * h + j, dev,
                 lambda j=j: a1b.at[h, j])

    def a_s2(h):
        g, o = hat(h)
        for j, (dev, rr) in enumerate(((dev_up, r_up), (dev_dn, r_dn))):
            wrecv(a1b.at[h, j], R_A1 + 2 * h + j)
            add_into(g.at[rr, pl.ds(o + 32 * j, 32)], a1b.at[h, j])
            send(g.at[rr, pl.ds(o, 64)], a2b.at[h, j], S_A2 + 2 * h + j, R_A2 + 2 * h + j, dev,
                 lambda j=j: a2b.at[h, j])

    def a_s3(h):
        g, o = hat(h)
        for j in (0, 1):
            wrecv(a2b.at[h, j], R_A2 + 2 * h + j)
        add_into(g.at[r, pl.ds(o, 64)], a2b.at[h, 0], a2b.at[h, 1])
        zz, to = h // 3, (h % 3) * 64

        def go():
            zd = 2 * c + zz
            slot = (zd - z + 3) % 4
            send(g.at[r, pl.ds(o, 64)], azb.at[slot, pl.ds(to, 64)], S_AZ + h, R_AZ + 3 * h + slot, (dp, zd),
                 lambda: a2b.at[h, 0], need(zz))

        pl.when(need(zz))(go)

    def a_fin(jj):
        def go(zz):
            h = 3 * zz + jj
            g, o = hat(h)
            for slot in range(3):
                wrecv(azb.at[slot, pl.ds(jj * 64, 64)], R_AZ + 3 * h + slot)
            t = g[r, o : o + 64].astype(F32)
            for slot in range(3):
                t = t + azb[slot, jj * 64 : jj * 64 + 64].astype(F32)
            fa[jj * 64 : jj * 64 + 64] = t.astype(BF)

        for zz in (0, 1):
            when(mine[zz], functools.partial(go, zz))

    def a_ag(jj):
        part = fa.at[pl.ds(jj * 64, 64)]
        for i, dev in enumerate((dev_up, dev_dn, dev_pair)):
            send(part, ga_out.at[r, pl.ds(jj * 64, 64)], S_HA + 3 * jj + i, R_HA + 3 * jj + i, dev,
                 lambda: fa.at[pl.ds(0, 64)], own_c)

    def a_ag2(jj):
        for j, (dev, rr) in enumerate(((dev_up, r_dn), (dev_dn, r_up))):
            part = ga_out.at[rr, pl.ds(jj * 64, 64)]
            wrecv(part, R_HA + 3 * jj + j)
            piece = ga_out.at[rr, pl.ds(jj * 64 + 32 * j, 32)]
            send(piece, piece, S_HB + 2 * jj + j, R_HB + 2 * jj + j, dev, lambda: fa.at[pl.ds(0, 32)], own_c)
            send(part, part, S_HC + 3 * jj + j, R_HC + 3 * jj + j, dev_pair, lambda: fa.at[pl.ds(0, 64)], own_c)

    def a_ag3(jj):
        for j in (0, 1):
            wrecv(ga_out.at[r_op, pl.ds(jj * 64 + 32 * j, 32)], R_HB + 2 * jj + j)
        part = ga_out.at[r_op, pl.ds(jj * 64, 64)]
        send(part, part, S_HC + 3 * jj + 2, R_HC + 3 * jj + 2, dev_pair, lambda: fa.at[pl.ds(0, 64)], own_c)

    def a_end():
        for jj in range(3):
            part = pl.ds(jj * 64, 64)
            wrecv(ga_out.at[r, part], R_HA + 3 * jj + 2)
            for j, rr in enumerate((r_dn, r_up, r_op)):
                wrecv(ga_out.at[rr, part], R_HC + 3 * jj + j)

    GA_ = 0.7978845608028654

    def gr(steps):
        for st in steps.split():
            kind, u = int(st[0]), int(st[1:])
            if kind > 3:
                (g_fin, g_ag, g_ag2)[kind - 4](u)
            elif u < 8:
                (g_s1, g_s2, g_s3)[kind - 1](1 - u % 2, u // 2)
            else:
                (a_s1, a_s2, a_s3)[kind - 1](u - 8)

    def mlp_body(i, _):
        zp = zdst(i)

        def got(dz):
            mg_done(0, dz)
            mg_done(1, dz)

        for it, dz in ((1, 1), (2, 3), (3, 2)):
            pl.when(i == it)(functools.partial(got, dz))
        for fb in range(D // 256):
            cols = slice(fb * 256, fb * 256 + 256)
            fcb = wmlp[0, zp, :, :, :, cols].reshape(D, 256)
            pre = dot(n2[...], fcb) + bfa[zp, 0:1, cols]
            sq = pre * pre
            t = jnp.tanh(pre * (GA_ + (0.044715 * GA_) * sq))
            hf = 0.5 * (1.0 + t)
            act[:, cols] = (pre * hf).astype(BF)
            gp = hf * (1.0 + (1.0 - hf) * (pre * (2.0 * GA_ + (0.26829 * GA_) * sq)))
            prj = wmlp[1, zp].reshape(D, D)[cols, :]
            dp_ = (nt(og[...], prj) * gp).astype(BF)
            dpre[:, cols] = dp_
            sb[pl.ds(6 + zp, 1), cols] = jnp.sum(dp_.astype(F32), axis=0, keepdims=True)
        prj = wmlp[1, zp].reshape(D, D)
        for rb in range(R // 256):
            rows = slice(rb * 256, rb * 256 + 256)
            oacc[rows, :] += dot(act[rows, :], prj)
        for j in range(2):
            cols = slice(j * HC, j * HC + HC)
            wmlp[1, zp, 2 * j : 2 * j + 2] = tn(act[:, cols], og[...]).astype(BF).reshape(2, 2, D // 8, D)
        at(i, 0)
        fc = wmlp[0, zp].reshape(D, D)
        for rb in range(R // 256):
            rows = slice(rb * 256, rb * 256 + 256)
            dn2[rows, :] += nt(dpre[rows, :], fc)
        for j in range(2):
            cols = slice(j * HC, j * HC + HC)
            wmlp[0, zp, 2 * j : 2 * j + 2] = tn(n2[:, cols], dpre[...]).astype(BF).reshape(2, 2, D // 8, D)
        at(i, 1)
        return 0

    def at(i, where):
        for kk_ in range(4):
            def here(kk_=kk_):
                g_s0(1 - where, kk_)
                mg(G_LOOP[kk_][where])
                gr(T_LOOP[kk_][where])

            pl.when(i == kk_)(here)

    mg(G_MLP)
    lax.fori_loop(0, 4, mlp_body, 0)

    def bwd2_body(i, _):
        rows = pl.ds(al(i * LB, LB), LB)
        x = mid[rows, :]
        p0 = lax.broadcasted_iota(jnp.int32, (LB, 1), 0).astype(F32) + (row0 + i * LB).astype(F32)
        ok = jnp.where(p0 < length, 1.0, 0.0)
        bo[rows, :] = ((x + oacc[rows, :] + vecs[5:6, :]) * ok).astype(BF)
        n, rstd = stats(x)
        dn = dn2[rows, :]
        e = dn * vecs[3:4, :]
        em = jnp.mean(e, axis=1, keepdims=True)
        en = jnp.mean(e * n, axis=1, keepdims=True)
        gm = og[rows, :].astype(F32) + (e - em - n * en) * rstd
        mid[rows, :] = gm
        ga[pl.ds(al(row0 + i * LB, LB), LB), :] = gm.astype(BF)
        sb[2:3, :] += jnp.sum(dn * n, axis=0, keepdims=True)
        sb[3:4, :] += jnp.sum(dn, axis=0, keepdims=True)
        sb[4:5, :] += jnp.sum(gm, axis=0, keepdims=True)
        return 0

    lax.fori_loop(0, R // LB, bwd2_body, 0)
    send(ga.at[mine_rows], ga.at[mine_rows], S_GA, R_GA, dev_pair, lambda: ga.at[mine_rows])
    when(swap, lambda: send(bo, bo_out, S_BO, R_BO, dev_swap, lambda: bo, swap))
    w_bo = local(lambda: bo, lambda: bo_out, keep)
    gr(T_BWD2)
    wrecv(ga.at[pair_rows], R_GA)

    def dctx_body(i, _):
        rows = pl.ds(al(i * BQ, BQ), BQ)
        d = nt(ga[rows, :], watt[3])
        do[rows, :] = d.astype(BF)
        for hp in range(3):
            lanes = slice(hp * 128, hp * 128 + 128)
            dot_[lanes, rows] = do[rows, lanes].T
        return 0

    lax.fori_loop(0, NB, dctx_body, 0)
    gr(T_DCTX)

    def bwd_pair(hp, _):
        prep = []
        for hh in (0, 1):
            h = hp * 2 + hh
            lanes, inhead = head_prep(hp, hh)
            hrows = pl.ds(al(h * 64, 64), 64)
            vh[hh] = jnp.where(inhead, v[:, lanes].astype(F32), 0.0).astype(BF)
            dl = jnp.sum(dot_[hrows, :].astype(F32) * ot[hrows, :].astype(F32), axis=0, keepdims=True)
            prep.append((h, hrows, dl, lse[h]))
        for kb in range(NB):
            krows = slice(kb * BQ, kb * BQ + BQ)
            qs = slice(kb * BQ, T)
            dks, dvs = [], []
            for hh in (0, 1):
                h, hrows, dl, ls_h = prep[hh]
                s = dot(kh[hh, krows, :], qh[hh, :, qs])
                diag = s[:, :BQ] + cmask[...]
                s = diag if kb == NB - 1 else jnp.concatenate([diag, s[:, BQ:]], axis=1)
                p = jnp.exp2(s * CS - ls_h[0:1, qs])
                dpr = dot(vh[hh, krows, :], dot_[lanes, qs])
                ds = (p * (dpr - dl[:, qs])).astype(BF)
                dvs.append(dot(p.astype(BF), do[qs, lanes]))
                dks.append(dot(ds, q[qs, lanes]) * 0.125)
                piece = dot(kt[hrows, krows], ds)
                if kb == 0:
                    dqa[hh] = piece
                else:
                    dqa[hh, :, qs] += piece
            first = lane < 64
            v[krows, lanes] = jnp.where(first, dvs[0], dvs[1]).astype(BF)
            k[krows, lanes] = jnp.where(first, dks[0], dks[1]).astype(BF)
            by_pair(hp, gr, [T_ATT[j][kb] for j in range(3)])
        for hh in (0, 1):
            qt[prep[hh][1], :] = (dqa[hh] * 0.125).astype(BF)
        lanes = pl.ds(al(hp * 128, 128), 128)

        def tr2(i, _):
            rows = pl.ds(al(i * BQ, BQ), BQ)
            q[rows, lanes] = qt[lanes, rows].T
            kt[lanes, rows] = k[rows, lanes].T
            vt[lanes, rows] = v[rows, lanes].T
            return 0

        lax.fori_loop(0, NB, tr2, 0)
        for t, ref in enumerate((qt, kt, vt)):
            gatt[hp, t] = dot(ref[lanes, :], n1[...]).astype(BF)
        gatt[hp, 3] = dot(ot[lanes, :], ga[...]).astype(BF)
        for j in range(3):
            pl.when(hp == j)(functools.partial(gr, T_PAIR[j]))
        return 0

    lax.fori_loop(0, 3, bwd_pair, 0)

    def dx(rows):
        return dot(q[rows, :], watt[0]) + dot(k[rows, :], watt[1]) + dot(v[rows, :], watt[2])

    ps2[...] = dx(pair_rows).astype(BF)
    send(ps2, pr2, S_DX, R_DX, dev_pair, lambda: ps2)
    gr(T_DX)
    dn2[...] = dx(mine_rows)
    gr(T_DX2)
    sb[pl.ds(10 + c, 1), :] = jnp.concatenate(
        [jnp.sum(q[...].astype(F32), axis=0, keepdims=True), jnp.sum(v[...].astype(F32), axis=0, keepdims=True)],
        axis=1,
    )
    wrecv(pr2, R_DX)

    def bwd1_body(i, _):
        rows = pl.ds(al(i * LB, LB), LB)
        n, rstd = stats(hid[rows, :].astype(F32))
        dn = dn2[rows, :] + pr2[rows, :].astype(F32)
        e = dn * vecs[0:1, :]
        em = jnp.mean(e, axis=1, keepdims=True)
        en = jnp.mean(e * n, axis=1, keepdims=True)
        gi[rows, :] = (mid[rows, :] + (e - em - n * en) * rstd).astype(BF)
        sb[0:1, :] += jnp.sum(dn * n, axis=0, keepdims=True)
        sb[1:2, :] += jnp.sum(dn, axis=0, keepdims=True)
        for j in range(R // LB):
            def out(j=j):
                part = pl.ds(j * LB, LB)
                send(gi.at[part], gi_out.at[part], S_GI + j, R_GI + j, dev_swap, lambda: gi.at[part], swap)

            pl.when((i == j) & swap)(out)
        return 0

    gr(T_AG)
    lax.fori_loop(0, R // LB, bwd1_body, 0)
    gr(T_LAST)
    w_gi = local(lambda: gi, lambda: gi_out, keep)

    def small_pair():
        send(sb.at[pl.ds(0, 16)], srb.at[8], S_SM, R_SM + 8, dev_pair, lambda: srb.at[0])

    def small_ring():
        wrecv(srb.at[8], R_SM + 8)
        t = sb[0:16] + srb[8]
        sb[16:32] = t
        srb[r] = t
        for j, dev in enumerate((dev_up, dev_dn, dev_op)):
            send(sb.at[pl.ds(16, 16)], srb.at[r], S_SM + 1 + j, R_SM + r, dev, lambda: srb.at[0])

    def small_z():
        for o in (r_up, r_dn, r_op):
            wrecv(srb.at[o], R_SM + o)
        t = (srb[0] + srb[1]) + (srb[2] + srb[3])
        sb[32:48] = t
        srb[4 + z] = t
        for dz in (1, 2, 3):
            send(sb.at[pl.ds(32, 16)], srb.at[4 + z], S_SM + 3 + dz, R_SM + 4 + z, dev_z[dz], lambda: srb.at[0])

    def small_end():
        for dz in (1, 2, 3):
            wrecv(srb.at[4 + zsh(dz)], R_SM + 4 + zsh(dz))
        t = (srb[4] + srb[5]) + (srb[6] + srb[7])
        sb[48:64] = t
        small_out[0:6, :] = t[0:6]
        small_out[6:7, :] = sb[pl.ds(54 + z, 1), :]
        row = sb[pl.ds(58 + z // 2, 1), :]
        odd = (z % 2).astype(F32)
        even = 1.0 - odd
        bq = even * row[:, :ZS] + odd * row[:, ZS : 2 * ZS]
        bv = even * row[:, 2 * ZS : 3 * ZS] + odd * row[:, 3 * ZS :]
        gap = jnp.zeros((1, HC - ZS), F32)
        small_out[7:8, :] = jnp.concatenate([bq, gap, bv, gap], axis=1)

    small_pair()
    gr(T_AG2)
    small_ring()
    for jj in range(3):
        a_fin(jj)
        when(own_c, functools.partial(a_ag, jj))
    small_z()
    for jj in range(3):
        when(own_c, functools.partial(a_ag2, jj))
    for jj in range(3):
        when(own_c, functools.partial(a_ag3, jj))
    small_end()

    w_fs = [local(lambda: fs.at[0], lambda: gm_out.at[0, r, c]), local(lambda: fs.at[1], lambda: gm_out.at[1, r, c])]
    w_fa = local(lambda: fa, lambda: ga_out.at[r], own_c)
    w_bo()
    w_gi()
    for w in w_fs:
        w()
    w_fa()
    for m in (0, 1):
        g_end(m)
    when(not_own, a_end)
    when(swap, lambda: wrecv(bo_out, R_BO))
    for j in range(R // LB):
        when(swap, lambda: wrecv(gi_out.at[pl.ds(j * LB, LB)], R_GI + j))
    for sid, (ref, cond) in pending.items():
        when(cond, lambda sid=sid, ref=ref: wsend(ref(), sid))


def widen_kernel(bo, gi, gm, ga, small, bo_o, gi_o, fc_o, proj_o, qkv_o, out_o, *vec_o):
    bo_o[...] = bo[...]
    gi_o[...] = gi[...]
    fc_o[...] = gm[0].astype(F32)
    proj_o[...] = gm[1].astype(F32)
    qkv_o[...] = ga[:3].astype(F32)
    out_o[...] = ga[3].astype(F32)
    for j, o in enumerate(vec_o):
        if j < 7:
            o[...] = small[j]
        else:
            n = o.shape[0]
            at = (j - 7) * small.shape[1] // 2
            o[...] = small[7, at : at + n]


def widen(bo, gi, gm, ga, small):
    n = 4
    (R, D), ZS = bo.shape, ga.shape[1]
    lens = (D,) * 7 + (ZS,) * 2
    rows = lambda m: pl.BlockSpec((m // n, D), lambda i: (i, 0))
    vec = lambda m: pl.BlockSpec((m,), lambda i: (0,))
    stack = lambda k, m: pl.BlockSpec((k, m // n, D), lambda i: (0, i, 0))
    return pl.pallas_call(
        widen_kernel,
        grid=(n,),
        out_shape=(
            jax.ShapeDtypeStruct((R, D), BF), jax.ShapeDtypeStruct((R, D), BF),
            jax.ShapeDtypeStruct((D, D), F32), jax.ShapeDtypeStruct((D, D), F32),
            jax.ShapeDtypeStruct((3, ZS, D), F32), jax.ShapeDtypeStruct((ZS, D), F32),
            *(jax.ShapeDtypeStruct((m,), F32) for m in lens),
        ),
        in_specs=[rows(R), rows(R), stack(2, D), stack(4, ZS), pl.BlockSpec((8, D), lambda i: (0, 0))],
        out_specs=(rows(R), rows(R), rows(D), rows(D), stack(3, ZS), rows(ZS), *(vec(m) for m in lens)),
        compiler_params=pltpu.CompilerParams(vmem_limit_bytes=64 * 1024 * 1024 - 65536),
        name="widen",
    )(bo, gi, gm, ga, small)


def body(
    hidden_in, lengths, ln1_gain, ln1_bias, w_qkv, b_query, b_value, w_out, b_out,
    ln2_gain, ln2_bias, w_fc, b_fc, w_proj, b_proj, out_grad,
):
    R, D = hidden_in.shape
    T, HC, ZS, EB = 2 * R, D // 2, D // 4, D // 8
    z = lax.axis_index("tensor")
    odd = z % 2 == 1
    lo, hi = (lambda t: jnp.pad(t, (0, HC - ZS))), (lambda t: jnp.pad(t, (HC - ZS, 0)))
    place = lambda t: jnp.where(odd, hi(t), lo(t))
    qv_row = jnp.pad(place(b_query), (0, HC)) + jnp.pad(place(b_value), (HC, 0))
    row = lax.broadcasted_iota(jnp.int32, (16, D), 0)
    vecs = jnp.zeros((16, D), BF)
    for at_row, vec in (
        (0, ln1_gain), (1, ln1_bias), (2, b_out), (3, ln2_gain), (4, ln2_bias), (5, b_proj), (8, b_fc), (9, qv_row),
    ):
        vecs = jnp.where(row == at_row, vec[None, :], vecs)
    vecs = vecs.astype(F32)
    wq = jnp.transpose(w_qkv, (1, 2, 0))
    wf = w_fc.reshape(4, 2, EB, D)
    wp = w_proj.reshape(4, 2, EB, D)
    vm = lambda *s: pltpu.VMEM(s, BF)
    vf = lambda *s: pltpu.VMEM(s, F32)
    scratch = [
        vf(8, 128), vf(8, 128), vf(4, 8, D), vm(R, D), vm(R, D), vm(T, D), vm(4, HC, D), vm(2, 4, 4, 2, EB, D),
        vm(T, HC), vm(T, HC), vm(T, HC), vm(HC, T), vm(HC, T), vm(HC, T),
        vm(T, HC), vm(HC, T), vm(HC, T),
        vf(R, D), vm(R, D), vf(R, D), vf(R, D), vm(R, D), vm(R, D), vm(T, D),
        vm(R, D), vm(R, D), vm(R, D), vm(R, D), vm(R, D), vm(R, D),
        vf(6, 1, T), vf(2, 64, T), vf(256, 256), vm(2, T, 128), vm(2, T, 128), vm(2, 128, T),
        vm(8, 4, EB, D), vm(8, 2, EB // 2, D), vm(8, 2, EB, D), vm(2, 3, EB, D), vm(2, EB, D),
        vm(3, 4, 128, D), vm(6, 2, 32, D), vm(6, 2, 64, D), vm(3, ZS, D), vm(ZS, D),
        vf(64, D), vf(9, 16, D),
        pltpu.SemaphoreType.DMA((SID.n,)), pltpu.SemaphoreType.DMA((RID.n,)), pltpu.SemaphoreType.DMA((12,)),
    ]
    anyspec = pl.BlockSpec(memory_space=pl.ANY)
    vspec = pl.BlockSpec(memory_space=pltpu.VMEM)
    block_out, grad_input, gm, gatt, small = pl.pallas_call(
        kernel,
        out_shape=(
            jax.ShapeDtypeStruct((R, D), BF),
            jax.ShapeDtypeStruct((R, D), BF),
            jax.ShapeDtypeStruct((2, 4, 2, EB, D), BF),
            jax.ShapeDtypeStruct((4, ZS, D), BF),
            jax.ShapeDtypeStruct((8, D), F32),
        ),
        in_specs=[pl.BlockSpec(memory_space=pltpu.SMEM), vspec] + [anyspec] * 6,
        out_specs=(anyspec, anyspec, anyspec, anyspec, vspec),
        scratch_shapes=scratch,
        compiler_params=pltpu.CompilerParams(
            collective_id=0, has_side_effects=True, vmem_limit_bytes=64 * 1024 * 1024 - 65536
        ),
        name="layer",
    )(lengths, vecs, hidden_in, out_grad, wq, w_out, wf, wp)
    data_count = lax.axis_size("dp")
    gm = gm.reshape(2, D, D)
    if data_count > GROUP:
        groups = [list(range(s, data_count, GROUP)) for s in range(GROUP)]
        gm, gatt, small = (
            lax.psum(t.astype(F32), "dp", axis_index_groups=groups) for t in (gm, gatt, small)
        )
    block_out, grad_input, g_fc, g_proj, g_qkv, g_out, *vec = widen(block_out, grad_input, gm, gatt, small)
    g_qkv = jnp.transpose(g_qkv, (2, 0, 1))
    return (
        block_out, grad_input, vec[0], vec[1], g_qkv, vec[7], vec[8], g_out, vec[4],
        vec[2], vec[3], g_fc, vec[6], g_proj, vec[5],
    )


def solution(mesh):
    rows = P(("dp", "tensor"), None)
    in_specs = (
        rows, P("dp"), P(), P(), P(None, None, "tensor"), P("tensor"), P("tensor"), P("tensor", None),
        P(), P(), P(), P(None, "tensor"), P("tensor"), P("tensor", None), P(), rows,
    )
    out_specs = (
        rows, rows, P(), P(), P(None, None, "tensor"), P("tensor"), P("tensor"), P("tensor", None),
        P(), P(), P(), P(None, "tensor"), P("tensor"), P("tensor", None), P(),
    )
    return jax.shard_map(body, mesh=mesh, in_specs=in_specs, out_specs=out_specs, check_vma=False)
```

```python
import functools

import jax
import jax.numpy as jnp
from jax import lax
from jax.experimental import pallas as pl
from jax.experimental.pallas import tpu as pltpu
from jax.sharding import PartitionSpec as P

BF = jnp.bfloat16
F32 = jnp.float32
EPS = 1e-5
NEG = -1e30
LOG2E = 1.4426950408889634
MESH = pl.DeviceIdType.MESH
RING = 4
GROUP = 2 * RING


T_LOOP = (("", "10"), ("11 20", "12"), ("13 21", "14"), ("15 22", "16"))
T_BWD2 = "17 23 30"
T_DCTX = "31"
T_ATT = (("24", "32", "25", "33"), ("26", "34", "27", "35"), ("28 36", "29", "37 210", "211"))
T_PAIR = ("18 19", "110 111", "112 113 41 40")
T_DX = "38 39"
T_DX2 = "212 213 310 311"
T_AG = "51 50"
T_LAST = "312 313"
T_AG2 = "61 60"
G_EARLY = ""
G_QKV = "a0"
G_TR = ""
G_ATT = (("a1", "", "b0", ""), ("b1 a2", "", "p0 a3", "p1"), ("b2", "", "b3 p2", "a4"))
G_CTX = ""
G_MLP = "p3 a5"
G_LOOP = (("b4", "b5"), ("p4", "p5"), ("", ""), ("", ""))


def dot(a, b, ca=1, cb=0):
    return lax.dot_general(a, b, (((ca,), (cb,)), ((), ())), preferred_element_type=F32)


def nt(a, b):
    return dot(a, b, 1, 1)


def tn(a, b):
    return dot(a, b, 0, 0)


def al(v, m):
    return pl.multiple_of(v, m)


class Ids:
    def __init__(self):
        self.n = 0

    def __call__(self, k):
        base = self.n
        self.n += k
        return base


SID = Ids()
S_LEN, S_BIAS, S_HID, S_OG, S_AS1 = SID(1), SID(3), SID(1), SID(1), SID(6)
S_ARA, S_ARB = SID(8), SID(8)
S_MS1, S_MRA, S_MRB, S_MP = SID(6), SID(12), SID(12), SID(6)
S_N1, S_PO, S_GA, S_DX, S_BO, S_GI = SID(1), SID(1), SID(1), SID(1), SID(1), SID(8)
S_GP, S_G1, S_G2, S_GZ = SID(8), SID(16), SID(16), SID(8)
S_FA, S_FB, S_FC = SID(6), SID(4), SID(6)
S_A1, S_A2, S_AZ = SID(12), SID(12), SID(6)
S_HA, S_HB, S_HC = SID(9), SID(6), SID(9)
S_SM = SID(7)
RID = Ids()
R_LEN, R_BIAS, R_HID, R_OG, R_AS1 = RID(1), RID(3), RID(1), RID(1), RID(4)
R_ARA, R_ARB = RID(8), RID(8)
R_MS1, R_MRA, R_MRB, R_MP = RID(6), RID(12), RID(12), RID(6)
R_N1, R_PO, R_GA, R_DX, R_BO, R_GI = RID(1), RID(1), RID(1), RID(1), RID(1), RID(8)
R_GP, R_G1, R_G2, R_GZ = RID(8), RID(16), RID(16), RID(6)
R_FA, R_FB, R_FC = RID(6), RID(4), RID(6)
R_A1, R_A2, R_AZ = RID(12), RID(12), RID(18)
R_HA, R_HB, R_HC = RID(9), RID(6), RID(9)
R_SM = RID(9)


def kernel(
    lengths, vecs, hid_in, og_in, wq, wo, wf, wp,
    bo_out, gi_out, gm_out, ga_out, small_out,
    lens, lrecv, bfa, hid, og, n1, watt, wmlp, q, k, v, qt, kt, vt, do, dot_, ot,
    mid, n2, oacc, dn2, act, dpre, ga, ps, pr, ps2, pr2, bo, gi,
    lse, dqa, cmask, kh, vh, qh,
    prb, r1b, r2b, zb, fs, gatt, a1b, a2b, azb, fa, sb, srb,
    ss, rs, ls,
):
    D = hid_in.shape[1]
    R = hid_in.shape[0]
    T = 2 * R
    HC = D // 2
    BQ = 256
    NB = T // BQ
    dp = lax.axis_index("dp")
    z = lax.axis_index("tensor")
    base = (dp // GROUP) * GROUP
    chip = (dp - base) // 2
    c = dp % 2
    oc = 1 - c
    cy = chip // 2
    cx = chip % 2
    r = 3 * cy + cx - 2 * cx * cy

    def ring_dp(rr, core):
        y = rr // 2
        x = rr % 2 + y - 2 * (rr % 2) * y
        return base + (2 * y + x) * 2 + core

    r_up = (r + 1) % RING
    r_dn = (r + 3) % RING
    r_op = (r + 2) % RING
    dev_up = (ring_dp(r_up, c), z)
    dev_dn = (ring_dp(r_dn, c), z)
    dev_op = (ring_dp(r_op, c), z)
    dev_pair = (dp + 1 - 2 * c, z)
    dev_z = [None] + [(dp, (z + dz) % 4) for dz in (1, 2, 3)]
    z_x = z + 1 - 2 * (z % 2)
    dev_swap = (dp + 1 - 2 * c, z_x)
    keep = c == z % 2
    swap = c != z % 2
    own_c = z // 2 == c
    mine = (z == 2 * c, z == 2 * c + 1)
    not_own = z // 2 != c
    zz_own = z % 2
    pending = {}

    def when(cond, fn):
        if cond is None:
            fn()
        else:
            pl.when(cond)(fn)

    def desc(src, dst, sid, rid, dev):
        return pltpu.make_async_remote_copy(
            src_ref=src, dst_ref=dst, send_sem=ss.at[sid], recv_sem=rs.at[rid],
            device_id=dev, device_id_type=MESH,
        )

    def send(src, dst, sid, rid, dev, late=None, cond=None):
        desc(src, dst, sid, rid, dev).start()
        if late is not None:
            pending[sid] = (late, cond)

    def wsend(ref, sid):
        desc(ref, ref, sid, 0, dev_pair).wait_send()

    def wrecv(ref, rid):
        desc(ref, ref, 0, rid, dev_pair).wait_recv()

    barrier = pltpu.get_barrier_semaphore()
    cross = [(dp + 1 - 2 * c, (z + dz) % 4) for dz in (1, 2, 3)]
    for dev in (dev_up, dev_dn, dev_op, dev_pair, dev_z[1], dev_z[2], dev_z[3], *cross):
        pl.semaphore_signal(barrier, inc=1, device_id=dev, device_id_type=MESH)

    loc_n = [0]

    def local(src, dst, cond=None):
        i = loc_n[0]
        loc_n[0] += 1
        cp = lambda: pltpu.make_async_copy(src(), dst(), ls.at[i])
        when(cond, lambda: cp().start())
        return lambda: when(cond, lambda: cp().wait())

    w_hid = local(lambda: hid_in, lambda: hid, keep)
    bias = vecs.at[pl.ds(8, 8)]
    ZS = D // 4

    def att_rows(zz):
        return pl.ds(al(zz * ZS, 16), ZS)

    ZQ = ZS // RING

    def att_piece(e, zz, rr):
        rows = pl.ds(al(zz * ZS + rr * ZQ, 16), ZQ)
        return watt.at[3, rows] if e else watt.at[pl.ds(0, 3), rows]

    def att_half(e, zz, rr, side):
        rows = pl.ds(al(zz * ZS + rr * ZQ, 16), ZQ)
        cols = pl.ds(side * HC, HC)
        return watt.at[3, rows, cols] if e else watt.at[pl.ds(0, 3), rows, cols]

    def att_s1(e):
        for dz in (1, 2, 3):
            rows = pl.ds(al(r * ZQ, 16), ZQ)
            src = wo.at[rows] if e else wq.at[:, rows]
            dev = (dp - c + z // 2, (z + dz) % 4)
            send(src, att_piece(e, zz_own, r), S_AS1 + 3 * e + dz - 1, R_AS1 + 2 * e + zz_own, dev,
                 lambda: att_piece(e, 0, 0), swap)

    w_wq = local(lambda: wq, lambda: watt.at[pl.ds(0, 3), att_rows(zz_own)], own_c)
    w_wo = local(lambda: wo, lambda: watt.at[3, att_rows(zz_own)], own_c)
    w_og = local(lambda: og_in, lambda: og, keep)
    w_mlp0 = [local(lambda: wf, lambda: wmlp.at[0, z]), local(lambda: wp, lambda: wmlp.at[1, z])]
    def zsh(dz):
        return (z - dz + 4) % 4

    def mg_s1(m, dz):
        w = (wf, wp)[m]
        u = m * 3 + dz - 1
        send(w.at[r, c], wmlp.at[m, z, r, c], S_MS1 + u, R_MS1 + u, dev_z[dz], lambda: w.at[r, c])

    def mg_a(m, dz):
        u = m * 3 + dz - 1
        piece = wmlp.at[m, zsh(dz), r, c]
        wrecv(piece, R_MS1 + u)
        send(piece, piece, S_MRA + 2 * u, R_MRA + 2 * u, dev_up)
        send(piece, piece, S_MRA + 2 * u + 1, R_MRA + 2 * u + 1, dev_dn)

    def mg_b(m, dz):
        u = m * 3 + dz - 1
        zp = zsh(dz)
        wrecv(wmlp.at[m, zp, r_dn, c], R_MRA + 2 * u)
        lo = wmlp.at[m, zp, r_dn, c, pl.ds(0, 48)]
        send(lo, lo, S_MRB + 2 * u, R_MRB + 2 * u, dev_up)
        wrecv(wmlp.at[m, zp, r_up, c], R_MRA + 2 * u + 1)
        hi = wmlp.at[m, zp, r_up, c, pl.ds(48, 48)]
        send(hi, hi, S_MRB + 2 * u + 1, R_MRB + 2 * u + 1, dev_dn)

    def mg_p(m, dz):
        u = m * 3 + dz - 1
        zp = zsh(dz)
        wrecv(wmlp.at[m, zp, r_op, c, pl.ds(0, 48)], R_MRB + 2 * u)
        wrecv(wmlp.at[m, zp, r_op, c, pl.ds(48, 48)], R_MRB + 2 * u + 1)
        mine = wmlp.at[m, zp, :, c]
        send(mine, mine, S_MP + u, R_MP + u, dev_pair)

    def mg_done(m, dz):
        u = m * 3 + dz - 1
        zp = zsh(dz)
        wrecv(wmlp.at[m, zp, :, oc], R_MP + u)
        for s in (0, 1):
            wsend(wmlp.at[m, zp, r, c], S_MRA + 2 * u + s)
            wsend(wmlp.at[m, zp, r, c, pl.ds(0, 48)], S_MRB + 2 * u + s)
        wsend(wmlp.at[m, zp, :, c], S_MP + u)

    munits = [(0, 1), (1, 1), (0, 3), (1, 3), (0, 2), (1, 2)]

    def mg(steps):
        for st in steps.split():
            {"a": mg_a, "b": mg_b, "p": mg_p}[st[0]](*munits[int(st[1])])

    row0 = c * R
    half = ZS // 2

    def stats(x):
        mu = jnp.mean(x, axis=1, keepdims=True)
        cen = x - mu
        var = jnp.mean(cen * cen, axis=1, keepdims=True)
        rstd = lax.rsqrt(var + EPS)
        return cen * rstd, rstd

    LB = 128

    def ln1_body(i, _):
        rows = pl.ds(al(i * LB, LB), LB)
        n, _r = stats(hid[rows, :].astype(F32))
        out = n * vecs[0:1, :] + vecs[1:2, :]
        n1[pl.ds(al(row0 + i * LB, LB), LB), :] = out.astype(BF)
        return 0

    mine_rows = pl.ds(al(row0, R), R)
    pair_rows = pl.ds(al(oc * R, R), R)

    def norm_one():
        lax.fori_loop(0, R // LB, ln1_body, 0)

    def norm_one_send():
        send(n1.at[mine_rows], n1.at[mine_rows], S_N1, R_N1, dev_pair, lambda: n1.at[mine_rows])

    def norm_one_far():
        wrecv(hid, R_HID)
        norm_one()
        norm_one_send()

    bfa[z] = bias[...]
    w_hid()
    pl.when(keep)(norm_one)

    kk = lax.broadcasted_iota(jnp.int32, (BQ, BQ), 0)
    qq = lax.broadcasted_iota(jnp.int32, (BQ, BQ), 1)
    cmask[...] = jnp.where(kk <= qq, 0.0, NEG)
    pl.semaphore_wait(barrier, 10)
    pl.when(swap)(lambda: att_s1(0))
    when(swap, lambda: send(hid_in, hid, S_HID, R_HID, dev_swap, lambda: hid_in, swap))
    pl.when(swap)(lambda: att_s1(1))
    for dz in (1, 2, 3):
        send(bias, bfa.at[z], S_BIAS + dz - 1, R_BIAS + dz - 1, dev_z[dz], lambda: bias)
    lens[...] = jnp.full((8, 128), lengths[z // 2].astype(F32))
    send(lens, lrecv, S_LEN, R_LEN, dev_pair, lambda: lens)
    pl.when(keep)(norm_one_send)

    needs = (z != 2 * c, z != 2 * c + 1)

    def need(zz):
        return needs[zz]

    def ar_a(e, zz):
        u = 2 * e + zz
        piece = att_piece(e, zz, r)
        wrecv(piece, R_AS1 + u)
        for j, dev in enumerate((dev_up, dev_dn)):
            send(piece, piece, S_ARA + 2 * u + j, R_ARA + 2 * u + j, dev, lambda: att_piece(e, 0, 0), need(zz))

    def ar_b(e, zz):
        u = 2 * e + zz
        for j, (dev, rr) in enumerate(((dev_up, r_dn), (dev_dn, r_up))):
            wrecv(att_piece(e, zz, rr), R_ARA + 2 * u + j)
            part = att_half(e, zz, rr, j)
            send(part, part, S_ARB + 2 * u + j, R_ARB + 2 * u + j, dev, lambda: att_half(e, 0, 0, 0), need(zz))

    def ar_c(e, zz):
        u = 2 * e + zz
        for j in (0, 1):
            wrecv(att_half(e, zz, r_op, j), R_ARB + 2 * u + j)

    def ar(step, e):
        for zz in (0, 1):
            when(need(zz), functools.partial(step, e, zz))

    ar(ar_a, 0)
    for dz in (1, 3):
        mg_s1(0, dz)
        mg_s1(1, dz)
    ar(ar_b, 0)
    pl.when(swap)(norm_one_far)
    ar(ar_a, 1)
    mg_s1(0, 2)
    mg_s1(1, 2)
    when(swap, lambda: send(og_in, og, S_OG, R_OG, dev_swap, lambda: og_in, swap))
    mg(G_EARLY)
    ar(ar_c, 0)
    w_wq()
    w_wo()
    for dz in (1, 2, 3):
        wrecv(bfa.at[zsh(dz)], R_BIAS + dz - 1)
    wrecv(lrecv, R_LEN)
    keepf = 1.0 - (c + z % 2 - 2 * c * (z % 2)).astype(F32)
    length = lens[0:1, 0:1] * keepf + lrecv[0:1, 0:1] * (1.0 - keepf)
    wrecv(n1.at[pair_rows], R_N1)

    bqv = bfa[2 * c, 1:2, :] + bfa[2 * c + 1, 1:2, :]

    def qkv_body(i, _):
        rows = pl.ds(al(i * BQ, BQ), BQ)
        x = n1[rows, :]
        q[rows, :] = (nt(x, watt[0]) + bqv[:, :HC]).astype(BF)
        k[rows, :] = nt(x, watt[1]).astype(BF)
        v[rows, :] = (nt(x, watt[2]) + bqv[:, HC:]).astype(BF)
        return 0

    lax.fori_loop(0, NB, qkv_body, 0)
    ar(ar_b, 1)
    mg(G_QKV)

    def tr_body(i, _):
        rows = pl.ds(al(i * BQ, BQ), BQ)
        for hp in range(3):
            lanes = slice(hp * 128, hp * 128 + 128)
            qt[lanes, rows] = q[rows, lanes].T
            kt[lanes, rows] = k[rows, lanes].T
            vt[lanes, rows] = v[rows, lanes].T
        return 0

    lax.fori_loop(0, NB, tr_body, 0)
    mg(G_TR)

    lane = lax.broadcasted_iota(jnp.int32, (1, 128), 1)
    sub = lax.broadcasted_iota(jnp.int32, (128, 1), 0)
    pos = lax.broadcasted_iota(jnp.int32, (T, 1), 0).astype(F32)
    keybias = jnp.where(pos < length, 0.0, NEG)
    CS = 0.125 * LOG2E

    def head_prep(hp, hh):
        lanes = pl.ds(al(hp * 128, 128), 128)
        inhead = (lane // 64) == hh
        aux = lane == (1 - hh) * 64
        kp = k[:, lanes].astype(F32)
        kh[hh] = jnp.where(inhead, kp, jnp.where(aux, keybias, 0.0)).astype(BF)
        qp = qt[lanes, :].astype(F32)
        qh[hh] = jnp.where(sub == (1 - hh) * 64, 1.0, qp).astype(BF)
        return lanes, inhead

    def by_pair(hp, run, steps):
        for j in range(3):
            if steps[j]:
                pl.when(hp == j)(functools.partial(run, steps[j]))

    def fwd_pair(hp, _):
        for hh in (0, 1):
            head_prep(hp, hh)
        for qb in range(NB):
            nk = (qb + 1) * BQ
            cols = slice(qb * BQ, nk)
            for hh in (0, 1):
                h = hp * 2 + hh
                hrows = pl.ds(al(h * 64, 64), 64)
                s = dot(kh[hh, :nk, :], qh[hh, :, cols])
                diag = s[nk - BQ :] + cmask[...]
                s = diag if qb == 0 else jnp.concatenate([s[: nk - BQ], diag], axis=0)
                m = jnp.max(s, axis=0, keepdims=True) * CS
                p = jnp.exp2(s * CS - m)
                l = jnp.sum(p, axis=0, keepdims=True)
                o = dot(vt[hrows, :nk], p.astype(BF)) * (1.0 / l)
                ot[hrows, cols] = o.astype(BF)
                lse[h, 0:1, cols] = m + jnp.log(l) * LOG2E
            by_pair(hp, mg, [G_ATT[j][qb] for j in range(3)])
        return 0

    lax.fori_loop(0, 3, fwd_pair, 0)

    ar(ar_c, 1)
    mg(G_CTX)

    ps[...] = tn(ot[:, pl.ds(al(oc * R, R), R)], watt[3]).astype(BF)
    send(ps, pr, S_PO, R_PO, dev_pair, lambda: ps)
    mid[...] = hid[...].astype(F32) + vecs[2:3, :] + tn(ot[:, pl.ds(al(row0, R), R)], watt[3])
    w_og()
    when(swap, lambda: wrecv(og, R_OG))
    wrecv(pr, R_PO)

    sb[...] = jnp.zeros_like(sb)

    def ln2_body(i, _):
        rows = pl.ds(al(i * LB, LB), LB)
        x = mid[rows, :] + pr[rows, :].astype(F32)
        mid[rows, :] = x
        n, _r = stats(x)
        n2[rows, :] = (n * vecs[3:4, :] + vecs[4:5, :]).astype(BF)
        p0 = lax.broadcasted_iota(jnp.int32, (LB, 1), 0).astype(F32) + (row0 + i * LB).astype(F32)
        g = og[rows, :].astype(F32) * jnp.where(p0 < length, 1.0, 0.0)
        og[rows, :] = g.astype(BF)
        sb[5:6, :] += jnp.sum(g, axis=0, keepdims=True)
        oacc[rows, :] = jnp.zeros((LB, D), F32)
        dn2[rows, :] = jnp.zeros((LB, D), F32)
        return 0

    lax.fori_loop(0, R // LB, ln2_body, 0)
    for w in w_mlp0:
        w()

    def zdst(i):
        return (z - i - (i // 2) * (1 - 2 * (i % 2)) + 4) % 4

    def blk(m, i):
        return wmlp.at[m, zdst(i)]

    def add_into(dst, *others):
        t = dst[...].astype(F32)
        for o in others:
            t = t + o[...].astype(F32)
        dst[...] = t.astype(BF)

    def g_s0(m, i):
        u = m * 4 + i
        send(blk(m, i).at[:, oc], prb.at[u], S_GP + u, R_GP + u, dev_pair, lambda: blk(m, i).at[:, oc])

    def g_s1(m, i):
        u = m * 4 + i
        g = blk(m, i)
        wrecv(prb.at[u], R_GP + u)
        add_into(g.at[:, c], prb.at[u])
        send(g.at[r_op, c, pl.ds(0, 48)], r1b.at[u, 0], S_G1 + 2 * u, R_G1 + 2 * u, dev_up,
             lambda: r1b.at[u, 0])
        send(g.at[r_op, c, pl.ds(48, 48)], r1b.at[u, 1], S_G1 + 2 * u + 1, R_G1 + 2 * u + 1, dev_dn,
             lambda: r1b.at[u, 1])

    def g_s2(m, i):
        u = m * 4 + i
        g = blk(m, i)
        wrecv(r1b.at[u, 0], R_G1 + 2 * u)
        add_into(g.at[r_up, c, pl.ds(0, 48)], r1b.at[u, 0])
        send(g.at[r_up, c], r2b.at[u, 0], S_G2 + 2 * u, R_G2 + 2 * u, dev_up, lambda: r2b.at[u, 0])
        wrecv(r1b.at[u, 1], R_G1 + 2 * u + 1)
        add_into(g.at[r_dn, c, pl.ds(48, 48)], r1b.at[u, 1])
        send(g.at[r_dn, c], r2b.at[u, 1], S_G2 + 2 * u + 1, R_G2 + 2 * u + 1, dev_dn, lambda: r2b.at[u, 1])

    def g_s3(m, i):
        u = m * 4 + i
        g = blk(m, i)
        wrecv(r2b.at[u, 0], R_G2 + 2 * u)
        wrecv(r2b.at[u, 1], R_G2 + 2 * u + 1)
        add_into(g.at[r, c], r2b.at[u, 0], r2b.at[u, 1])
        if i > 0:
            send(g.at[r, c], zb.at[m, i - 1], S_GZ + u, R_GZ + m * 3 + i - 1, (dp, zdst(i)),
                 lambda: zb.at[m, i - 1])

    def g_fin(m):
        for i in (1, 2, 3):
            wrecv(zb.at[m, i - 1], R_GZ + m * 3 + i - 1)
        t = wmlp[m, z, r, c].astype(F32)
        for i in range(3):
            t = t + zb[m, i].astype(F32)
        fs[m] = t.astype(BF)
        dst = gm_out.at[m, r, c]
        send(fs.at[m], dst, S_FA + 3 * m, R_FA + 3 * m, dev_up, lambda: fs.at[m])
        send(fs.at[m], dst, S_FA + 3 * m + 1, R_FA + 3 * m + 1, dev_dn, lambda: fs.at[m])
        send(fs.at[m], dst, S_FA + 3 * m + 2, R_FA + 3 * m + 2, dev_pair, lambda: fs.at[m])

    def g_ag(m):
        lo = gm_out.at[m, r_dn, c, pl.ds(0, 48)]
        hi = gm_out.at[m, r_up, c, pl.ds(48, 48)]
        wrecv(gm_out.at[m, r_dn, c], R_FA + 3 * m)
        send(lo, lo, S_FB + 2 * m, R_FB + 2 * m, dev_up, lambda: r1b.at[0, 0])
        full = gm_out.at[m, r_dn, c]
        send(full, full, S_FC + 3 * m, R_FC + 3 * m, dev_pair, lambda: fs.at[m])
        wrecv(gm_out.at[m, r_up, c], R_FA + 3 * m + 1)
        send(hi, hi, S_FB + 2 * m + 1, R_FB + 2 * m + 1, dev_dn, lambda: r1b.at[0, 0])
        full2 = gm_out.at[m, r_up, c]
        send(full2, full2, S_FC + 3 * m + 1, R_FC + 3 * m + 1, dev_pair, lambda: fs.at[m])

    def g_ag2(m):
        wrecv(gm_out.at[m, r_op, c, pl.ds(0, 48)], R_FB + 2 * m)
        wrecv(gm_out.at[m, r_op, c, pl.ds(48, 48)], R_FB + 2 * m + 1)
        full = gm_out.at[m, r_op, c]
        send(full, full, S_FC + 3 * m + 2, R_FC + 3 * m + 2, dev_pair, lambda: fs.at[m])

    def g_end(m):
        wrecv(gm_out.at[m, r, oc], R_FA + 3 * m + 2)
        wrecv(gm_out.at[m, r_dn, oc], R_FC + 3 * m)
        wrecv(gm_out.at[m, r_up, oc], R_FC + 3 * m + 1)
        wrecv(gm_out.at[m, r_op, oc], R_FC + 3 * m + 2)

    def hat(h):
        return gatt.at[h // 2], (h % 2) * 64

    def a_s1(h):
        g, o = hat(h)
        for j, dev in enumerate((dev_up, dev_dn)):
            send(g.at[r_op, pl.ds(o + 32 * j, 32)], a1b.at[h, j], S_A1 + 2 * h + j, R_A1 + 2 * h + j, dev,
                 lambda j=j: a1b.at[h, j])

    def a_s2(h):
        g, o = hat(h)
        for j, (dev, rr) in enumerate(((dev_up, r_up), (dev_dn, r_dn))):
            wrecv(a1b.at[h, j], R_A1 + 2 * h + j)
            add_into(g.at[rr, pl.ds(o + 32 * j, 32)], a1b.at[h, j])
            send(g.at[rr, pl.ds(o, 64)], a2b.at[h, j], S_A2 + 2 * h + j, R_A2 + 2 * h + j, dev,
                 lambda j=j: a2b.at[h, j])

    def a_s3(h):
        g, o = hat(h)
        for j in (0, 1):
            wrecv(a2b.at[h, j], R_A2 + 2 * h + j)
        add_into(g.at[r, pl.ds(o, 64)], a2b.at[h, 0], a2b.at[h, 1])
        zz, to = h // 3, (h % 3) * 64

        def go():
            zd = 2 * c + zz
            slot = (zd - z + 3) % 4
            send(g.at[r, pl.ds(o, 64)], azb.at[slot, pl.ds(to, 64)], S_AZ + h, R_AZ + 3 * h + slot, (dp, zd),
                 lambda: a2b.at[h, 0], need(zz))

        pl.when(need(zz))(go)

    def a_fin(jj):
        def go(zz):
            h = 3 * zz + jj
            g, o = hat(h)
            for slot in range(3):
                wrecv(azb.at[slot, pl.ds(jj * 64, 64)], R_AZ + 3 * h + slot)
            t = g[r, o : o + 64].astype(F32)
            for slot in range(3):
                t = t + azb[slot, jj * 64 : jj * 64 + 64].astype(F32)
            fa[jj * 64 : jj * 64 + 64] = t.astype(BF)

        for zz in (0, 1):
            when(mine[zz], functools.partial(go, zz))

    def a_ag(jj):
        part = fa.at[pl.ds(jj * 64, 64)]
        for i, dev in enumerate((dev_up, dev_dn, dev_pair)):
            send(part, ga_out.at[r, pl.ds(jj * 64, 64)], S_HA + 3 * jj + i, R_HA + 3 * jj + i, dev,
                 lambda: fa.at[pl.ds(0, 64)], own_c)

    def a_ag2(jj):
        for j, (dev, rr) in enumerate(((dev_up, r_dn), (dev_dn, r_up))):
            part = ga_out.at[rr, pl.ds(jj * 64, 64)]
            wrecv(part, R_HA + 3 * jj + j)
            piece = ga_out.at[rr, pl.ds(jj * 64 + 32 * j, 32)]
            send(piece, piece, S_HB + 2 * jj + j, R_HB + 2 * jj + j, dev, lambda: fa.at[pl.ds(0, 32)], own_c)
            send(part, part, S_HC + 3 * jj + j, R_HC + 3 * jj + j, dev_pair, lambda: fa.at[pl.ds(0, 64)], own_c)

    def a_ag3(jj):
        for j in (0, 1):
            wrecv(ga_out.at[r_op, pl.ds(jj * 64 + 32 * j, 32)], R_HB + 2 * jj + j)
        part = ga_out.at[r_op, pl.ds(jj * 64, 64)]
        send(part, part, S_HC + 3 * jj + 2, R_HC + 3 * jj + 2, dev_pair, lambda: fa.at[pl.ds(0, 64)], own_c)

    def a_end():
        for jj in range(3):
            part = pl.ds(jj * 64, 64)
            wrecv(ga_out.at[r, part], R_HA + 3 * jj + 2)
            for j, rr in enumerate((r_dn, r_up, r_op)):
                wrecv(ga_out.at[rr, part], R_HC + 3 * jj + j)

    GA_ = 0.7978845608028654

    def gr(steps):
        for st in steps.split():
            kind, u = int(st[0]), int(st[1:])
            if kind > 3:
                (g_fin, g_ag, g_ag2)[kind - 4](u)
            elif u < 8:
                (g_s1, g_s2, g_s3)[kind - 1](1 - u % 2, u // 2)
            else:
                (a_s1, a_s2, a_s3)[kind - 1](u - 8)

    def mlp_body(i, _):
        zp = zdst(i)

        def got(dz):
            mg_done(0, dz)
            mg_done(1, dz)

        for it, dz in ((1, 1), (2, 3), (3, 2)):
            pl.when(i == it)(functools.partial(got, dz))
        for fb in range(D // 256):
            cols = slice(fb * 256, fb * 256 + 256)
            fcb = wmlp[0, zp, :, :, :, cols].reshape(D, 256)
            pre = dot(n2[...], fcb) + bfa[zp, 0:1, cols]
            sq = pre * pre
            t = jnp.tanh(pre * (GA_ + (0.044715 * GA_) * sq))
            hf = 0.5 * (1.0 + t)
            act[:, cols] = (pre * hf).astype(BF)
            gp = hf * (1.0 + (1.0 - hf) * (pre * (2.0 * GA_ + (0.26829 * GA_) * sq)))
            prj = wmlp[1, zp].reshape(D, D)[cols, :]
            dp_ = (nt(og[...], prj) * gp).astype(BF)
            dpre[:, cols] = dp_
            sb[pl.ds(6 + zp, 1), cols] = jnp.sum(dp_.astype(F32), axis=0, keepdims=True)
        prj = wmlp[1, zp].reshape(D, D)
        for rb in range(R // 256):
            rows = slice(rb * 256, rb * 256 + 256)
            oacc[rows, :] += dot(act[rows, :], prj)
        for j in range(2):
            cols = slice(j * HC, j * HC + HC)
            wmlp[1, zp, 2 * j : 2 * j + 2] = tn(act[:, cols], og[...]).astype(BF).reshape(2, 2, D // 8, D)
        at(i, 0)
        fc = wmlp[0, zp].reshape(D, D)
        for rb in range(R // 256):
            rows = slice(rb * 256, rb * 256 + 256)
            dn2[rows, :] += nt(dpre[rows, :], fc)
        for j in range(2):
            cols = slice(j * HC, j * HC + HC)
            wmlp[0, zp, 2 * j : 2 * j + 2] = tn(n2[:, cols], dpre[...]).astype(BF).reshape(2, 2, D // 8, D)
        at(i, 1)
        return 0

    def at(i, where):
        for kk_ in range(4):
            def here(kk_=kk_):
                g_s0(1 - where, kk_)
                mg(G_LOOP[kk_][where])
                gr(T_LOOP[kk_][where])

            pl.when(i == kk_)(here)

    mg(G_MLP)
    lax.fori_loop(0, 4, mlp_body, 0)

    def bwd2_body(i, _):
        rows = pl.ds(al(i * LB, LB), LB)
        x = mid[rows, :]
        p0 = lax.broadcasted_iota(jnp.int32, (LB, 1), 0).astype(F32) + (row0 + i * LB).astype(F32)
        ok = jnp.where(p0 < length, 1.0, 0.0)
        bo[rows, :] = ((x + oacc[rows, :] + vecs[5:6, :]) * ok).astype(BF)
        n, rstd = stats(x)
        dn = dn2[rows, :]
        e = dn * vecs[3:4, :]
        em = jnp.mean(e, axis=1, keepdims=True)
        en = jnp.mean(e * n, axis=1, keepdims=True)
        gm = og[rows, :].astype(F32) + (e - em - n * en) * rstd
        mid[rows, :] = gm
        ga[pl.ds(al(row0 + i * LB, LB), LB), :] = gm.astype(BF)
        sb[2:3, :] += jnp.sum(dn * n, axis=0, keepdims=True)
        sb[3:4, :] += jnp.sum(dn, axis=0, keepdims=True)
        sb[4:5, :] += jnp.sum(gm, axis=0, keepdims=True)
        return 0

    lax.fori_loop(0, R // LB, bwd2_body, 0)
    send(ga.at[mine_rows], ga.at[mine_rows], S_GA, R_GA, dev_pair, lambda: ga.at[mine_rows])
    when(swap, lambda: send(bo, bo_out, S_BO, R_BO, dev_swap, lambda: bo, swap))
    w_bo = local(lambda: bo, lambda: bo_out, keep)
    gr(T_BWD2)
    wrecv(ga.at[pair_rows], R_GA)

    def dctx_body(i, _):
        rows = pl.ds(al(i * BQ, BQ), BQ)
        d = nt(ga[rows, :], watt[3])
        do[rows, :] = d.astype(BF)
        for hp in range(3):
            lanes = slice(hp * 128, hp * 128 + 128)
            dot_[lanes, rows] = do[rows, lanes].T
        return 0

    lax.fori_loop(0, NB, dctx_body, 0)
    gr(T_DCTX)

    def bwd_pair(hp, _):
        prep = []
        for hh in (0, 1):
            h = hp * 2 + hh
            lanes, inhead = head_prep(hp, hh)
            hrows = pl.ds(al(h * 64, 64), 64)
            vh[hh] = jnp.where(inhead, v[:, lanes].astype(F32), 0.0).astype(BF)
            dl = jnp.sum(dot_[hrows, :].astype(F32) * ot[hrows, :].astype(F32), axis=0, keepdims=True)
            prep.append((h, hrows, dl, lse[h]))
        for kb in range(NB):
            krows = slice(kb * BQ, kb * BQ + BQ)
            qs = slice(kb * BQ, T)
            dks, dvs = [], []
            for hh in (0, 1):
                h, hrows, dl, ls_h = prep[hh]
                s = dot(kh[hh, krows, :], qh[hh, :, qs])
                diag = s[:, :BQ] + cmask[...]
                s = diag if kb == NB - 1 else jnp.concatenate([diag, s[:, BQ:]], axis=1)
                p = jnp.exp2(s * CS - ls_h[0:1, qs])
                dpr = dot(vh[hh, krows, :], dot_[lanes, qs])
                ds = (p * (dpr - dl[:, qs])).astype(BF)
                dvs.append(dot(p.astype(BF), do[qs, lanes]))
                dks.append(dot(ds, q[qs, lanes]) * 0.125)
                piece = dot(kt[hrows, krows], ds)
                if kb == 0:
                    dqa[hh] = piece
                else:
                    dqa[hh, :, qs] += piece
            first = lane < 64
            v[krows, lanes] = jnp.where(first, dvs[0], dvs[1]).astype(BF)
            k[krows, lanes] = jnp.where(first, dks[0], dks[1]).astype(BF)
            by_pair(hp, gr, [T_ATT[j][kb] for j in range(3)])
        for hh in (0, 1):
            qt[prep[hh][1], :] = (dqa[hh] * 0.125).astype(BF)
        lanes = pl.ds(al(hp * 128, 128), 128)

        def tr2(i, _):
            rows = pl.ds(al(i * BQ, BQ), BQ)
            q[rows, lanes] = qt[lanes, rows].T
            kt[lanes, rows] = k[rows, lanes].T
            vt[lanes, rows] = v[rows, lanes].T
            return 0

        lax.fori_loop(0, NB, tr2, 0)
        for t, ref in enumerate((qt, kt, vt)):
            gatt[hp, t] = dot(ref[lanes, :], n1[...]).astype(BF)
        gatt[hp, 3] = dot(ot[lanes, :], ga[...]).astype(BF)
        for j in range(3):
            pl.when(hp == j)(functools.partial(gr, T_PAIR[j]))
        return 0

    lax.fori_loop(0, 3, bwd_pair, 0)

    def dx(rows):
        return dot(q[rows, :], watt[0]) + dot(k[rows, :], watt[1]) + dot(v[rows, :], watt[2])

    ps2[...] = dx(pair_rows).astype(BF)
    send(ps2, pr2, S_DX, R_DX, dev_pair, lambda: ps2)
    gr(T_DX)
    dn2[...] = dx(mine_rows)
    gr(T_DX2)
    sb[pl.ds(10 + c, 1), :] = jnp.concatenate(
        [jnp.sum(q[...].astype(F32), axis=0, keepdims=True), jnp.sum(v[...].astype(F32), axis=0, keepdims=True)],
        axis=1,
    )
    wrecv(pr2, R_DX)

    def bwd1_body(i, _):
        rows = pl.ds(al(i * LB, LB), LB)
        n, rstd = stats(hid[rows, :].astype(F32))
        dn = dn2[rows, :] + pr2[rows, :].astype(F32)
        e = dn * vecs[0:1, :]
        em = jnp.mean(e, axis=1, keepdims=True)
        en = jnp.mean(e * n, axis=1, keepdims=True)
        gi[rows, :] = (mid[rows, :] + (e - em - n * en) * rstd).astype(BF)
        sb[0:1, :] += jnp.sum(dn * n, axis=0, keepdims=True)
        sb[1:2, :] += jnp.sum(dn, axis=0, keepdims=True)
        for j in range(R // LB):
            def out(j=j):
                part = pl.ds(j * LB, LB)
                send(gi.at[part], gi_out.at[part], S_GI + j, R_GI + j, dev_swap, lambda: gi.at[part], swap)

            pl.when((i == j) & swap)(out)
        return 0

    gr(T_AG)
    lax.fori_loop(0, R // LB, bwd1_body, 0)
    gr(T_LAST)
    w_gi = local(lambda: gi, lambda: gi_out, keep)

    def small_pair():
        send(sb.at[pl.ds(0, 16)], srb.at[8], S_SM, R_SM + 8, dev_pair, lambda: srb.at[0])

    def small_ring():
        wrecv(srb.at[8], R_SM + 8)
        t = sb[0:16] + srb[8]
        sb[16:32] = t
        srb[r] = t
        for j, dev in enumerate((dev_up, dev_dn, dev_op)):
            send(sb.at[pl.ds(16, 16)], srb.at[r], S_SM + 1 + j, R_SM + r, dev, lambda: srb.at[0])

    def small_z():
        for o in (r_up, r_dn, r_op):
            wrecv(srb.at[o], R_SM + o)
        t = (srb[0] + srb[1]) + (srb[2] + srb[3])
        sb[32:48] = t
        srb[4 + z] = t
        for dz in (1, 2, 3):
            send(sb.at[pl.ds(32, 16)], srb.at[4 + z], S_SM + 3 + dz, R_SM + 4 + z, dev_z[dz], lambda: srb.at[0])

    def small_end():
        for dz in (1, 2, 3):
            wrecv(srb.at[4 + zsh(dz)], R_SM + 4 + zsh(dz))
        t = (srb[4] + srb[5]) + (srb[6] + srb[7])
        sb[48:64] = t
        small_out[0:6, :] = t[0:6]
        small_out[6:7, :] = sb[pl.ds(54 + z, 1), :]
        row = sb[pl.ds(58 + z // 2, 1), :]
        odd = (z % 2).astype(F32)
        even = 1.0 - odd
        bq = even * row[:, :ZS] + odd * row[:, ZS : 2 * ZS]
        bv = even * row[:, 2 * ZS : 3 * ZS] + odd * row[:, 3 * ZS :]
        gap = jnp.zeros((1, HC - ZS), F32)
        small_out[7:8, :] = jnp.concatenate([bq, gap, bv, gap], axis=1)

    small_pair()
    gr(T_AG2)
    small_ring()
    for jj in range(3):
        a_fin(jj)
        when(own_c, functools.partial(a_ag, jj))
    small_z()
    for jj in range(3):
        when(own_c, functools.partial(a_ag2, jj))
    for jj in range(3):
        when(own_c, functools.partial(a_ag3, jj))
    small_end()

    w_fs = [local(lambda: fs.at[0], lambda: gm_out.at[0, r, c]), local(lambda: fs.at[1], lambda: gm_out.at[1, r, c])]
    w_fa = local(lambda: fa, lambda: ga_out.at[r], own_c)
    w_bo()
    w_gi()
    for w in w_fs:
        w()
    w_fa()
    for m in (0, 1):
        g_end(m)
    when(not_own, a_end)
    when(swap, lambda: wrecv(bo_out, R_BO))
    for j in range(R // LB):
        when(swap, lambda: wrecv(gi_out.at[pl.ds(j * LB, LB)], R_GI + j))
    for sid, (ref, cond) in pending.items():
        when(cond, lambda sid=sid, ref=ref: wsend(ref(), sid))


def widen_kernel(bo, gi, gm, ga, small, bo_o, gi_o, fc_o, proj_o, qkv_o, out_o, *vec_o):
    bo_o[...] = bo[...]
    gi_o[...] = gi[...]
    fc_o[...] = gm[0].astype(F32)
    proj_o[...] = gm[1].astype(F32)
    qkv_o[...] = ga[:3].astype(F32)
    out_o[...] = ga[3].astype(F32)
    for j, o in enumerate(vec_o):
        if j < 7:
            o[...] = small[j]
        else:
            n = o.shape[0]
            at = (j - 7) * small.shape[1] // 2
            o[...] = small[7, at : at + n]


def widen(bo, gi, gm, ga, small):
    n = 2
    (R, D), ZS = bo.shape, ga.shape[1]
    lens = (D,) * 7 + (ZS,) * 2
    rows = lambda m: pl.BlockSpec((m // n, D), lambda i: (i, 0))
    vec = lambda m: pl.BlockSpec((m,), lambda i: (0,))
    stack = lambda k, m: pl.BlockSpec((k, m // n, D), lambda i: (0, i, 0))
    return pl.pallas_call(
        widen_kernel,
        grid=(n,),
        out_shape=(
            jax.ShapeDtypeStruct((R, D), BF), jax.ShapeDtypeStruct((R, D), BF),
            jax.ShapeDtypeStruct((D, D), F32), jax.ShapeDtypeStruct((D, D), F32),
            jax.ShapeDtypeStruct((3, ZS, D), F32), jax.ShapeDtypeStruct((ZS, D), F32),
            *(jax.ShapeDtypeStruct((m,), F32) for m in lens),
        ),
        in_specs=[rows(R), rows(R), stack(2, D), stack(4, ZS), pl.BlockSpec((8, D), lambda i: (0, 0))],
        out_specs=(rows(R), rows(R), rows(D), rows(D), stack(3, ZS), rows(ZS), *(vec(m) for m in lens)),
        compiler_params=pltpu.CompilerParams(vmem_limit_bytes=64 * 1024 * 1024 - 65536),
        name="widen",
    )(bo, gi, gm, ga, small)


def body(
    hidden_in, lengths, ln1_gain, ln1_bias, w_qkv, b_query, b_value, w_out, b_out,
    ln2_gain, ln2_bias, w_fc, b_fc, w_proj, b_proj, out_grad,
):
    R, D = hidden_in.shape
    T, HC, ZS, EB = 2 * R, D // 2, D // 4, D // 8
    z = lax.axis_index("tensor")
    odd = z % 2 == 1
    lo, hi = (lambda t: jnp.pad(t, (0, HC - ZS))), (lambda t: jnp.pad(t, (HC - ZS, 0)))
    place = lambda t: jnp.where(odd, hi(t), lo(t))
    qv_row = jnp.pad(place(b_query), (0, HC)) + jnp.pad(place(b_value), (HC, 0))
    row = lax.broadcasted_iota(jnp.int32, (16, D), 0)
    vecs = jnp.zeros((16, D), BF)
    for at_row, vec in (
        (0, ln1_gain), (1, ln1_bias), (2, b_out), (3, ln2_gain), (4, ln2_bias), (5, b_proj), (8, b_fc), (9, qv_row),
    ):
        vecs = jnp.where(row == at_row, vec[None, :], vecs)
    vecs = vecs.astype(F32)
    wq = jnp.transpose(w_qkv, (1, 2, 0))
    wf = w_fc.reshape(4, 2, EB, D)
    wp = w_proj.reshape(4, 2, EB, D)
    vm = lambda *s: pltpu.VMEM(s, BF)
    vf = lambda *s: pltpu.VMEM(s, F32)
    scratch = [
        vf(8, 128), vf(8, 128), vf(4, 8, D), vm(R, D), vm(R, D), vm(T, D), vm(4, HC, D), vm(2, 4, 4, 2, EB, D),
        vm(T, HC), vm(T, HC), vm(T, HC), vm(HC, T), vm(HC, T), vm(HC, T),
        vm(T, HC), vm(HC, T), vm(HC, T),
        vf(R, D), vm(R, D), vf(R, D), vf(R, D), vm(R, D), vm(R, D), vm(T, D),
        vm(R, D), vm(R, D), vm(R, D), vm(R, D), vm(R, D), vm(R, D),
        vf(6, 1, T), vf(2, 64, T), vf(256, 256), vm(2, T, 128), vm(2, T, 128), vm(2, 128, T),
        vm(8, 4, EB, D), vm(8, 2, EB // 2, D), vm(8, 2, EB, D), vm(2, 3, EB, D), vm(2, EB, D),
        vm(3, 4, 128, D), vm(6, 2, 32, D), vm(6, 2, 64, D), vm(3, ZS, D), vm(ZS, D),
        vf(64, D), vf(9, 16, D),
        pltpu.SemaphoreType.DMA((SID.n,)), pltpu.SemaphoreType.DMA((RID.n,)), pltpu.SemaphoreType.DMA((12,)),
    ]
    anyspec = pl.BlockSpec(memory_space=pl.ANY)
    vspec = pl.BlockSpec(memory_space=pltpu.VMEM)
    block_out, grad_input, gm, gatt, small = pl.pallas_call(
        kernel,
        out_shape=(
            jax.ShapeDtypeStruct((R, D), BF),
            jax.ShapeDtypeStruct((R, D), BF),
            jax.ShapeDtypeStruct((2, 4, 2, EB, D), BF),
            jax.ShapeDtypeStruct((4, ZS, D), BF),
            jax.ShapeDtypeStruct((8, D), F32),
        ),
        in_specs=[pl.BlockSpec(memory_space=pltpu.SMEM), vspec] + [anyspec] * 6,
        out_specs=(anyspec, anyspec, anyspec, anyspec, vspec),
        scratch_shapes=scratch,
        compiler_params=pltpu.CompilerParams(
            collective_id=0, has_side_effects=True, vmem_limit_bytes=64 * 1024 * 1024 - 65536
        ),
        name="layer",
    )(lengths, vecs, hidden_in, out_grad, wq, w_out, wf, wp)
    data_count = lax.axis_size("dp")
    gm = gm.reshape(2, D, D)
    if data_count > GROUP:
        groups = [list(range(s, data_count, GROUP)) for s in range(GROUP)]
        gm, gatt, small = (
            lax.psum(t.astype(F32), "dp", axis_index_groups=groups) for t in (gm, gatt, small)
        )
    block_out, grad_input, g_fc, g_proj, g_qkv, g_out, *vec = widen(block_out, grad_input, gm, gatt, small)
    g_qkv = jnp.transpose(g_qkv, (2, 0, 1))
    return (
        block_out, grad_input, vec[0], vec[1], g_qkv, vec[7], vec[8], g_out, vec[4],
        vec[2], vec[3], g_fc, vec[6], g_proj, vec[5],
    )


def solution(mesh):
    rows = P(("dp", "tensor"), None)
    in_specs = (
        rows, P("dp"), P(), P(), P(None, None, "tensor"), P("tensor"), P("tensor"), P("tensor", None),
        P(), P(), P(), P(None, "tensor"), P("tensor"), P("tensor", None), P(), rows,
    )
    out_specs = (
        rows, rows, P(), P(), P(None, None, "tensor"), P("tensor"), P("tensor"), P("tensor", None),
        P(), P(), P(), P(None, "tensor"), P("tensor"), P("tensor", None), P(),
    )
    return jax.shard_map(body, mesh=mesh, in_specs=in_specs, out_specs=out_specs, check_vma=False)
```
